256 devices in a mesh: tm: 16 (over z, core), tile: 4 (over x), group: 4 (over y).
Axes of the slice: x: 4, y: 4, z: 8, core: 2. Of those that a mesh axis runs over, the one named last changes fastest.
Arguments:
- latents: bfloat16 [4, 32, 12, 64, 384], P('group', 'tm', 'tile'), may hold values from -6 to 6
- frame_counts: int32 [4, 4], P('group'), may hold values from 1 to 15, 32 in all within a row
- gain_one: float32 [384], replicated, may hold values from 0.1 to 1.9
- gain_two: float32 [384], replicated, may hold values from 0.1 to 1.9
- conv_one: bfloat16 [10368, 384], P(('tm', 'group')), may hold values from -0.0625 to 0.0625
- conv_two: bfloat16 [10368, 384], P(('tm', 'group')), may hold values from -0.0625 to 0.0625
Outputs:
- upsampled: bfloat16 [4, 32, 24, 128, 384], P('group', 'tm', 'tile')
The draws below stay inside these ranges and needn't reach their ends.
Inputs may be any that keep to these rules, and one draw needn't show every extreme that they name: `frame_counts`: each group's counts sum to 32; in each group the largest count equals 15.
All inputs are finite; a program needn't handle non-finite values.
Results may differ from the reference program's by a relative error of at most 0.0041.
Values may be sent and summed in bfloat16 or wider, within the bound.
No kernel may reach another device: no remote copies, remote signals or barrier semaphores. Data moves between devices by JAX's collectives and lax.ppermute only.
A program may use at most 128 MiB of HBM per device.

```python
import math
import jax
import jax.numpy as jnp
import numpy as np
from jax import lax

C = 384
WIDTH = 64
VID_GROUP = 4
TAPS = 27
SLOTS = 32
ROWS = 12
GROUPS = 4
MOST_FRAMES = 15


def steps_of(rng, shape, shards, low, largest):
    level, own = 1.0, jax.random.fold_in(rng, 6)
    for dim, blocks in shards:
        steps = jnp.exp(jax.random.uniform(jax.random.fold_in(own, dim), (blocks,), jnp.float32, low / len(shards), largest / len(shards)))
        level = level * jnp.repeat(steps, shape[dim] // blocks).reshape([-1 if axis == dim else 1 for axis in range(len(shape))])
    return level


def profile(number_of, total, bound, skew):
    loads = [(1 << 20) // math.isqrt(standing ** skew) + 1 for standing in range(2, number_of + 1)]
    spare, holding = total - bound - (number_of - 1), [1] * (number_of - 1)
    while spare > 0:
        movable = [i for i in range(number_of - 1) if holding[i] < bound]
        pool, remaining = sum([loads[i] for i in movable]), spare
        for i in movable:
            extra = min(bound - holding[i], max(1, remaining * loads[i] // pool), spare)
            holding[i] = holding[i] + extra
            spare = spare - extra
    return np.array([bound] + holding)


def uneven_parts(key, number_of, total, most, skew):
    if number_of == 2:
        one = jax.random.randint(key, (), max(1, total - most), min(most, total - 1) + 1)
        return jnp.stack([one, total - one])
    sizes = jnp.asarray(profile(number_of, total, most, skew), jnp.int32)
    twos = (number_of - 1) // 2
    source_of, taker = sizes[1:1 + 2 * twos:2], sizes[2:2 + 2 * twos:2]
    margin = jnp.minimum(source_of - 1, most - taker)
    shifted = jax.random.randint(jax.random.fold_in(key, 1), (twos,), 0, 1 << 20) % (margin + 1)
    sizes = sizes.at[1:1 + 2 * twos:2].set(source_of - shifted).at[2:2 + 2 * twos:2].set(taker + shifted)
    return sizes[jax.random.permutation(jax.random.fold_in(key, 2), number_of)]


def noise(own_key, extent, scale, reach, split=(), held_as=jnp.bfloat16):
    values = jax.random.normal(own_key, extent, jnp.float32) * scale
    if len(split) > 0:
        values = steps_of(own_key, extent, split, -0.22, 0.18) * values
    return jnp.clip(values, min=-reach, max=reach).astype(held_as)


def setup_inputs(seed: int = 0) -> dict:
    key_of = jax.random.split(jax.random.key(seed), 7)
    latents = noise(key_of[0], (GROUPS, SLOTS, ROWS, WIDTH, C), 1.0, 6.0, ((0, 4), (1, 16), (2, 4)))
    frame_counts = jax.vmap(lambda own: uneven_parts(own, VID_GROUP, SLOTS, MOST_FRAMES, 2))(jax.random.split(key_of[1], GROUPS)).reshape((GROUPS, VID_GROUP)).astype(jnp.int32)
    gain_one = jnp.clip(1.0 + 0.18 * jax.random.normal(key_of[2], (C,), jnp.float32), 0.1, 1.9)
    gain_two = jnp.clip(1.0 + 0.18 * jax.random.normal(key_of[3], (C,), jnp.float32), 0.1, 1.9)
    conv_one = noise(key_of[4], (TAPS * C, C), (TAPS * C) ** -0.5, 0.0625, ((0, 64),))
    conv_two = noise(key_of[5], (TAPS * C, C), (TAPS * C) ** -0.5, 0.0625, ((0, 64),))
    return dict(latents=latents, frame_counts=frame_counts, gain_one=gain_one, gain_two=gain_two, conv_one=conv_one, conv_two=conv_two)


EPS = 1e-06

def norm_silu(values, gain):
    mean_sq = lax.optimization_barrier(jnp.mean(values * values, axis=-1, keepdims=True))
    return jax.nn.silu(values * lax.rsqrt(mean_sq + EPS) * gain)

def video_start(slots, counts):
    starts = jnp.cumsum(counts) - counts
    hit = starts[None, :] <= slots[:, None]
    return lax.optimization_barrier(jnp.max(jnp.where(hit, starts[None, :], 0), axis=1))

def causal_conv(padded, weight, out_slots, counts):
    channels = weight.shape[1]
    padded = jnp.pad(padded, ((0, 0), (0, 0), (1, 1), (0, 0)))
    frames = padded.shape[0] - 2
    height = padded.shape[1] - 2
    width = padded.shape[2] - 2
    begins = video_start(out_slots, counts)
    total = jnp.zeros((frames, height, width, channels), jnp.float32)
    for time_tap in range(3):
        partial_sum = jnp.zeros((frames * height * width, channels), jnp.float32)
        for row_tap in range(3):
            columns = jnp.concatenate([padded[time_tap:time_tap + frames, row_tap:row_tap + height, col_tap:col_tap + width] for col_tap in range(3)], axis=-1)
            first_row = (time_tap * 3 + row_tap) * 3 * channels
            block_w = weight[first_row:first_row + 3 * channels]
            partial_sum = partial_sum + jnp.dot(columns.reshape(-1, 3 * channels), block_w, preferred_element_type=jnp.float32)
        valid = (out_slots - (2 - time_tap) >= begins).astype(jnp.float32)
        total = total + valid[:, None, None, None] * partial_sum.reshape(frames, height, width, channels)
    return total

def one_group(latent, counts, gain_one, gain_two, conv_one, conv_two):
    slots = jnp.arange(latent.shape[0], dtype=jnp.int32)
    source = latent.astype(jnp.float32)
    hidden_one = norm_silu(source, gain_one).astype(jnp.bfloat16)
    padded = jnp.pad(hidden_one, ((2, 0), (1, 1), (0, 0), (0, 0)))
    first = causal_conv(padded, conv_one, slots, counts)
    hidden_two = norm_silu(first, gain_two).astype(jnp.bfloat16)
    padded = jnp.pad(hidden_two, ((2, 0), (1, 1), (0, 0), (0, 0)))
    second = causal_conv(padded, conv_two, slots, counts)
    block = (source + second).astype(jnp.bfloat16)
    frames, height, width, channels = block.shape
    return jnp.broadcast_to(block[:, :, None, :, None, :], (frames, height, 2, width, 2, channels)).reshape(frames, 2 * height, 2 * width, channels)

def reference(latents, frame_counts, gain_one, gain_two, conv_one, conv_two):

    def apply_group(pair):
        return one_group(pair[0], pair[1], gain_one, gain_two, conv_one, conv_two)
    return lax.map(apply_group, (latents, frame_counts))
```

```python
import functools
import jax
import jax.numpy as jnp
from jax import lax
from jax.experimental import pallas as pl
from jax.experimental.pallas import tpu as pltpu
from jax.sharding import Mesh, PartitionSpec as P

EPS = 1e-06
SLOT = ("z", "core")
LANE = 128


def video_start(slots, counts):
    starts = jnp.cumsum(counts) - counts
    hit = starts[None, :] <= slots[:, None]
    return jnp.max(jnp.where(hit, starts[None, :], 0), axis=1)


def spread(x, axis):
    n = lax.axis_size(axis)
    return lax.all_to_all(jnp.broadcast_to(x[None], (n,) + x.shape), axis, 0, 0)


def earlier(x):
    n = lax.axis_size(SLOT)
    return lax.ppermute(x, SLOT, [(i, i + 1) for i in range(n - 1)])


def fill_shifted(taps, slot, row, frame_row):
    width, channels = frame_row.shape
    wide = frame_row.astype(jnp.float32)
    col = lax.broadcasted_iota(jnp.int32, (width, channels), 0)
    left = jnp.where(col == 0, 0.0, pltpu.roll(wide, 1, 0))
    right = jnp.where(col == width - 1, 0.0, pltpu.roll(wide, width - 1, 0))
    taps[0, slot, row] = left.astype(frame_row.dtype)
    taps[1, slot, row] = frame_row
    taps[2, slot, row] = right.astype(frame_row.dtype)


def clear_border(taps):
    _, slots, rows, width, channels = taps.shape
    blank = jnp.zeros((width, channels), taps.dtype)
    for e in range(3):
        for slot in range(slots):
            taps[e, slot, 0] = blank
            taps[e, slot, rows - 1] = blank


def conv_one_kernel(valid, halo, own, weight, out, taps):
    parts, frames, each, width, channels = own.shape
    rows = parts * each
    clear_border(taps)
    for slot in range(2 * frames):
        source = halo if slot < frames else own
        for row in range(rows):
            fill_shifted(taps, slot, row + 1, source[row // each, slot % frames, row % each])
    for slot in range(2 * frames):
        pairs = [(s, slot - s) for s in range(frames) if 0 <= slot - s < 3]
        total = None
        for b in range(3):
            columns = jnp.concatenate(
                [taps[e, slot, b : b + rows].reshape(rows * width, channels) for e in range(3)], axis=1
            )
            blocks = []
            for _, a in pairs:
                first = (a * 3 + b) * 3 * channels
                blocks.append(weight[first : first + 3 * channels, :])
            packed = blocks[0] if len(blocks) == 1 else jnp.concatenate(blocks, axis=1)
            term = jnp.dot(columns, packed, preferred_element_type=jnp.float32)
            total = term if total is None else total + term
        for i, (s, a) in enumerate(pairs):
            piece = valid[s, a] * total[:, i * LANE : (i + 1) * LANE]
            piece = piece.reshape(rows, width, LANE)
            if a == 0:
                out[s] = piece
            else:
                out[s] = out[s] + piece


def conv_two_kernel(valid, halo, own, weight, out, taps, acc):
    frames, rows, width, lanes = own.shape
    parts = out.shape[0]
    each = rows // parts
    channels = weight.shape[1]
    clear_border(taps)
    for slot in range(2 * frames):
        source = halo if slot < frames else own
        for row in range(rows):
            fill_shifted(taps, slot, row + 1, source[slot % frames, row])
    for s in range(frames):
        for a in range(3):
            slot = s + a
            columns = jnp.concatenate(
                [
                    taps[e, slot, b : b + rows].reshape(rows * width, lanes)
                    for b in range(3)
                    for e in range(3)
                ],
                axis=1,
            )
            block = weight[a * 9 * lanes : (a + 1) * 9 * lanes, :]
            term = valid[s, a] * jnp.dot(columns, block, preferred_element_type=jnp.float32)
            if a == 0:
                acc[...] = term
            else:
                acc[...] = acc[...] + term
        done = acc[...].astype(out.dtype).reshape(parts, each, width, channels)
        for part in range(parts):
            out[part, s] = done[part]


VMEM = pl.BlockSpec(memory_space=pltpu.VMEM)
SMEM = pl.BlockSpec(memory_space=pltpu.SMEM)
PARAMS = pltpu.CompilerParams(vmem_limit_bytes=52 * 1024 * 1024)


def conv_one_call(valid, halo, own, weight):
    parts, frames, each, width, channels = own.shape
    rows = parts * each
    flops = 2 * 6 * rows * width * 9 * channels * LANE
    return pl.pallas_call(
        conv_one_kernel,
        out_shape=jax.ShapeDtypeStruct((frames, rows, width, LANE), jnp.float32),
        in_specs=[SMEM, VMEM, VMEM, VMEM],
        out_specs=VMEM,
        scratch_shapes=[pltpu.VMEM((3, 2 * frames, rows + 2, width, channels), jnp.bfloat16)],
        compiler_params=PARAMS,
        cost_estimate=pl.CostEstimate(flops=flops, bytes_accessed=6_000_000, transcendentals=0),
        name="conv_one",
    )(valid, halo, own, weight)


def conv_two_call(valid, halo, own, weight, parts):
    frames, rows, width, lanes = own.shape
    channels = weight.shape[1]
    flops = 2 * 6 * rows * width * 9 * lanes * channels
    return pl.pallas_call(
        conv_two_kernel,
        out_shape=jax.ShapeDtypeStruct((parts, frames, rows // parts, width, channels), jnp.bfloat16),
        in_specs=[SMEM, VMEM, VMEM, VMEM],
        out_specs=VMEM,
        scratch_shapes=[
            pltpu.VMEM((3, 2 * frames, rows + 2, width, lanes), jnp.bfloat16),
            pltpu.VMEM((rows * width, channels), jnp.float32),
        ],
        compiler_params=PARAMS,
        cost_estimate=pl.CostEstimate(flops=flops, bytes_accessed=6_000_000, transcendentals=0),
        name="conv_two",
    )(valid, halo, own, weight)


def pick(rows, columns, transposed, part, step):
    big = lax.broadcasted_iota(jnp.int32, (rows, columns), 1 if transposed else 0)
    small = lax.broadcasted_iota(jnp.int32, (rows, columns), 0 if transposed else 1)
    return (big == step * small + part).astype(jnp.bfloat16)


def body(latents, frame_counts, gain_one, gain_two, conv_one, conv_two):
    part = lax.axis_index("tile")
    parts = lax.axis_size("tile")
    side = lax.axis_index("group") % 2
    counts = frame_counts.reshape(-1)
    source = latents[0].astype(jnp.float32)
    frames, each, width, channels = source.shape
    share = channels // parts
    shard = conv_one.shape[0]
    rows = parts * each

    with jax.named_scope("weights"):
        take = pick(channels, share, False, part, parts)
        mine_one = jnp.dot(conv_one, take, preferred_element_type=jnp.float32).astype(jnp.bfloat16)
        pairs = [(i, i ^ 1) for i in range(lax.axis_size("group"))]
        other = lax.ppermute(conv_two, "group", pairs)
        couple = jnp.concatenate(
            [jnp.where(side == 0, conv_two, other), jnp.where(side == 0, other, conv_two)], axis=0
        )
        half = shard // 2
        rows_take = pick(half, 2 * shard, True, part, parts)
        mine_two = jnp.dot(rows_take, couple, preferred_element_type=jnp.float32).astype(jnp.bfloat16)
        mine_two = lax.dynamic_slice_in_dim(mine_two, side * (channels // 2), channels // 2, axis=1)
        mine = jnp.concatenate([mine_one[:half], mine_one[half:], mine_two], axis=1)
        everything = lax.all_gather(mine, SLOT + ("group",), axis=0)
        weight_one = jnp.stack([everything[:, :, :share], everything[:, :, share : 2 * share]], axis=1)
        weight_one = weight_one.reshape(-1, share)
        weight_one = jnp.pad(weight_one, ((0, 0), (0, LANE - share)))
        weight_two = everything[:, :, 2 * share :].reshape(-1, 2, half, channels // 2)
        weight_two = jnp.swapaxes(weight_two, 1, 2).reshape(-1, share, channels)
        weight_two = jnp.pad(weight_two, ((0, 0), (0, LANE - share), (0, 0))).reshape(-1, channels)

    base = lax.axis_index(SLOT) * frames
    slots = base + jnp.arange(frames, dtype=jnp.int32)
    begins = video_start(slots, counts)
    before = 2 - jnp.arange(3, dtype=jnp.int32)
    valid = (slots[:, None] - before[None, :] >= begins[:, None]).astype(jnp.float32)

    with jax.named_scope("first"):
        mean_sq = jnp.mean(source * source, axis=-1, keepdims=True)
        hidden_one = jax.nn.silu(source * lax.rsqrt(mean_sq + EPS) * gain_one).astype(jnp.bfloat16)
        prior = earlier(hidden_one)
        own_all = spread(hidden_one, "tile")
        prior_all = spread(prior, "tile")
        first = conv_one_call(valid, prior_all, own_all, weight_one)

    with jax.named_scope("second"):
        squares = jnp.sum(first * first, axis=-1)
        squares = jnp.sum(spread(squares, "tile"), axis=0)
        gain_mine = lax.dynamic_index_in_dim(gain_two.reshape(share, parts), part, 1, keepdims=False)
        gain_mine = jnp.pad(gain_mine, (0, LANE - share))
        scale = lax.rsqrt(squares / channels + EPS)
        hidden_two = jax.nn.silu(first * scale[..., None] * gain_mine).astype(jnp.bfloat16)
        prior_two = earlier(hidden_two)
        partial_sums = conv_two_call(valid, prior_two, hidden_two, weight_two, parts)
        arrived = lax.all_to_all(partial_sums, "tile", 0, 0)
        second = jnp.sum(arrived.astype(jnp.float32), axis=0)

    block = (source + second).astype(jnp.bfloat16)
    result = jnp.broadcast_to(
        block[:, :, None, :, None, :], (frames, each, 2, width, 2, channels)
    ).reshape(frames, 2 * each, 2 * width, channels)
    return result[None]


def solution(mesh):
    sizes = mesh.devices.shape
    fine = Mesh(mesh.devices.reshape((sizes[0] // 2, 2) + sizes[1:]), ("z", "core", "tile", "group"))
    in_specs = (
        P("group", SLOT, "tile", None, None),
        P("group", None),
        P(),
        P(),
        P(SLOT + ("group",), None),
        P(SLOT + ("group",), None),
    )
    out_specs = P("group", SLOT, "tile", None, None)
    return jax.shard_map(body, mesh=fine, in_specs=in_specs, out_specs=out_specs, check_vma=False)
```

```python
import functools
import jax
import jax.numpy as jnp
from jax import lax
from jax.experimental import pallas as pl
from jax.experimental.pallas import tpu as pltpu
from jax.sharding import Mesh, PartitionSpec as P

EPS = 1e-06
SLOT = ("z", "core")
LANE = 128


def video_start(slots, counts):
    starts = jnp.cumsum(counts) - counts
    hit = starts[None, :] <= slots[:, None]
    return jnp.max(jnp.where(hit, starts[None, :], 0), axis=1)


def spread(x, axis):
    n = lax.axis_size(axis)
    return lax.all_to_all(jnp.broadcast_to(x[None], (n,) + x.shape), axis, 0, 0)


def earlier(x):
    n = lax.axis_size(SLOT)
    return lax.ppermute(x, SLOT, [(i, i + 1) for i in range(n - 1)])


def fill_shifted(taps, slot, row, frame_row):
    width, channels = frame_row.shape
    wide = frame_row.astype(jnp.float32)
    col = lax.broadcasted_iota(jnp.int32, (width, channels), 0)
    left = jnp.where(col == 0, 0.0, pltpu.roll(wide, 1, 0))
    right = jnp.where(col == width - 1, 0.0, pltpu.roll(wide, width - 1, 0))
    taps[0, slot, row] = left.astype(frame_row.dtype)
    taps[1, slot, row] = frame_row
    taps[2, slot, row] = right.astype(frame_row.dtype)


def clear_border(taps):
    _, slots, rows, width, channels = taps.shape
    blank = jnp.zeros((width, channels), taps.dtype)
    for e in range(3):
        for slot in range(slots):
            taps[e, slot, 0] = blank
            taps[e, slot, rows - 1] = blank


def conv_one_kernel(share, valid, halo, own, weight, out, taps):
    parts, frames, each, width, channels = own.shape
    rows = parts * each
    clear_border(taps)
    for slot in range(2 * frames):
        source = halo if slot < frames else own
        for row in range(rows):
            fill_shifted(taps, slot, row + 1, source[row // each, slot % frames, row % each])
    for slot in range(2 * frames):
        pairs = [(s, slot - s) for s in range(frames) if 0 <= slot - s < 3]
        total = None
        for b in range(3):
            columns = jnp.concatenate(
                [taps[e, slot, b : b + rows].reshape(rows * width, channels) for e in range(3)], axis=1
            )
            blocks = []
            for _, a in pairs:
                first = (a * 3 + b) * 3 * channels
                blocks.append(weight[first : first + 3 * channels, :])
            packed = blocks[0] if len(blocks) == 1 else jnp.concatenate(blocks, axis=1)
            term = jnp.dot(columns, packed, preferred_element_type=jnp.float32)
            total = term if total is None else total + term
        for i, (s, a) in enumerate(pairs):
            piece = valid[s, a] * total[:, i * LANE : (i + 1) * LANE]
            lane = lax.broadcasted_iota(jnp.int32, piece.shape, 1)
            piece = jnp.where(lane < share, piece, 0.0).reshape(rows, width, LANE)
            if a == 0:
                out[s] = piece
            else:
                out[s] = out[s] + piece


def conv_two_kernel(valid, halo, own, weight, out, taps, acc):
    frames, rows, width, lanes = own.shape
    parts = out.shape[0]
    each = rows // parts
    channels = weight.shape[1]
    clear_border(taps)
    for slot in range(2 * frames):
        source = halo if slot < frames else own
        for row in range(rows):
            fill_shifted(taps, slot, row + 1, source[slot % frames, row])
    for s in range(frames):
        for a in range(3):
            slot = s + a
            columns = jnp.concatenate(
                [
                    taps[e, slot, b : b + rows].reshape(rows * width, lanes)
                    for b in range(3)
                    for e in range(3)
                ],
                axis=1,
            )
            block = weight[a * 9 * lanes : (a + 1) * 9 * lanes, :]
            term = valid[s, a] * jnp.dot(columns, block, preferred_element_type=jnp.float32)
            if a == 0:
                acc[...] = term
            else:
                acc[...] = acc[...] + term
        done = acc[...].astype(out.dtype).reshape(parts, each, width, channels)
        for part in range(parts):
            out[part, s] = done[part]


VMEM = pl.BlockSpec(memory_space=pltpu.VMEM)
SMEM = pl.BlockSpec(memory_space=pltpu.SMEM)
PARAMS = pltpu.CompilerParams(vmem_limit_bytes=52 * 1024 * 1024)


def conv_one_call(valid, halo, own, weight):
    parts, frames, each, width, channels = own.shape
    rows = parts * each
    flops = 2 * 6 * rows * width * 9 * channels * LANE
    return pl.pallas_call(
        functools.partial(conv_one_kernel, channels // parts),
        out_shape=jax.ShapeDtypeStruct((frames, rows, width, LANE), jnp.float32),
        in_specs=[SMEM, VMEM, VMEM, VMEM],
        out_specs=VMEM,
        scratch_shapes=[pltpu.VMEM((3, 2 * frames, rows + 2, width, channels), jnp.bfloat16)],
        compiler_params=PARAMS,
        cost_estimate=pl.CostEstimate(flops=flops, bytes_accessed=6_000_000, transcendentals=0),
        name="conv_one",
    )(valid, halo, own, weight)


def conv_two_call(valid, halo, own, weight, parts):
    frames, rows, width, lanes = own.shape
    channels = weight.shape[1]
    flops = 2 * 6 * rows * width * 9 * lanes * channels
    return pl.pallas_call(
        conv_two_kernel,
        out_shape=jax.ShapeDtypeStruct((parts, frames, rows // parts, width, channels), jnp.bfloat16),
        in_specs=[SMEM, VMEM, VMEM, VMEM],
        out_specs=VMEM,
        scratch_shapes=[
            pltpu.VMEM((3, 2 * frames, rows + 2, width, lanes), jnp.bfloat16),
            pltpu.VMEM((rows * width, channels), jnp.float32),
        ],
        compiler_params=PARAMS,
        cost_estimate=pl.CostEstimate(flops=flops, bytes_accessed=6_000_000, transcendentals=0),
        name="conv_two",
    )(valid, halo, own, weight)


def gathered(core, mine, other, k, c):
    left, right = mine[k].astype(jnp.float32), other[k].astype(jnp.float32)
    return jnp.where(core[0] == c, left, right)


def assemble_one_kernel(core, mine, other, out, wide):
    chips, piece_rows, lanes = mine.shape
    shard = out.shape[0] // (2 * chips)
    share = lanes // 4
    for k in range(chips):
        z, y = k // 4, k % 4
        for c in range(2):
            piece = gathered(core, mine, other, k, c)
            start = shard * (8 * z + 4 * c + y)
            for j in range(4):
                rows = min(piece_rows, shard - j * piece_rows)
                low = (j * share) // LANE * LANE
                window = piece[:, low : min(low + 2 * LANE, lanes)]
                shift = j * share - low
                if shift:
                    window = pltpu.roll(window, window.shape[1] - shift, 1)
                first = start + j * piece_rows
                wide[first : first + rows, :] = window[:rows, :LANE]
    out[...] = wide[...].astype(out.dtype)


def assemble_two_kernel(core, mine, other, out, wide, piece_buf):
    chips, piece_rows, channels = mine.shape
    share = piece_rows * 2 - 1
    taps = out.shape[0] // LANE
    width = share * chips // taps
    for t in range(taps):
        wide[t * LANE + width : (t + 1) * LANE, :] = jnp.zeros((LANE - width, channels), jnp.float32)
    for k in range(chips):
        z, y = k // 4, k % 4
        for c in range(2):
            i = 8 * z + 4 * c + y
            first = share * (i // 2) + (piece_rows - 1) * (i % 2)
            piece = gathered(core, mine, other, k, c)
            split = min(piece_rows, (first // width + 1) * width - first)
            at = first // width * LANE + first % width
            if split == piece_rows:
                wide[at : at + piece_rows, :] = piece
            else:
                piece_buf[0:piece_rows, :] = piece
                wide[at : at + split, :] = piece_buf[0:split, :]
                at = (first // width + 1) * LANE
                wide[at : at + piece_rows - split, :] = piece_buf[split:piece_rows, :]
    out[...] = wide[...].astype(out.dtype)


def assemble_call(kernel, core, mine, other, shape, extra, name):
    return pl.pallas_call(
        kernel,
        out_shape=jax.ShapeDtypeStruct(shape, jnp.bfloat16),
        in_specs=[SMEM, VMEM, VMEM],
        out_specs=VMEM,
        scratch_shapes=[pltpu.VMEM(shape, jnp.float32)] + extra,
        compiler_params=PARAMS,
        cost_estimate=pl.CostEstimate(flops=4_000_000, bytes_accessed=5_000_000, transcendentals=0),
        name=name,
    )(core, mine, other)


def pick(rows, columns, transposed, part, step):
    big = lax.broadcasted_iota(jnp.int32, (rows, columns), 1 if transposed else 0)
    small = lax.broadcasted_iota(jnp.int32, (rows, columns), 0 if transposed else 1)
    return (big == step * small + part).astype(jnp.bfloat16)


def body(latents, frame_counts, gain_one, gain_two, conv_one, conv_two):
    part = lax.axis_index("tile")
    parts = lax.axis_size("tile")
    side = lax.axis_index("group") % 2
    core = lax.axis_index("core")
    counts = frame_counts.reshape(-1)
    source = latents[0].astype(jnp.float32)
    frames, each, width, channels = source.shape
    share = channels // parts
    shard = conv_one.shape[0]
    piece_rows = shard // 4 + 1
    chips = lax.axis_size("z") * lax.axis_size("group")
    flag = core.astype(jnp.int32).reshape(1)

    def from_all_chips(piece):
        mine = spread(piece, ("z", "group"))
        return mine, lax.ppermute(mine, "core", [(0, 1), (1, 0)])

    with jax.named_scope("weight_one"):
        take = pick(channels, share, False, part, parts)
        piece = jnp.dot(conv_one, take, preferred_element_type=jnp.float32).astype(jnp.bfloat16)
        piece = jnp.pad(piece, ((0, 4 * piece_rows - shard), (0, 0)))
        piece = jnp.concatenate([piece[j * piece_rows : (j + 1) * piece_rows] for j in range(4)], axis=1)
        mine_one, other_one = from_all_chips(piece)
        weight_one = assemble_call(
            assemble_one_kernel, flag, mine_one, other_one, (2 * chips * shard, LANE), [], "assemble_one"
        )

    with jax.named_scope("weight_two"):
        conv_two, mine_one = lax.optimization_barrier((conv_two, mine_one))
        pairs = [(i, i ^ 1) for i in range(lax.axis_size("group"))]
        other = lax.ppermute(conv_two, "group", pairs)
        couple = jnp.concatenate(
            [jnp.where(side == 0, conv_two, other), jnp.where(side == 0, other, conv_two)], axis=0
        )
        rows_take = pick(piece_rows, 2 * shard, True, part + parts * (piece_rows - 1) * side, parts)
        piece = jnp.dot(rows_take, couple, preferred_element_type=jnp.float32).astype(jnp.bfloat16)
        mine_two, other_two = from_all_chips(piece)
        taps = 2 * chips * shard // channels
        weight_two = assemble_call(
            assemble_two_kernel, flag, mine_two, other_two, (taps * LANE, channels),
            [pltpu.VMEM((48, channels), jnp.float32)], "assemble_two"
        )

    base = lax.axis_index(SLOT) * frames
    slots = base + jnp.arange(frames, dtype=jnp.int32)
    begins = video_start(slots, counts)
    before = 2 - jnp.arange(3, dtype=jnp.int32)
    valid = (slots[:, None] - before[None, :] >= begins[:, None]).astype(jnp.float32)

    with jax.named_scope("first"):
        mean_sq = jnp.mean(source * source, axis=-1, keepdims=True)
        hidden_one = jax.nn.silu(source * lax.rsqrt(mean_sq + EPS) * gain_one).astype(jnp.bfloat16)
        prior = earlier(hidden_one)
        own_all = spread(hidden_one, "tile")
        prior_all = spread(prior, "tile")
        first = conv_one_call(valid, prior_all, own_all, weight_one)

    with jax.named_scope("second"):
        squares = jnp.sum(first * first, axis=-1)
        squares = jnp.sum(spread(squares, "tile"), axis=0)
        gain_mine = lax.dynamic_index_in_dim(gain_two.reshape(share, parts), part, 1, keepdims=False)
        gain_mine = jnp.pad(gain_mine, (0, LANE - share))
        scale = lax.rsqrt(squares / channels + EPS)
        hidden_two = jax.nn.silu(first * scale[..., None] * gain_mine).astype(jnp.bfloat16)
        prior_two = earlier(hidden_two)
        partial_sums = conv_two_call(valid, prior_two, hidden_two, weight_two, parts)
        arrived = lax.all_to_all(partial_sums, "tile", 0, 0)
        second = jnp.sum(arrived.astype(jnp.float32), axis=0)

    block = (source + second).astype(jnp.bfloat16)
    result = jnp.broadcast_to(
        block[:, :, None, :, None, :], (frames, each, 2, width, 2, channels)
    ).reshape(frames, 2 * each, 2 * width, channels)
    return result[None]


def solution(mesh):
    sizes = mesh.devices.shape
    fine = Mesh(mesh.devices.reshape((sizes[0] // 2, 2) + sizes[1:]), ("z", "core", "tile", "group"))
    in_specs = (
        P("group", SLOT, "tile", None, None),
        P("group", None),
        P(),
        P(),
        P(SLOT + ("group",), None),
        P(SLOT + ("group",), None),
    )
    out_specs = P("group", SLOT, "tile", None, None)
    return jax.shard_map(body, mesh=fine, in_specs=in_specs, out_specs=out_specs, check_vma=False)
```

```python
import functools
import jax
import jax.numpy as jnp
from jax import lax
from jax.experimental import pallas as pl
from jax.experimental.pallas import tpu as pltpu
from jax.sharding import Mesh, PartitionSpec as P

EPS = 1e-06
SLOT = ("z", "core")
LANE = 128
TILE_ROWS = 48


def video_start(slots, counts):
    starts = jnp.cumsum(counts) - counts
    hit = starts[None, :] <= slots[:, None]
    return jnp.max(jnp.where(hit, starts[None, :], 0), axis=1)


def spread(x, axis):
    n = lax.axis_size(axis)
    return lax.all_to_all(jnp.broadcast_to(x[None], (n,) + x.shape), axis, 0, 0)


def earlier(x):
    n = lax.axis_size(SLOT)
    return lax.ppermute(x, SLOT, [(i, i + 1) for i in range(n - 1)])


def onward(x, by):
    n = lax.axis_size("tile")
    return lax.ppermute(x, "tile", [(i, (i + by) % n) for i in range(n)])


def fill_shifted(taps, slot, row, frame_row):
    width, channels = frame_row.shape
    wide = frame_row.astype(jnp.float32)
    col = lax.broadcasted_iota(jnp.int32, (width, channels), 0)
    left = jnp.where(col == 0, 0.0, pltpu.roll(wide, 1, 0))
    right = jnp.where(col == width - 1, 0.0, pltpu.roll(wide, width - 1, 0))
    taps[0, slot, row] = left.astype(frame_row.dtype)
    taps[1, slot, row] = frame_row
    taps[2, slot, row] = right.astype(frame_row.dtype)


def clear_border(taps):
    _, slots, rows, width, channels = taps.shape
    blank = jnp.zeros((width, channels), taps.dtype)
    for e in range(3):
        for slot in range(slots):
            taps[e, slot, 0] = blank
            taps[e, slot, rows - 1] = blank


def conv_one_kernel(share, valid, part, halo, own, weight, out, taps):
    parts, frames, each, width, channels = own.shape
    rows = parts * each
    clear_border(taps)
    for back in range(parts):
        top = lax.rem(part[0] + parts - back, parts) * each + 1
        for slot in range(2 * frames):
            source = halo if slot < frames else own
            for j in range(each):
                fill_shifted(taps, slot, top + j, source[back, slot % frames, j])
    for slot in range(2 * frames):
        pairs = [(s, slot - s) for s in range(frames) if 0 <= slot - s < 3]
        total = None
        for b in range(3):
            columns = jnp.concatenate(
                [taps[e, slot, b : b + rows].reshape(rows * width, channels) for e in range(3)], axis=1
            )
            blocks = []
            for _, a in pairs:
                first = (a * 3 + b) * 3 * channels
                blocks.append(weight[first : first + 3 * channels, :])
            packed = blocks[0] if len(blocks) == 1 else jnp.concatenate(blocks, axis=1)
            term = jnp.dot(columns, packed, preferred_element_type=jnp.float32)
            total = term if total is None else total + term
        for i, (s, a) in enumerate(pairs):
            piece = valid[s, a] * total[:, i * LANE : (i + 1) * LANE]
            lane = lax.broadcasted_iota(jnp.int32, piece.shape, 1)
            piece = jnp.where(lane < share, piece, 0.0).reshape(rows, width, LANE)
            if a == 0:
                out[s] = piece
            else:
                out[s] = out[s] + piece


def conv_two_kernel(s, valid, part, halo, own, weight, *rest):
    *outs, taps, acc = rest
    frames, rows, width, lanes = own.shape
    parts = len(outs)
    each = rows // parts
    channels = weight.shape[1]
    clear_border(taps)
    for a in range(3):
        source = halo if s + a < frames else own
        for row in range(rows):
            fill_shifted(taps, a, row + 1, source[(s + a) % frames, row])
    for a in range(3):
        columns = jnp.concatenate(
            [
                taps[e, a, b : b + rows].reshape(rows * width, lanes)
                for b in range(3)
                for e in range(3)
            ],
            axis=1,
        )
        block = weight[a * 9 * lanes : (a + 1) * 9 * lanes, :]
        term = valid[s, a] * jnp.dot(columns, block, preferred_element_type=jnp.float32)
        if a == 0:
            acc[...] = term
        else:
            acc[...] = acc[...] + term
    for d in range(parts):
        top = pl.multiple_of(lax.rem(part[0] + d, parts) * (each * width), 64)
        outs[d][...] = acc[pl.ds(top, each * width), :].astype(outs[d].dtype).reshape(each, width, channels)


VMEM = pl.BlockSpec(memory_space=pltpu.VMEM)
SMEM = pl.BlockSpec(memory_space=pltpu.SMEM)
PARAMS = pltpu.CompilerParams(vmem_limit_bytes=52 * 1024 * 1024)


def conv_one_call(valid, part, halo, own, weight):
    parts, frames, each, width, channels = own.shape
    rows = parts * each
    flops = 2 * 6 * rows * width * 9 * channels * LANE
    return pl.pallas_call(
        functools.partial(conv_one_kernel, channels // parts),
        out_shape=jax.ShapeDtypeStruct((frames, rows, width, LANE), jnp.float32),
        in_specs=[SMEM, SMEM, VMEM, VMEM, VMEM],
        out_specs=VMEM,
        scratch_shapes=[pltpu.VMEM((3, 2 * frames, rows + 2, width, channels), jnp.bfloat16)],
        compiler_params=PARAMS,
        cost_estimate=pl.CostEstimate(flops=flops, bytes_accessed=6_000_000, transcendentals=0),
        name="conv_one",
    )(valid, part, halo, own, weight)


def conv_two_call(slot, valid, part, halo, own, weight, parts):
    frames, rows, width, lanes = own.shape
    channels = weight.shape[1]
    flops = 2 * 3 * rows * width * 9 * lanes * channels
    return pl.pallas_call(
        functools.partial(conv_two_kernel, slot),
        out_shape=[jax.ShapeDtypeStruct((rows // parts, width, channels), jnp.bfloat16)] * parts,
        in_specs=[SMEM, SMEM, VMEM, VMEM, VMEM],
        out_specs=[VMEM] * parts,
        scratch_shapes=[
            pltpu.VMEM((3, 3, rows + 2, width, lanes), jnp.bfloat16),
            pltpu.VMEM((rows * width, channels), jnp.float32),
        ],
        compiler_params=PARAMS,
        cost_estimate=pl.CostEstimate(flops=flops, bytes_accessed=6_000_000, transcendentals=0),
        name="conv_two",
    )(valid, part, halo, own, weight)


def gathered(core, mine, other, k, c):
    left, right = mine[k].astype(jnp.float32), other[k].astype(jnp.float32)
    return jnp.where(core[0] == c, left, right)


def assemble_one_kernel(core, mine, other, out, wide):
    chips, _, lanes = mine.shape
    shard = out.shape[0] // (2 * chips)
    share = lanes // 4
    piece_rows = shard // 4 + 1
    for k in range(chips):
        y, z = k // 8, k % 8
        for c in range(2):
            piece = gathered(core, mine, other, k, c)
            start = shard * (8 * z + 4 * c + y)
            for j in range(4):
                rows = min(piece_rows, shard - j * piece_rows)
                low = (j * share) // LANE * LANE
                window = piece[:, low : min(low + 2 * LANE, lanes)]
                shift = j * share - low
                if shift:
                    window = pltpu.roll(window, window.shape[1] - shift, 1)
                first = start + j * piece_rows
                wide[first : first + rows, :] = window[:rows, :LANE]
    out[...] = wide[...].astype(out.dtype)


def assemble_two_kernel(core, mine, other, out, wide, piece_buf):
    chips, _, channels = mine.shape
    taps = out.shape[0] // LANE
    width = channels // 4
    share = taps * width // chips
    piece_rows = (share + 1) // 2
    for t in range(taps):
        wide[t * LANE + width : (t + 1) * LANE, :] = jnp.zeros((LANE - width, channels), jnp.float32)
    for k in range(chips):
        y, z = k // 8, k % 8
        for c in range(2):
            i = 8 * z + 4 * c + y
            first = share * (i // 2) + (piece_rows - 1) * (i % 2)
            piece = gathered(core, mine, other, k, c)[:piece_rows]
            split = min(piece_rows, (first // width + 1) * width - first)
            at = first // width * LANE + first % width
            if split == piece_rows:
                wide[at : at + piece_rows, :] = piece
            else:
                piece_buf[0:piece_rows, :] = piece
                wide[at : at + split, :] = piece_buf[0:split, :]
                at = (first // width + 1) * LANE
                wide[at : at + piece_rows - split, :] = piece_buf[split:piece_rows, :]
    out[...] = wide[...].astype(out.dtype)


def assemble_call(kernel, core, mine, other, shape, extra, name):
    return pl.pallas_call(
        kernel,
        out_shape=jax.ShapeDtypeStruct(shape, jnp.bfloat16),
        in_specs=[SMEM, VMEM, VMEM],
        out_specs=VMEM,
        scratch_shapes=[pltpu.VMEM(shape, jnp.float32)] + extra,
        compiler_params=PARAMS,
        cost_estimate=pl.CostEstimate(flops=4_000_000, bytes_accessed=5_000_000, transcendentals=0),
        name=name,
    )(core, mine, other)


def pick(rows, columns, transposed, part, step):
    big = lax.broadcasted_iota(jnp.int32, (rows, columns), 1 if transposed else 0)
    small = lax.broadcasted_iota(jnp.int32, (rows, columns), 0 if transposed else 1)
    return (big == step * small + part).astype(jnp.bfloat16)


def body(latents, frame_counts, gain_one, gain_two, conv_one, conv_two):
    part = lax.axis_index("tile")
    parts = lax.axis_size("tile")
    side = lax.axis_index("group") % 2
    core = lax.axis_index("core")
    counts = frame_counts.reshape(-1)
    source = latents[0].astype(jnp.float32)
    frames, each, width, channels = source.shape
    share = channels // parts
    shard = conv_one.shape[0]
    piece_rows = shard // 4 + 1
    chips = lax.axis_size("z") * lax.axis_size("group")
    flag = core.astype(jnp.int32).reshape(1)

    def from_all_chips(piece):
        mine = spread(spread(piece, "z"), "group").reshape(chips, TILE_ROWS, channels)
        return mine, lax.ppermute(mine, "core", [(0, 1), (1, 0)])

    with jax.named_scope("weight_one"):
        take = pick(channels, share, False, part, parts)
        piece = jnp.dot(conv_one, take, preferred_element_type=jnp.float32).astype(jnp.bfloat16)
        piece = jnp.pad(piece, ((0, 4 * piece_rows - shard), (0, 0)))
        piece = jnp.concatenate([piece[j * piece_rows : (j + 1) * piece_rows] for j in range(4)], axis=1)
        piece = jnp.pad(piece, ((0, TILE_ROWS - piece_rows), (0, 0)))
        mine_one, other_one = from_all_chips(piece)
        weight_one = assemble_call(
            assemble_one_kernel, flag, mine_one, other_one, (2 * chips * shard, LANE), [], "assemble_one"
        )

    with jax.named_scope("weight_two"):
        conv_two, mine_one = lax.optimization_barrier((conv_two, mine_one))
        pairs = [(i, i ^ 1) for i in range(lax.axis_size("group"))]
        other = lax.ppermute(conv_two, "group", pairs)
        couple = jnp.concatenate(
            [jnp.where(side == 0, conv_two, other), jnp.where(side == 0, other, conv_two)], axis=0
        )
        rows_take = pick(TILE_ROWS, 2 * shard, True, part + parts * (piece_rows - 1) * side, parts)
        piece = jnp.dot(rows_take, couple, preferred_element_type=jnp.float32).astype(jnp.bfloat16)
        mine_two, other_two = from_all_chips(piece)
        taps = 2 * chips * shard // channels
        weight_two = assemble_call(
            assemble_two_kernel, flag, mine_two, other_two, (taps * LANE, channels),
            [pltpu.VMEM((TILE_ROWS, channels), jnp.float32)], "assemble_two"
        )

    base = lax.axis_index(SLOT) * frames
    slots = base + jnp.arange(frames, dtype=jnp.int32)
    begins = video_start(slots, counts)
    before = 2 - jnp.arange(3, dtype=jnp.int32)
    valid = (slots[:, None] - before[None, :] >= begins[:, None]).astype(jnp.float32)

    with jax.named_scope("first"):
        mean_sq = jnp.mean(source * source, axis=-1, keepdims=True)
        hidden_one = jax.nn.silu(source * lax.rsqrt(mean_sq + EPS) * gain_one).astype(jnp.bfloat16)
        own_all = jnp.stack([hidden_one] + [onward(hidden_one, d) for d in range(1, parts)])
        prior_all = earlier(own_all)
        part_ref = part.astype(jnp.int32).reshape(1)
        first = conv_one_call(valid, part_ref, prior_all, own_all, weight_one)

    with jax.named_scope("second"):
        squares = jnp.sum(first * first, axis=-1)
        squares = squares + sum(onward(squares, d) for d in range(1, parts))
        gain_mine = lax.dynamic_index_in_dim(gain_two.reshape(share, parts), part, 1, keepdims=False)
        gain_mine = jnp.pad(gain_mine, (0, LANE - share))
        scale = lax.rsqrt(squares / channels + EPS)
        hidden_two = jax.nn.silu(first * scale[..., None] * gain_mine).astype(jnp.bfloat16)
        prior_two = earlier(hidden_two)
        sums = []
        for slot in reversed(range(frames)):
            mine, *rest = conv_two_call(slot, valid, part_ref, prior_two, hidden_two, weight_two, parts)
            arrived = [onward(r, d) for d, r in enumerate(rest, 1)]
            sums.append(sum((r.astype(jnp.float32) for r in arrived), mine.astype(jnp.float32)))
        second = jnp.stack(sums[::-1])

    block = (source + second).astype(jnp.bfloat16)
    result = jnp.broadcast_to(
        block[:, :, None, :, None, :], (frames, each, 2, width, 2, channels)
    ).reshape(frames, 2 * each, 2 * width, channels)
    return result[None]


def solution(mesh):
    sizes = mesh.devices.shape
    fine = Mesh(mesh.devices.reshape((sizes[0] // 2, 2) + sizes[1:]), ("z", "core", "tile", "group"))
    in_specs = (
        P("group", SLOT, "tile", None, None),
        P("group", None),
        P(),
        P(),
        P(SLOT + ("group",), None),
        P(SLOT + ("group",), None),
    )
    out_specs = P("group", SLOT, "tile", None, None)
    return jax.shard_map(body, mesh=fine, in_specs=in_specs, out_specs=out_specs, check_vma=False)
```

```python
import functools
import jax
import jax.numpy as jnp
from jax import lax
from jax.experimental import pallas as pl
from jax.experimental.pallas import tpu as pltpu
from jax.sharding import Mesh, PartitionSpec as P

EPS = 1e-06
SLOT = ("z", "core")
LANE = 128
TILE_ROWS = 48


def video_start(slots, counts):
    starts = jnp.cumsum(counts) - counts
    hit = starts[None, :] <= slots[:, None]
    return jnp.max(jnp.where(hit, starts[None, :], 0), axis=1)


def earlier(x):
    n = lax.axis_size(SLOT)
    return lax.ppermute(x, SLOT, [(i, i + 1) for i in range(n - 1)])


def onward(x, by, axis="tile"):
    n = lax.axis_size(axis)
    return lax.ppermute(x, axis, [(i, (i + by) % n) for i in range(n)])


def from_all(x, axis):
    return jnp.stack([x] + [onward(x, d, axis) for d in range(1, lax.axis_size(axis))])


def fill_shifted(taps, slot, row, frame_row):
    width, channels = frame_row.shape
    wide = frame_row.astype(jnp.float32)
    col = lax.broadcasted_iota(jnp.int32, (width, channels), 0)
    left = jnp.where(col == 0, 0.0, pltpu.roll(wide, 1, 0))
    right = jnp.where(col == width - 1, 0.0, pltpu.roll(wide, width - 1, 0))
    taps[0, slot, row] = left.astype(frame_row.dtype)
    taps[1, slot, row] = frame_row
    taps[2, slot, row] = right.astype(frame_row.dtype)


def clear_border(taps):
    _, slots, rows, width, channels = taps.shape
    blank = jnp.zeros((width, channels), taps.dtype)
    for e in range(3):
        for slot in range(slots):
            taps[e, slot, 0] = blank
            taps[e, slot, rows - 1] = blank


def conv_one_kernel(share, valid, part, halo, own, weight, out, taps):
    parts, frames, each, width, channels = own.shape
    rows = parts * each
    clear_border(taps)
    for back in range(parts):
        top = lax.rem(part[0] + parts - back, parts) * each + 1
        for slot in range(2 * frames):
            source = halo if slot < frames else own
            for j in range(each):
                fill_shifted(taps, slot, top + j, source[back, slot % frames, j])
    for slot in range(2 * frames):
        pairs = [(s, slot - s) for s in range(frames) if 0 <= slot - s < 3]
        total = None
        for b in range(3):
            columns = jnp.concatenate(
                [taps[e, slot, b : b + rows].reshape(rows * width, channels) for e in range(3)], axis=1
            )
            blocks = []
            for _, a in pairs:
                first = (a * 3 + b) * 3 * channels
                blocks.append(weight[first : first + 3 * channels, :])
            packed = blocks[0] if len(blocks) == 1 else jnp.concatenate(blocks, axis=1)
            term = jnp.dot(columns, packed, preferred_element_type=jnp.float32)
            total = term if total is None else total + term
        for i, (s, a) in enumerate(pairs):
            piece = valid[s, a] * total[:, i * LANE : (i + 1) * LANE]
            lane = lax.broadcasted_iota(jnp.int32, piece.shape, 1)
            piece = jnp.where(lane < share, piece, 0.0).reshape(rows, width, LANE)
            if a == 0:
                out[s] = piece
            else:
                out[s] = out[s] + piece


def conv_two_kernel(s, valid, part, halo, own, weight, *rest):
    *outs, taps, acc = rest
    frames, rows, width, lanes = own.shape
    parts = len(outs)
    each = rows // parts
    channels = weight.shape[1]
    clear_border(taps)
    for a in range(3):
        source = halo if s + a < frames else own
        for row in range(rows):
            fill_shifted(taps, a, row + 1, source[(s + a) % frames, row])
    for a in range(3):
        columns = jnp.concatenate(
            [
                taps[e, a, b : b + rows].reshape(rows * width, lanes)
                for b in range(3)
                for e in range(3)
            ],
            axis=1,
        )
        block = weight[a * 9 * lanes : (a + 1) * 9 * lanes, :]
        term = valid[s, a] * jnp.dot(columns, block, preferred_element_type=jnp.float32)
        if a == 0:
            acc[...] = term
        else:
            acc[...] = acc[...] + term
    for d in range(parts):
        top = pl.multiple_of(lax.rem(part[0] + d, parts) * (each * width), 64)
        outs[d][...] = acc[pl.ds(top, each * width), :].astype(outs[d].dtype).reshape(each, width, channels)


VMEM = pl.BlockSpec(memory_space=pltpu.VMEM)
SMEM = pl.BlockSpec(memory_space=pltpu.SMEM)
PARAMS = pltpu.CompilerParams(vmem_limit_bytes=52 * 1024 * 1024)


def conv_one_call(valid, part, halo, own, weight):
    parts, frames, each, width, channels = own.shape
    rows = parts * each
    flops = 2 * 6 * rows * width * 9 * channels * LANE
    return pl.pallas_call(
        functools.partial(conv_one_kernel, channels // parts),
        out_shape=jax.ShapeDtypeStruct((frames, rows, width, LANE), jnp.float32),
        in_specs=[SMEM, SMEM, VMEM, VMEM, VMEM],
        out_specs=VMEM,
        scratch_shapes=[pltpu.VMEM((3, 2 * frames, rows + 2, width, channels), jnp.bfloat16)],
        compiler_params=PARAMS,
        cost_estimate=pl.CostEstimate(flops=flops, bytes_accessed=6_000_000, transcendentals=0),
        name="conv_one",
    )(valid, part, halo, own, weight)


def conv_two_call(slot, valid, part, halo, own, weight, parts):
    frames, rows, width, lanes = own.shape
    channels = weight.shape[1]
    flops = 2 * 3 * rows * width * 9 * lanes * channels
    return pl.pallas_call(
        functools.partial(conv_two_kernel, slot),
        out_shape=[jax.ShapeDtypeStruct((rows // parts, width, channels), jnp.bfloat16)] * parts,
        in_specs=[SMEM, SMEM, VMEM, VMEM, VMEM],
        out_specs=[VMEM] * parts,
        scratch_shapes=[
            pltpu.VMEM((3, 3, rows + 2, width, lanes), jnp.bfloat16),
            pltpu.VMEM((rows * width, channels), jnp.float32),
        ],
        compiler_params=PARAMS,
        cost_estimate=pl.CostEstimate(flops=flops, bytes_accessed=6_000_000, transcendentals=0),
        name="conv_two",
    )(valid, part, halo, own, weight)


def gathered(place, mine, other, i):
    ys, zs = mine.shape[:2]
    z, c, y = i // (2 * ys), i // ys % 2, i % ys
    back_y = lax.rem(place[1] + ys - y, ys)
    left, right = mine[back_y, z].astype(jnp.float32), other[back_y, z].astype(jnp.float32)
    return jnp.where(place[0] == c, left, right)


def assemble_one_kernel(place, mine, other, out, wide):
    shards = 2 * mine.shape[0] * mine.shape[1]
    lanes = mine.shape[3]
    shard = out.shape[0] // shards
    share = lanes // 4
    piece_rows = shard // 4 + 1
    for i in range(shards):
        piece = gathered(place, mine, other, i)
        for j in range(4):
            rows = min(piece_rows, shard - j * piece_rows)
            low = (j * share) // LANE * LANE
            window = piece[:, low : min(low + 2 * LANE, lanes)]
            shift = j * share - low
            if shift:
                window = pltpu.roll(window, window.shape[1] - shift, 1)
            first = shard * i + j * piece_rows
            wide[first : first + rows, :] = window[:rows, :LANE]
    out[...] = wide[...].astype(out.dtype)


def assemble_two_kernel(place, mine, other, out, wide, piece_buf):
    shards = 2 * mine.shape[0] * mine.shape[1]
    channels = mine.shape[3]
    taps = out.shape[0] // LANE
    width = channels // 4
    share = 2 * taps * width // shards
    piece_rows = (share + 1) // 2
    for t in range(taps):
        wide[t * LANE + width : (t + 1) * LANE, :] = jnp.zeros((LANE - width, channels), jnp.float32)
    for i in range(shards):
        first = share * (i // 2) + (piece_rows - 1) * (i % 2)
        piece = gathered(place, mine, other, i)[:piece_rows]
        split = min(piece_rows, (first // width + 1) * width - first)
        at = first // width * LANE + first % width
        if split == piece_rows:
            wide[at : at + piece_rows, :] = piece
        else:
            piece_buf[0:piece_rows, :] = piece
            wide[at : at + split, :] = piece_buf[0:split, :]
            at = (first // width + 1) * LANE
            wide[at : at + piece_rows - split, :] = piece_buf[split:piece_rows, :]
    out[...] = wide[...].astype(out.dtype)


def assemble_call(kernel, place, mine, other, shape, extra, name):
    return pl.pallas_call(
        kernel,
        out_shape=jax.ShapeDtypeStruct(shape, jnp.bfloat16),
        in_specs=[SMEM, VMEM, VMEM],
        out_specs=VMEM,
        scratch_shapes=[pltpu.VMEM(shape, jnp.float32)] + extra,
        compiler_params=PARAMS,
        cost_estimate=pl.CostEstimate(flops=4_000_000, bytes_accessed=5_000_000, transcendentals=0),
        name=name,
    )(place, mine, other)


def pick(rows, columns, transposed, part, step):
    big = lax.broadcasted_iota(jnp.int32, (rows, columns), 1 if transposed else 0)
    small = lax.broadcasted_iota(jnp.int32, (rows, columns), 0 if transposed else 1)
    return (big == step * small + part).astype(jnp.bfloat16)


def body(latents, frame_counts, gain_one, gain_two, conv_one, conv_two):
    part = lax.axis_index("tile")
    parts = lax.axis_size("tile")
    side = lax.axis_index("group") % 2
    core = lax.axis_index("core")
    counts = frame_counts.reshape(-1)
    source = latents[0].astype(jnp.float32)
    frames, each, width, channels = source.shape
    share = channels // parts
    shard = conv_one.shape[0]
    piece_rows = shard // 4 + 1
    shards = lax.axis_size(SLOT) * lax.axis_size("group")
    place = jnp.stack([core, lax.axis_index("group")]).astype(jnp.int32)

    with jax.named_scope("pixels"):
        mean_sq = jnp.mean(source * source, axis=-1, keepdims=True)
        hidden_one = jax.nn.silu(source * lax.rsqrt(mean_sq + EPS) * gain_one).astype(jnp.bfloat16)
        own_all = from_all(hidden_one, "tile")

    with jax.named_scope("pieces"):
        pairs = [(i, i ^ 1) for i in range(lax.axis_size("group"))]
        other = lax.ppermute(conv_two, "group", pairs)
        couple = jnp.concatenate(
            [jnp.where(side == 0, conv_two, other), jnp.where(side == 0, other, conv_two)], axis=0
        )
        rows_take = pick(TILE_ROWS, 2 * shard, True, part + parts * (piece_rows - 1) * side, parts)
        piece_two = jnp.dot(rows_take, couple, preferred_element_type=jnp.float32).astype(jnp.bfloat16)
        take = pick(channels, share, False, part, parts)
        piece = jnp.dot(conv_one, take, preferred_element_type=jnp.float32).astype(jnp.bfloat16)
        piece = jnp.pad(piece, ((0, 4 * piece_rows - shard), (0, 0)))
        piece = jnp.concatenate([piece[j * piece_rows : (j + 1) * piece_rows] for j in range(4)], axis=1)
        piece = jnp.pad(piece, ((0, TILE_ROWS - piece_rows), (0, 0)))
        pieces = jnp.concatenate([piece, piece_two], axis=0)
        column = lax.all_to_all(jnp.broadcast_to(pieces, (lax.axis_size("z"),) + pieces.shape), "z", 0, 0)

    column, own_all = lax.optimization_barrier((column, own_all))
    with jax.named_scope("weight_one"):
        mine = from_all(column[:, :TILE_ROWS], "group")
        prior_all = earlier(own_all)
        mine, prior_all = lax.optimization_barrier((mine, prior_all))
        swapped = lax.ppermute(mine, "core", [(0, 1), (1, 0)])
        weight_one = assemble_call(
            assemble_one_kernel, place, mine, swapped, (shards * shard, LANE), [], "assemble_one"
        )

    with jax.named_scope("weight_two"):
        column, _ = lax.optimization_barrier((column, mine))
        later = column[:, TILE_ROWS:]
        later = [later] + [onward(later, d, "group") for d in range(1, lax.axis_size("group"))]

    base = lax.axis_index(SLOT) * frames
    slots = base + jnp.arange(frames, dtype=jnp.int32)
    begins = video_start(slots, counts)
    before = 2 - jnp.arange(3, dtype=jnp.int32)
    valid = (slots[:, None] - before[None, :] >= begins[:, None]).astype(jnp.float32)

    with jax.named_scope("first"):
        part_ref = part.astype(jnp.int32).reshape(1)
        first = conv_one_call(valid, part_ref, prior_all, own_all, weight_one)

    with jax.named_scope("weight_two"):
        squares = jnp.sum(first * first, axis=-1)
        squares, later = lax.optimization_barrier((squares, later))
        mine = jnp.stack(later)
        swapped = lax.ppermute(mine, "core", [(0, 1), (1, 0)])
        taps = shards * shard // channels
        weight_two = assemble_call(
            assemble_two_kernel, place, mine, swapped, (taps * LANE, channels),
            [pltpu.VMEM((TILE_ROWS, channels), jnp.float32)], "assemble_two"
        )

    with jax.named_scope("second"):
        squares = squares + sum(onward(squares, d) for d in range(1, parts))
        gain_mine = lax.dynamic_index_in_dim(gain_two.reshape(share, parts), part, 1, keepdims=False)
        gain_mine = jnp.pad(gain_mine, (0, LANE - share))
        scale = lax.rsqrt(squares / channels + EPS)
        hidden_two = jax.nn.silu(first * scale[..., None] * gain_mine).astype(jnp.bfloat16)
        prior_two = earlier(hidden_two)
        sums = []
        for slot in reversed(range(frames)):
            mine, *rest = conv_two_call(slot, valid, part_ref, prior_two, hidden_two, weight_two, parts)
            arrived = [onward(r, d) for d, r in enumerate(rest, 1)]
            sums.append(sum((r.astype(jnp.float32) for r in arrived), mine.astype(jnp.float32)))
        second = jnp.stack(sums[::-1])

    block = (source + second).astype(jnp.bfloat16)
    result = jnp.broadcast_to(
        block[:, :, None, :, None, :], (frames, each, 2, width, 2, channels)
    ).reshape(frames, 2 * each, 2 * width, channels)
    return result[None]


def solution(mesh):
    sizes = mesh.devices.shape
    fine = Mesh(mesh.devices.reshape((sizes[0] // 2, 2) + sizes[1:]), ("z", "core", "tile", "group"))
    in_specs = (
        P("group", SLOT, "tile", None, None),
        P("group", None),
        P(),
        P(),
        P(SLOT + ("group",), None),
        P(SLOT + ("group",), None),
    )
    out_specs = P("group", SLOT, "tile", None, None)
    return jax.shard_map(body, mesh=fine, in_specs=in_specs, out_specs=out_specs, check_vma=False)
```

```python
import functools
import jax
import jax.numpy as jnp
from jax import lax
from jax.experimental import pallas as pl
from jax.experimental.pallas import tpu as pltpu
from jax.sharding import Mesh, PartitionSpec as P

EPS = 1e-06
SLOT = ("z", "core")
LANE = 128
TILE_ROWS = 48


def video_start(slots, counts):
    starts = jnp.cumsum(counts) - counts
    hit = starts[None, :] <= slots[:, None]
    return jnp.max(jnp.where(hit, starts[None, :], 0), axis=1)


def earlier(x):
    n = lax.axis_size(SLOT)
    return lax.ppermute(x, SLOT, [(i, i + 1) for i in range(n - 1)])


def onward(x, by, axis="tile"):
    n = lax.axis_size(axis)
    return lax.ppermute(x, axis, [(i, (i + by) % n) for i in range(n)])


def from_all(x, axis):
    return jnp.stack([x] + [onward(x, d, axis) for d in range(1, lax.axis_size(axis))])


def fill_shifted(taps, slot, row, frame_row):
    width, channels = frame_row.shape
    wide = frame_row.astype(jnp.float32)
    col = lax.broadcasted_iota(jnp.int32, (width, channels), 0)
    left = jnp.where(col == 0, 0.0, pltpu.roll(wide, 1, 0))
    right = jnp.where(col == width - 1, 0.0, pltpu.roll(wide, width - 1, 0))
    taps[0, slot, row] = left.astype(frame_row.dtype)
    taps[1, slot, row] = frame_row
    taps[2, slot, row] = right.astype(frame_row.dtype)


def clear_border(taps):
    _, slots, rows, width, channels = taps.shape
    blank = jnp.zeros((width, channels), taps.dtype)
    for e in range(3):
        for slot in range(slots):
            taps[e, slot, 0] = blank
            taps[e, slot, rows - 1] = blank


def conv_one_kernel(share, valid, halo, own, weight, out, frame_buf, acc):
    parts, frames, each, width, channels = own.shape
    rows = parts * each
    blank = jnp.zeros((width, channels), own.dtype)
    for slot in range(2 * frames):
        frame_buf[slot, 0] = blank
        frame_buf[slot, rows + 1] = blank
        source = halo if slot < frames else own
        for row in range(rows):
            frame_buf[slot, row + 1] = source[row // each, slot % frames, row % each]
    for slot in range(2 * frames):
        pairs = [(s, slot - s) for s in range(frames) if 0 <= slot - s < 3]
        columns = jnp.concatenate(
            [frame_buf[slot, b : b + rows].reshape(rows * width, channels) for b in range(3)], axis=1
        )
        for e in range(3):
            blocks = []
            for _, a in pairs:
                taps = [(a * 3 + b) * 3 + e for b in range(3)]
                blocks.append(jnp.concatenate([weight[t * channels : (t + 1) * channels, :] for t in taps], axis=0))
            packed = blocks[0] if len(blocks) == 1 else jnp.concatenate(blocks, axis=1)
            term = jnp.dot(columns, packed, preferred_element_type=jnp.float32)
            for i, (s, a) in enumerate(pairs):
                piece = valid[s, a] * term[:, i * LANE : (i + 1) * LANE]
                if a == 0:
                    acc[s, e] = piece
                else:
                    acc[s, e] = acc[s, e] + piece
    pixels = rows * width
    lane = lax.broadcasted_iota(jnp.int32, (pixels, LANE), 1)
    col = lax.rem(lax.broadcasted_iota(jnp.int32, (pixels, LANE), 0), width)
    for s in range(frames):
        left = jnp.where(col == 0, 0.0, pltpu.roll(acc[s, 0], 1, 0))
        right = jnp.where(col == width - 1, 0.0, pltpu.roll(acc[s, 2], pixels - 1, 0))
        done = jnp.where(lane < share, acc[s, 1] + left + right, 0.0)
        out[s] = done.reshape(rows, width, LANE)


def conv_two_kernel(s, valid, part, halo, own, weight, *rest):
    *outs, taps, acc = rest
    frames, rows, width, lanes = own.shape
    parts = len(outs)
    each = rows // parts
    channels = weight.shape[1]
    clear_border(taps)
    for a in range(3):
        source = halo if s + a < frames else own
        for row in range(rows):
            fill_shifted(taps, a, row + 1, source[(s + a) % frames, row])
    for a in range(3):
        columns = jnp.concatenate(
            [
                taps[e, a, b : b + rows].reshape(rows * width, lanes)
                for b in range(3)
                for e in range(3)
            ],
            axis=1,
        )
        block = weight[a * 9 * lanes : (a + 1) * 9 * lanes, :]
        term = valid[s, a] * jnp.dot(columns, block, preferred_element_type=jnp.float32)
        if a == 0:
            acc[...] = term
        else:
            acc[...] = acc[...] + term
    for d in range(parts):
        top = pl.multiple_of(lax.rem(part[0] + d, parts) * (each * width), 64)
        outs[d][...] = acc[pl.ds(top, each * width), :].astype(outs[d].dtype).reshape(each, width, channels)


VMEM = pl.BlockSpec(memory_space=pltpu.VMEM)
SMEM = pl.BlockSpec(memory_space=pltpu.SMEM)
PARAMS = pltpu.CompilerParams(vmem_limit_bytes=52 * 1024 * 1024)


def conv_one_call(valid, halo, own, weight):
    parts, frames, each, width, channels = own.shape
    rows = parts * each
    flops = 2 * 6 * rows * width * 9 * channels * LANE
    return pl.pallas_call(
        functools.partial(conv_one_kernel, channels // parts),
        out_shape=jax.ShapeDtypeStruct((frames, rows, width, LANE), jnp.float32),
        in_specs=[SMEM, VMEM, VMEM, VMEM],
        out_specs=VMEM,
        scratch_shapes=[
            pltpu.VMEM((2 * frames, rows + 2, width, channels), jnp.bfloat16),
            pltpu.VMEM((frames, 3, rows * width, LANE), jnp.float32),
        ],
        compiler_params=PARAMS,
        cost_estimate=pl.CostEstimate(flops=flops, bytes_accessed=6_000_000, transcendentals=0),
        name="conv_one",
    )(valid, halo, own, weight)


def conv_two_call(slot, valid, part, halo, own, weight, parts):
    frames, rows, width, lanes = own.shape
    channels = weight.shape[1]
    flops = 2 * 3 * rows * width * 9 * lanes * channels
    return pl.pallas_call(
        functools.partial(conv_two_kernel, slot),
        out_shape=[jax.ShapeDtypeStruct((rows // parts, width, channels), jnp.bfloat16)] * parts,
        in_specs=[SMEM, SMEM, VMEM, VMEM, VMEM],
        out_specs=[VMEM] * parts,
        scratch_shapes=[
            pltpu.VMEM((3, 3, rows + 2, width, lanes), jnp.bfloat16),
            pltpu.VMEM((rows * width, channels), jnp.float32),
        ],
        compiler_params=PARAMS,
        cost_estimate=pl.CostEstimate(flops=flops, bytes_accessed=6_000_000, transcendentals=0),
        name="conv_two",
    )(valid, part, halo, own, weight)


def gathered(place, mine, other, i):
    ys, zs = mine.shape[:2]
    z, c, y = i // (2 * ys), i // ys % 2, i % ys
    at = lax.rem(place[2] + ys - y, ys), lax.rem(place[1] + zs - z, zs)
    return jnp.where(place[0] == c, mine[at].astype(jnp.float32), other[at].astype(jnp.float32))


def assemble_one_kernel(place, mine, other, out, wide):
    ys, zs, _, lanes = mine.shape
    shard = out.shape[0] // (2 * ys * zs)
    share = lanes // 4
    piece_rows = shard // 4 + 1
    for pieces, core in ((mine, place[0]), (other, 1 - place[0])):
        for z in range(zs):
            top = pl.multiple_of((2 * z + core) * (ys * shard), 8)
            view = wide.at[pl.ds(top, ys * shard), :]
            for y in range(ys):
                piece = pieces[lax.rem(place[2] + ys - y, ys), lax.rem(place[1] + zs - z, zs)].astype(jnp.float32)
                for j in range(4):
                    rows = min(piece_rows, shard - j * piece_rows)
                    low = (j * share) // LANE * LANE
                    window = piece[:, low : min(low + 2 * LANE, lanes)]
                    shift = j * share - low
                    if shift:
                        window = pltpu.roll(window, window.shape[1] - shift, 1)
                    first = shard * y + j * piece_rows
                    view[first : first + rows, :] = window[:rows, :LANE]
    out[...] = wide[...].astype(out.dtype)


def assemble_two_kernel(place, mine, other, out, wide, piece_buf):
    shards = 2 * mine.shape[0] * mine.shape[1]
    channels = mine.shape[3]
    taps = out.shape[0] // LANE
    width = channels // 4
    share = 2 * taps * width // shards
    piece_rows = (share + 1) // 2
    for t in range(taps):
        wide[t * LANE + width : (t + 1) * LANE, :] = jnp.zeros((LANE - width, channels), jnp.float32)
    for i in range(shards):
        first = share * (i // 2) + (piece_rows - 1) * (i % 2)
        piece = gathered(place, mine, other, i)[:piece_rows]
        split = min(piece_rows, (first // width + 1) * width - first)
        at = first // width * LANE + first % width
        if split == piece_rows:
            wide[at : at + piece_rows, :] = piece
        else:
            piece_buf[0:piece_rows, :] = piece
            wide[at : at + split, :] = piece_buf[0:split, :]
            at = (first // width + 1) * LANE
            wide[at : at + piece_rows - split, :] = piece_buf[split:piece_rows, :]
    out[...] = wide[...].astype(out.dtype)


def assemble_call(kernel, place, mine, other, shape, extra, name):
    return pl.pallas_call(
        kernel,
        out_shape=jax.ShapeDtypeStruct(shape, jnp.bfloat16),
        in_specs=[SMEM, VMEM, VMEM],
        out_specs=VMEM,
        scratch_shapes=[pltpu.VMEM(shape, jnp.float32)] + extra,
        compiler_params=PARAMS,
        cost_estimate=pl.CostEstimate(flops=4_000_000, bytes_accessed=5_000_000, transcendentals=0),
        name=name,
    )(place, mine, other)


def pick(rows, columns, transposed, part, step):
    big = lax.broadcasted_iota(jnp.int32, (rows, columns), 1 if transposed else 0)
    small = lax.broadcasted_iota(jnp.int32, (rows, columns), 0 if transposed else 1)
    return (big == step * small + part).astype(jnp.bfloat16)


def body(latents, frame_counts, gain_one, gain_two, conv_one, conv_two):
    part = lax.axis_index("tile")
    parts = lax.axis_size("tile")
    side = lax.axis_index("group") % 2
    core = lax.axis_index("core")
    counts = frame_counts.reshape(-1)
    source = latents[0].astype(jnp.float32)
    frames, each, width, channels = source.shape
    share = channels // parts
    shard = conv_one.shape[0]
    piece_rows = shard // 4 + 1
    shards = lax.axis_size(SLOT) * lax.axis_size("group")
    place = jnp.stack([core, lax.axis_index("z"), lax.axis_index("group")]).astype(jnp.int32)

    with jax.named_scope("pixels"):
        mean_sq = jnp.mean(source * source, axis=-1, keepdims=True)
        hidden_one = jax.nn.silu(source * lax.rsqrt(mean_sq + EPS) * gain_one).astype(jnp.bfloat16)
        own_all = lax.all_to_all(jnp.broadcast_to(hidden_one, (parts,) + hidden_one.shape), "tile", 0, 0)

    with jax.named_scope("pieces"):
        conv_one, conv_two, hidden_one = lax.optimization_barrier((conv_one, conv_two, hidden_one))
        pairs = [(i, i ^ 1) for i in range(lax.axis_size("group"))]
        other = lax.ppermute(conv_two, "group", pairs)
        take = pick(channels, share, False, part, parts)
        piece = jnp.dot(conv_one, take, preferred_element_type=jnp.float32).astype(jnp.bfloat16)
        piece = jnp.pad(piece, ((0, 4 * piece_rows - shard), (0, 0)))
        piece = jnp.concatenate([piece[j * piece_rows : (j + 1) * piece_rows] for j in range(4)], axis=1)
        piece = jnp.pad(piece, ((0, TILE_ROWS - piece_rows), (0, 0)))
        couple = jnp.concatenate(
            [jnp.where(side == 0, conv_two, other), jnp.where(side == 0, other, conv_two)], axis=0
        )
        rows_take = pick(TILE_ROWS, 2 * shard, True, part + parts * (piece_rows - 1) * side, parts)
        piece_two = jnp.dot(rows_take, couple, preferred_element_type=jnp.float32).astype(jnp.bfloat16)
        pieces = jnp.concatenate([piece, piece_two], axis=0)
        column = from_all(pieces, "z")

    column, own_all = lax.optimization_barrier((column, own_all))
    with jax.named_scope("weight_one"):
        mine = from_all(column[:, :TILE_ROWS], "group")
        prior_all = earlier(own_all)
        mine, prior_all = lax.optimization_barrier((mine, prior_all))
        swapped = lax.ppermute(mine, "core", [(0, 1), (1, 0)])
        weight_one = assemble_call(
            assemble_one_kernel, place, mine, swapped, (shards * shard, LANE), [], "assemble_one"
        )

    with jax.named_scope("weight_two"):
        column, _ = lax.optimization_barrier((column, mine))
        later = column[:, TILE_ROWS:]
        later = [later] + [onward(later, d, "group") for d in range(1, lax.axis_size("group"))]

    base = lax.axis_index(SLOT) * frames
    slots = base + jnp.arange(frames, dtype=jnp.int32)
    begins = video_start(slots, counts)
    before = 2 - jnp.arange(3, dtype=jnp.int32)
    valid = (slots[:, None] - before[None, :] >= begins[:, None]).astype(jnp.float32)

    with jax.named_scope("first"):
        part_ref = part.astype(jnp.int32).reshape(1)
        first = conv_one_call(valid, prior_all, own_all, weight_one)

    with jax.named_scope("weight_two"):
        squares = jnp.sum(first * first, axis=-1)
        squares, later = lax.optimization_barrier((squares, later))
        mine = jnp.stack(later)
        swapped = lax.ppermute(mine, "core", [(0, 1), (1, 0)])
        taps = shards * shard // channels
        weight_two = assemble_call(
            assemble_two_kernel, place, mine, swapped, (taps * LANE, channels),
            [pltpu.VMEM((TILE_ROWS, channels), jnp.float32)], "assemble_two"
        )

    with jax.named_scope("second"):
        squares = squares + sum(onward(squares, d) for d in range(1, parts))
        gain_mine = lax.dynamic_index_in_dim(gain_two.reshape(share, parts), part, 1, keepdims=False)
        gain_mine = jnp.pad(gain_mine, (0, LANE - share))
        scale = lax.rsqrt(squares / channels + EPS)
        hidden_two = jax.nn.silu(first * scale[..., None] * gain_mine).astype(jnp.bfloat16)
        prior_two = earlier(hidden_two)
        sums = []
        for slot in reversed(range(frames)):
            mine, *rest = conv_two_call(slot, valid, part_ref, prior_two, hidden_two, weight_two, parts)
            arrived = [onward(r, d) for d, r in enumerate(rest, 1)]
            sums.append(sum((r.astype(jnp.float32) for r in arrived), mine.astype(jnp.float32)))
        second = jnp.stack(sums[::-1])

    block = (source + second).astype(jnp.bfloat16)
    result = jnp.broadcast_to(
        block[:, :, None, :, None, :], (frames, each, 2, width, 2, channels)
    ).reshape(frames, 2 * each, 2 * width, channels)
    return result[None]


def solution(mesh):
    sizes = mesh.devices.shape
    fine = Mesh(mesh.devices.reshape((sizes[0] // 2, 2) + sizes[1:]), ("z", "core", "tile", "group"))
    in_specs = (
        P("group", SLOT, "tile", None, None),
        P("group", None),
        P(),
        P(),
        P(SLOT + ("group",), None),
        P(SLOT + ("group",), None),
    )
    out_specs = P("group", SLOT, "tile", None, None)
    return jax.shard_map(body, mesh=fine, in_specs=in_specs, out_specs=out_specs, check_vma=False)
```

```python
import functools
import jax
import jax.numpy as jnp
from jax import lax
from jax.experimental import pallas as pl
from jax.experimental.pallas import tpu as pltpu
from jax.sharding import Mesh, PartitionSpec as P

EPS = 1e-06
SLOT = ("z", "core")
LANE = 128
TILE_ROWS = 48


def video_start(slots, counts):
    starts = jnp.cumsum(counts) - counts
    hit = starts[None, :] <= slots[:, None]
    return jnp.max(jnp.where(hit, starts[None, :], 0), axis=1)


def earlier(x):
    n = lax.axis_size(SLOT)
    return lax.ppermute(x, SLOT, [(i, i + 1) for i in range(n - 1)])


def onward(x, by, axis="tile"):
    n = lax.axis_size(axis)
    return lax.ppermute(x, axis, [(i, (i + by) % n) for i in range(n)])


def across(x, bit):
    return lax.ppermute(x, "tile", [(i, i ^ bit) for i in range(lax.axis_size("tile"))])


def from_all(x, axis):
    return jnp.stack([x] + [onward(x, d, axis) for d in range(1, lax.axis_size(axis))])


def fill_shifted(taps, slot, row, frame_row):
    width, channels = frame_row.shape
    wide = frame_row.astype(jnp.float32)
    col = lax.broadcasted_iota(jnp.int32, (width, channels), 0)
    left = jnp.where(col == 0, 0.0, pltpu.roll(wide, 1, 0))
    right = jnp.where(col == width - 1, 0.0, pltpu.roll(wide, width - 1, 0))
    taps[0, slot, row] = left.astype(frame_row.dtype)
    taps[1, slot, row] = frame_row
    taps[2, slot, row] = right.astype(frame_row.dtype)


def clear_border(taps):
    _, slots, rows, width, channels = taps.shape
    blank = jnp.zeros((width, channels), taps.dtype)
    for e in range(3):
        for slot in range(slots):
            taps[e, slot, 0] = blank
            taps[e, slot, rows - 1] = blank


def assemble_one(place, mine, other, out, wide):
    ys, zs, _, lanes = mine.shape
    shard = out.shape[0] // (2 * ys * zs)
    share = lanes // 4
    piece_rows = shard // 4 + 1
    for pieces, core in ((mine, place[0]), (other, 1 - place[0])):
        for z in range(zs):
            top = pl.multiple_of((2 * z + core) * (ys * shard), 8)
            view = wide.at[pl.ds(top, ys * shard), :]
            for y in range(ys):
                piece = pieces[lax.rem(place[1] + ys - y, ys), z].astype(jnp.float32)
                for j in range(4):
                    rows = min(piece_rows, shard - j * piece_rows)
                    low = (j * share) // LANE * LANE
                    window = piece[:, low : min(low + 2 * LANE, lanes)]
                    shift = j * share - low
                    if shift:
                        window = pltpu.roll(window, window.shape[1] - shift, 1)
                    first = shard * y + j * piece_rows
                    view[first : first + rows, :] = window[:rows, :LANE]
    out[...] = wide[...].astype(out.dtype)


def conv_one_kernel(share, valid, place, halo, own, mine, other, out, frame_buf, acc, weight, wide):
    parts, frames, each, width, channels = own.shape
    rows = parts * each
    blank = jnp.zeros((width, channels), own.dtype)
    for slot in range(2 * frames):
        frame_buf[slot, 0] = blank
        frame_buf[slot, rows + 1] = blank
        source = halo if slot < frames else own
        for back in range(parts):
            top = lax.rem(place[2] + parts - back, parts) * each + 1
            for j in range(each):
                frame_buf[slot, top + j] = source[back, slot % frames, j]
    assemble_one(place, mine, other, weight, wide)
    for slot in range(2 * frames):
        pairs = [(s, slot - s) for s in range(frames) if 0 <= slot - s < 3]
        columns = jnp.concatenate(
            [frame_buf[slot, b : b + rows].reshape(rows * width, channels) for b in range(3)], axis=1
        )
        for e in range(3):
            blocks = []
            for _, a in pairs:
                taps = [(a * 3 + b) * 3 + e for b in range(3)]
                blocks.append(jnp.concatenate([weight[t * channels : (t + 1) * channels, :] for t in taps], axis=0))
            packed = blocks[0] if len(blocks) == 1 else jnp.concatenate(blocks, axis=1)
            term = jnp.dot(columns, packed, preferred_element_type=jnp.float32)
            for i, (s, a) in enumerate(pairs):
                piece = valid[s, a] * term[:, i * LANE : (i + 1) * LANE]
                if a == 0:
                    acc[s, e] = piece
                else:
                    acc[s, e] = acc[s, e] + piece
    pixels = rows * width
    lane = lax.broadcasted_iota(jnp.int32, (pixels, LANE), 1)
    col = lax.rem(lax.broadcasted_iota(jnp.int32, (pixels, LANE), 0), width)
    for s in range(frames):
        left = jnp.where(col == 0, 0.0, pltpu.roll(acc[s, 0], 1, 0))
        right = jnp.where(col == width - 1, 0.0, pltpu.roll(acc[s, 2], pixels - 1, 0))
        done = jnp.where(lane < share, acc[s, 1] + left + right, 0.0)
        out[s] = done.reshape(rows, width, LANE)


def conv_two_kernel(valid, place, halo, own, weight, *rest):
    *outs, taps, acc = rest
    frames, rows, width, lanes = own.shape
    parts = len(outs)
    each = rows // parts
    channels = weight.shape[1]
    clear_border(taps)
    for slot in range(2 * frames):
        source = halo if slot < frames else own
        for row in range(rows):
            fill_shifted(taps, slot, row + 1, source[slot % frames, row])
    for slot in range(2 * frames):
        pairs = [(s, slot - s) for s in range(frames) if 0 <= slot - s < 3]
        columns = jnp.concatenate(
            [
                taps[e, slot, b : b + rows].reshape(rows * width, lanes)
                for b in range(3)
                for e in range(3)
            ],
            axis=1,
        )
        blocks = [weight[a * 9 * lanes : (a + 1) * 9 * lanes, :] for _, a in pairs]
        packed = blocks[0] if len(blocks) == 1 else jnp.concatenate(blocks, axis=1)
        term = jnp.dot(columns, packed, preferred_element_type=jnp.float32)
        for i, (s, a) in enumerate(pairs):
            piece = valid[s, a] * term[:, i * channels : (i + 1) * channels]
            if a == 0:
                acc[s] = piece
            else:
                acc[s] = acc[s] + piece
    for d in range(parts):
        top = pl.multiple_of(lax.rem(place[2] + d, parts) * (each * width), 64)
        for s in range(frames):
            done = acc[s, pl.ds(top, each * width), :].astype(outs[d].dtype)
            outs[d][s] = done.reshape(each, width, channels)


VMEM = pl.BlockSpec(memory_space=pltpu.VMEM)
SMEM = pl.BlockSpec(memory_space=pltpu.SMEM)
PARAMS = pltpu.CompilerParams(vmem_limit_bytes=52 * 1024 * 1024)


def conv_one_call(valid, place, halo, own, mine, other):
    parts, frames, each, width, channels = own.shape
    rows = parts * each
    flops = 2 * 6 * rows * width * 9 * channels * LANE
    return pl.pallas_call(
        functools.partial(conv_one_kernel, channels // parts),
        out_shape=jax.ShapeDtypeStruct((frames, rows, width, LANE), jnp.float32),
        in_specs=[SMEM, SMEM, VMEM, VMEM, VMEM, VMEM],
        out_specs=VMEM,
        scratch_shapes=[
            pltpu.VMEM((2 * frames, rows + 2, width, channels), jnp.bfloat16),
            pltpu.VMEM((frames, 3, rows * width, LANE), jnp.float32),
            pltpu.VMEM((27 * channels, LANE), jnp.bfloat16),
            pltpu.VMEM((27 * channels, LANE), jnp.float32),
        ],
        compiler_params=PARAMS,
        cost_estimate=pl.CostEstimate(flops=flops, bytes_accessed=6_000_000, transcendentals=0),
        name="conv_one",
    )(valid, place, halo, own, mine, other)


def conv_two_call(valid, place, halo, own, weight, parts):
    frames, rows, width, lanes = own.shape
    channels = weight.shape[1]
    flops = 2 * 6 * rows * width * 9 * lanes * channels
    return pl.pallas_call(
        conv_two_kernel,
        out_shape=[jax.ShapeDtypeStruct((frames, rows // parts, width, channels), jnp.bfloat16)] * parts,
        in_specs=[SMEM, SMEM, VMEM, VMEM, VMEM],
        out_specs=[VMEM] * parts,
        scratch_shapes=[
            pltpu.VMEM((3, 2 * frames, rows + 2, width, lanes), jnp.bfloat16),
            pltpu.VMEM((frames, rows * width, channels), jnp.float32),
        ],
        compiler_params=PARAMS,
        cost_estimate=pl.CostEstimate(flops=flops, bytes_accessed=6_000_000, transcendentals=0),
        name="conv_two",
    )(valid, place, halo, own, weight)


def gathered(place, mine, other, i):
    ys, zs = mine.shape[:2]
    z, c, y = i // (2 * ys), i // ys % 2, i % ys
    at = lax.rem(place[1] + ys - y, ys), z
    return jnp.where(place[0] == c, mine[at].astype(jnp.float32), other[at].astype(jnp.float32))


def assemble_two_kernel(place, mine, other, out, wide, piece_buf):
    shards = 2 * mine.shape[0] * mine.shape[1]
    channels = mine.shape[3]
    taps = out.shape[0] // LANE
    width = channels // 4
    share = 2 * taps * width // shards
    piece_rows = (share + 1) // 2
    for t in range(taps):
        wide[t * LANE + width : (t + 1) * LANE, :] = jnp.zeros((LANE - width, channels), jnp.float32)
    for m in range(shards // 2):
        even, odd = gathered(place, mine, other, 2 * m), gathered(place, mine, other, 2 * m + 1)
        half = piece_rows - 1
        piece_buf[0:TILE_ROWS, :] = even
        piece_buf[TILE_ROWS : 2 * TILE_ROWS, :] = odd
        piece_buf[half : half + 1, :] = even[half : half + 1] + odd[0:1]
        done = 0
        while done < share:
            first = share * m + done
            source = done if done <= half else done - half + TILE_ROWS
            count = min((first // width + 1) * width - first, (piece_rows if done <= half else share) - done)
            at = first // width * LANE + first % width
            wide[at : at + count, :] = piece_buf[source : source + count, :]
            done += count
    out[...] = wide[...].astype(out.dtype)


def assemble_call(kernel, place, mine, other, shape, extra, name):
    return pl.pallas_call(
        kernel,
        out_shape=jax.ShapeDtypeStruct(shape, jnp.bfloat16),
        in_specs=[SMEM, VMEM, VMEM],
        out_specs=VMEM,
        scratch_shapes=[pltpu.VMEM(shape, jnp.float32)] + extra,
        compiler_params=PARAMS,
        cost_estimate=pl.CostEstimate(flops=4_000_000, bytes_accessed=5_000_000, transcendentals=0),
        name=name,
    )(place, mine, other)


def pick(rows, columns, transposed, part, step):
    big = lax.broadcasted_iota(jnp.int32, (rows, columns), 1 if transposed else 0)
    small = lax.broadcasted_iota(jnp.int32, (rows, columns), 0 if transposed else 1)
    return (big == step * small + part).astype(jnp.bfloat16)


def body(latents, frame_counts, gain_one, gain_two, conv_one, conv_two):
    part = lax.axis_index("tile")
    parts = lax.axis_size("tile")
    side = lax.axis_index("group") % 2
    core = lax.axis_index("core")
    counts = frame_counts.reshape(-1)
    source = latents[0].astype(jnp.float32)
    frames, each, width, channels = source.shape
    share = channels // parts
    shard = conv_one.shape[0]
    piece_rows = shard // 4 + 1
    shards = lax.axis_size(SLOT) * lax.axis_size("group")
    place = jnp.stack([core, lax.axis_index("group"), part]).astype(jnp.int32)

    with jax.named_scope("pixels"):
        mean_sq = jnp.mean(source * source, axis=-1, keepdims=True)
        hidden_one = jax.nn.silu(source * lax.rsqrt(mean_sq + EPS) * gain_one).astype(jnp.bfloat16)
        own_all = from_all(hidden_one, "tile")

    with jax.named_scope("pieces"):
        take = pick(channels, share, False, part, parts)
        piece = jnp.dot(conv_one, take, preferred_element_type=jnp.float32).astype(jnp.bfloat16)
        piece = jnp.pad(piece, ((0, 4 * piece_rows - shard), (0, 0)))
        piece = jnp.concatenate([piece[j * piece_rows : (j + 1) * piece_rows] for j in range(4)], axis=1)
        piece = jnp.pad(piece, ((0, TILE_ROWS - piece_rows), (0, 0)))
        rows_take = pick(TILE_ROWS, shard, True, part - 2 * side, parts)
        piece_two = jnp.dot(rows_take, conv_two, preferred_element_type=jnp.float32).astype(jnp.bfloat16)
        pieces = jnp.concatenate([piece, piece_two], axis=0)
        column = lax.all_to_all(jnp.broadcast_to(pieces, (lax.axis_size("z"),) + pieces.shape), "z", 0, 0)

    column, own_all = lax.optimization_barrier((column, own_all))
    with jax.named_scope("weight_one"):
        mine = from_all(column[:, :TILE_ROWS], "group")
        prior_all = earlier(own_all)
        mine, prior_all = lax.optimization_barrier((mine, prior_all))
        swapped = lax.ppermute(mine, "core", [(0, 1), (1, 0)])
        one_mine, one_swapped = mine, swapped

    with jax.named_scope("weight_two"):
        column, _ = lax.optimization_barrier((column, mine))
        later = column[:, TILE_ROWS:]
        later = [later] + [onward(later, d, "group") for d in range(1, lax.axis_size("group"))]

    base = lax.axis_index(SLOT) * frames
    slots = base + jnp.arange(frames, dtype=jnp.int32)
    begins = video_start(slots, counts)
    before = 2 - jnp.arange(3, dtype=jnp.int32)
    valid = (slots[:, None] - before[None, :] >= begins[:, None]).astype(jnp.float32)

    with jax.named_scope("first"):
        first = conv_one_call(valid, place, prior_all, own_all, one_mine, one_swapped)

    with jax.named_scope("weight_two"):
        squares = jnp.sum(first * first, axis=-1)
        squares = squares + across(squares, 1)
        squares, later = lax.optimization_barrier((squares, later))
        mine = jnp.stack(later)
        swapped = lax.ppermute(mine, "core", [(0, 1), (1, 0)])
        taps = shards * shard // channels
        weight_two = assemble_call(
            assemble_two_kernel, place, mine, swapped, (taps * LANE, channels),
            [pltpu.VMEM((2 * TILE_ROWS, channels), jnp.float32)], "assemble_two"
        )

    with jax.named_scope("second"):
        squares = squares + across(squares, 2)
        gain_mine = lax.dynamic_index_in_dim(gain_two.reshape(share, parts), part, 1, keepdims=False)
        gain_mine = jnp.pad(gain_mine, (0, LANE - share))
        scale = lax.rsqrt(squares / channels + EPS)
        hidden_two = jax.nn.silu(first * scale[..., None] * gain_mine).astype(jnp.bfloat16)
        prior_two = earlier(hidden_two)
        sums, *rest = conv_two_call(valid, place, prior_two, hidden_two, weight_two, parts)
        arrived = [onward(r, d) for d, r in enumerate(rest, 1)]
        second = sum((r.astype(jnp.float32) for r in arrived), sums.astype(jnp.float32))

    block = (source + second).astype(jnp.bfloat16)
    result = jnp.broadcast_to(
        block[:, :, None, :, None, :], (frames, each, 2, width, 2, channels)
    ).reshape(frames, 2 * each, 2 * width, channels)
    return result[None]


def solution(mesh):
    sizes = mesh.devices.shape
    fine = Mesh(mesh.devices.reshape((sizes[0] // 2, 2) + sizes[1:]), ("z", "core", "tile", "group"))
    in_specs = (
        P("group", SLOT, "tile", None, None),
        P("group", None),
        P(),
        P(),
        P(SLOT + ("group",), None),
        P(SLOT + ("group",), None),
    )
    out_specs = P("group", SLOT, "tile", None, None)
    return jax.shard_map(body, mesh=fine, in_specs=in_specs, out_specs=out_specs, check_vma=False)
```

```python
import functools
import jax
import jax.numpy as jnp
from jax import lax
from jax.experimental import pallas as pl
from jax.experimental.pallas import tpu as pltpu
from jax.sharding import Mesh, PartitionSpec as P

EPS = 1e-06
SLOT = ("z", "core")
LANE = 128
TILE_ROWS = 48


def video_start(slots, counts):
    starts = jnp.cumsum(counts) - counts
    hit = starts[None, :] <= slots[:, None]
    return jnp.max(jnp.where(hit, starts[None, :], 0), axis=1)


def earlier(x):
    n = lax.axis_size(SLOT)
    return lax.ppermute(x, SLOT, [(i, i + 1) for i in range(n - 1)])


def onward(x, by, axis="tile"):
    n = lax.axis_size(axis)
    return lax.ppermute(x, axis, [(i, (i + by) % n) for i in range(n)])


def across(x, bit):
    return lax.ppermute(x, "tile", [(i, i ^ bit) for i in range(lax.axis_size("tile"))])


def ring(x, axis):
    low, high = onward(x, 1, axis), onward(x, -1, axis)
    half = x.shape[0] // 2
    return [x, low, high, onward(low[:half], 1, axis), onward(high[half:], -1, axis)]


def from_all(x, axis):
    return jnp.stack([x] + [onward(x, d, axis) for d in range(1, lax.axis_size(axis))])


def fill_shifted(taps, slot, row, frame_row):
    width, channels = frame_row.shape
    wide = frame_row.astype(jnp.float32)
    col = lax.broadcasted_iota(jnp.int32, (width, channels), 0)
    left = jnp.where(col == 0, 0.0, pltpu.roll(wide, 1, 0))
    right = jnp.where(col == width - 1, 0.0, pltpu.roll(wide, width - 1, 0))
    taps[0, slot, row] = left.astype(frame_row.dtype)
    taps[1, slot, row] = frame_row
    taps[2, slot, row] = right.astype(frame_row.dtype)


def clear_border(taps):
    _, slots, rows, width, channels = taps.shape
    blank = jnp.zeros((width, channels), taps.dtype)
    for e in range(3):
        for slot in range(slots):
            taps[e, slot, 0] = blank
            taps[e, slot, rows - 1] = blank


def assemble_one(pieces, out, wide):
    cores, ys, zs, _, lanes = pieces.shape
    shard = out.shape[0] // (cores * ys * zs)
    share = lanes // 4
    piece_rows = shard // 4 + 1
    for z in range(zs):
        for c in range(cores):
            for y in range(ys):
                piece = pieces[c, y, z].astype(jnp.float32)
                for j in range(4):
                    rows = min(piece_rows, shard - j * piece_rows)
                    low = (j * share) // LANE * LANE
                    window = piece[:, low : min(low + 2 * LANE, lanes)]
                    shift = j * share - low
                    if shift:
                        window = pltpu.roll(window, window.shape[1] - shift, 1)
                    first = shard * (z * cores * ys + c * ys + y) + j * piece_rows
                    wide[first : first + rows, :] = window[:rows, :LANE]
    out[...] = wide[...].astype(out.dtype)


def conv_one_kernel(share, valid, place, *refs):
    own_refs, halo_refs, mine_refs, other_refs = refs[:5], refs[5:8], refs[8:13], refs[13:15]
    out, frame_buf, acc, weight, wide, pieces = refs[15:]
    frames, each, width, channels = own_refs[0].shape
    rows = out.shape[1]
    parts = rows // each
    cores, ys, zs = pieces.shape[:3]
    blank = jnp.zeros((width, channels), frame_buf.dtype)
    for slot in range(2 * frames):
        frame_buf[slot, 0] = blank
        frame_buf[slot, rows + 1] = blank

    def put(slot, back, block):
        top = lax.rem(place[2] + parts - back, parts) * each + 1
        for j in range(each):
            frame_buf[slot, top + j] = block[j]

    for s in range(frames):
        for back, ref in zip((0, 1, 3), own_refs):
            put(frames + s, back, ref[s])
        put(frames + s, 2, own_refs[3 + s][0])
        put(s, 0, halo_refs[0][s])
        put(s, 1, halo_refs[1][0, s])
        put(s, 3, halo_refs[1][1, s])
        put(s, 2, halo_refs[2][s])
    half = zs // 2
    for c, third in ((place[0], lambda i: mine_refs[i]), (1 - place[0], lambda i: other_refs[0].at[i])):
        for i, back in enumerate((0, 1, 3)):
            source = third(i)
            y = lax.rem(place[1] + ys - back, ys)
            for z in range(zs):
                pieces[c, y, z] = source[z]
    y = lax.rem(place[1] + ys - 2, ys)
    for z in range(zs):
        pieces[place[0], y, z] = mine_refs[3 + z // half][z % half]
        pieces[1 - place[0], y, z] = other_refs[1][z]
    assemble_one(pieces, weight, wide)
    for slot in range(2 * frames):
        pairs = [(s, slot - s) for s in range(frames) if 0 <= slot - s < 3]
        columns = jnp.concatenate(
            [frame_buf[slot, b : b + rows].reshape(rows * width, channels) for b in range(3)], axis=1
        )
        for e in range(3):
            blocks = []
            for _, a in pairs:
                taps = [(a * 3 + b) * 3 + e for b in range(3)]
                blocks.append(jnp.concatenate([weight[t * channels : (t + 1) * channels, :] for t in taps], axis=0))
            packed = blocks[0] if len(blocks) == 1 else jnp.concatenate(blocks, axis=1)
            term = jnp.dot(columns, packed, preferred_element_type=jnp.float32)
            for i, (s, a) in enumerate(pairs):
                piece = valid[s, a] * term[:, i * LANE : (i + 1) * LANE]
                if a == 0:
                    acc[s, e] = piece
                else:
                    acc[s, e] = acc[s, e] + piece
    pixels = rows * width
    lane = lax.broadcasted_iota(jnp.int32, (pixels, LANE), 1)
    col = lax.rem(lax.broadcasted_iota(jnp.int32, (pixels, LANE), 0), width)
    for s in range(frames):
        left = jnp.where(col == 0, 0.0, pltpu.roll(acc[s, 0], 1, 0))
        right = jnp.where(col == width - 1, 0.0, pltpu.roll(acc[s, 2], pixels - 1, 0))
        done = jnp.where(lane < share, acc[s, 1] + left + right, 0.0)
        out[s] = done.reshape(rows, width, LANE)


def conv_two_kernel(valid, place, halo, own, weight, own_sum, up, down, up_last, down_last, taps, acc):
    frames, rows, width, lanes = own.shape
    each = own_sum.shape[1]
    parts = rows // each
    channels = weight.shape[1]
    clear_border(taps)
    for slot in range(2 * frames):
        source = halo if slot < frames else own
        for row in range(rows):
            fill_shifted(taps, slot, row + 1, source[slot % frames, row])
    for slot in range(2 * frames):
        pairs = [(s, slot - s) for s in range(frames) if 0 <= slot - s < 3]
        columns = jnp.concatenate(
            [
                taps[e, slot, b : b + rows].reshape(rows * width, lanes)
                for b in range(3)
                for e in range(3)
            ],
            axis=1,
        )
        blocks = [weight[a * 9 * lanes : (a + 1) * 9 * lanes, :] for _, a in pairs]
        packed = blocks[0] if len(blocks) == 1 else jnp.concatenate(blocks, axis=1)
        term = jnp.dot(columns, packed, preferred_element_type=jnp.float32)
        for i, (s, a) in enumerate(pairs):
            piece = valid[s, a] * term[:, i * channels : (i + 1) * channels]
            if a == 0:
                acc[s] = piece
            else:
                acc[s] = acc[s] + piece
    for ref, d, s, at in ((own_sum, 0, 0, 0), (own_sum, 0, 1, 1), (up, 2, 0, 0), (up, 1, 1, 1),
                          (down, 3, 0, 0), (down, 2, 1, 1), (up_last, 1, 0, 0), (down_last, 3, 1, 0)):
        top = pl.multiple_of(lax.rem(place[2] + d, parts) * (each * width), 64)
        done = acc[s, pl.ds(top, each * width), :].astype(ref.dtype)
        ref[at] = done.reshape(each, width, channels)


VMEM = pl.BlockSpec(memory_space=pltpu.VMEM)
SMEM = pl.BlockSpec(memory_space=pltpu.SMEM)
PARAMS = pltpu.CompilerParams(vmem_limit_bytes=52 * 1024 * 1024)


def conv_one_call(valid, place, own, halo, mine, other):
    frames, each, width, channels = own[0].shape
    rows = each * lax.axis_size("tile")
    zs, piece_rows, lanes = mine[0].shape
    flops = 2 * 6 * rows * width * 9 * channels * LANE
    arrays = [*own, *halo, *mine, *other]
    return pl.pallas_call(
        functools.partial(conv_one_kernel, channels * each // rows),
        out_shape=jax.ShapeDtypeStruct((frames, rows, width, LANE), jnp.float32),
        in_specs=[SMEM, SMEM] + [VMEM] * len(arrays),
        out_specs=VMEM,
        scratch_shapes=[
            pltpu.VMEM((2 * frames, rows + 2, width, channels), jnp.bfloat16),
            pltpu.VMEM((frames, 3, rows * width, LANE), jnp.float32),
            pltpu.VMEM((27 * channels, LANE), jnp.bfloat16),
            pltpu.VMEM((27 * channels, LANE), jnp.float32),
            pltpu.VMEM((2, lax.axis_size("group"), zs, piece_rows, lanes), jnp.bfloat16),
        ],
        compiler_params=PARAMS,
        cost_estimate=pl.CostEstimate(flops=flops, bytes_accessed=6_000_000, transcendentals=0),
        name="conv_one",
    )(valid, place, *arrays)


def conv_two_call(valid, place, halo, own, weight, parts):
    frames, rows, width, lanes = own.shape
    channels = weight.shape[1]
    flops = 2 * 6 * rows * width * 9 * lanes * channels
    shapes = [(n, rows // parts, width, channels) for n in (frames, frames, frames, 1, 1)]
    return pl.pallas_call(
        conv_two_kernel,
        out_shape=[jax.ShapeDtypeStruct(shape, jnp.bfloat16) for shape in shapes],
        in_specs=[SMEM, SMEM, VMEM, VMEM, VMEM],
        out_specs=[VMEM] * len(shapes),
        scratch_shapes=[
            pltpu.VMEM((3, 2 * frames, rows + 2, width, lanes), jnp.bfloat16),
            pltpu.VMEM((frames, rows * width, channels), jnp.float32),
        ],
        compiler_params=PARAMS,
        cost_estimate=pl.CostEstimate(flops=flops, bytes_accessed=6_000_000, transcendentals=0),
        name="conv_two",
    )(valid, place, halo, own, weight)


def gathered(place, mine, other, i):
    ys, zs = mine.shape[:2]
    z, c, y = i // (2 * ys), i // ys % 2, i % ys
    at = lax.rem(place[1] + ys - y, ys), z
    return jnp.where(place[0] == c, mine[at].astype(jnp.float32), other[at].astype(jnp.float32))


def assemble_two_kernel(place, mine, other, out, wide, piece_buf):
    shards = 2 * mine.shape[0] * mine.shape[1]
    channels = mine.shape[3]
    taps = out.shape[0] // LANE
    width = channels // 4
    share = 2 * taps * width // shards
    piece_rows = (share + 1) // 2
    for t in range(taps):
        wide[t * LANE + width : (t + 1) * LANE, :] = jnp.zeros((LANE - width, channels), jnp.float32)
    for m in range(shards // 2):
        even, odd = gathered(place, mine, other, 2 * m), gathered(place, mine, other, 2 * m + 1)
        half = piece_rows - 1
        piece_buf[0:TILE_ROWS, :] = even
        piece_buf[TILE_ROWS : 2 * TILE_ROWS, :] = odd
        piece_buf[half : half + 1, :] = even[half : half + 1] + odd[0:1]
        done = 0
        while done < share:
            first = share * m + done
            source = done if done <= half else done - half + TILE_ROWS
            count = min((first // width + 1) * width - first, (piece_rows if done <= half else share) - done)
            at = first // width * LANE + first % width
            wide[at : at + count, :] = piece_buf[source : source + count, :]
            done += count
    out[...] = wide[...].astype(out.dtype)


def assemble_call(kernel, place, mine, other, shape, extra, name):
    return pl.pallas_call(
        kernel,
        out_shape=jax.ShapeDtypeStruct(shape, jnp.bfloat16),
        in_specs=[SMEM, VMEM, VMEM],
        out_specs=VMEM,
        scratch_shapes=[pltpu.VMEM(shape, jnp.float32)] + extra,
        compiler_params=PARAMS,
        cost_estimate=pl.CostEstimate(flops=4_000_000, bytes_accessed=5_000_000, transcendentals=0),
        name=name,
    )(place, mine, other)


def pick(rows, columns, transposed, part, step):
    big = lax.broadcasted_iota(jnp.int32, (rows, columns), 1 if transposed else 0)
    small = lax.broadcasted_iota(jnp.int32, (rows, columns), 0 if transposed else 1)
    return (big == step * small + part).astype(jnp.bfloat16)


def body(latents, frame_counts, gain_one, gain_two, conv_one, conv_two):
    part = lax.axis_index("tile")
    parts = lax.axis_size("tile")
    side = lax.axis_index("group") % 2
    core = lax.axis_index("core")
    counts = frame_counts.reshape(-1)
    source = latents[0].astype(jnp.float32)
    frames, each, width, channels = source.shape
    share = channels // parts
    shard = conv_one.shape[0]
    piece_rows = shard // 4 + 1
    shards = lax.axis_size(SLOT) * lax.axis_size("group")
    place = jnp.stack([core, lax.axis_index("group"), part]).astype(jnp.int32)

    with jax.named_scope("pixels"):
        mean_sq = jnp.mean(source * source, axis=-1, keepdims=True)
        hidden_one = jax.nn.silu(source * lax.rsqrt(mean_sq + EPS) * gain_one).astype(jnp.bfloat16)
        own = ring(hidden_one, "tile")
        halo = [earlier(own[0]), earlier(jnp.stack(own[1:3])), earlier(jnp.concatenate(own[3:]))]

    with jax.named_scope("pieces"):
        take = pick(channels, share, False, part, parts)
        piece = jnp.dot(conv_one, take, preferred_element_type=jnp.float32).astype(jnp.bfloat16)
        piece = jnp.pad(piece, ((0, 4 * piece_rows - shard), (0, 0)))
        piece = jnp.concatenate([piece[j * piece_rows : (j + 1) * piece_rows] for j in range(4)], axis=1)
        piece = jnp.pad(piece, ((0, TILE_ROWS - piece_rows), (0, 0)))
        rows_take = pick(TILE_ROWS, shard, True, part - 2 * side, parts)
        piece_two = jnp.dot(rows_take, conv_two, preferred_element_type=jnp.float32).astype(jnp.bfloat16)
        pieces = jnp.concatenate([piece, piece_two], axis=0)
        column = lax.all_to_all(jnp.broadcast_to(pieces, (lax.axis_size("z"),) + pieces.shape), "z", 0, 0)

    def other_core(x):
        return lax.ppermute(x, "core", [(0, 1), (1, 0)])

    with jax.named_scope("weight_one"):
        mine = ring(column[:, :TILE_ROWS], "group")
        swapped = [other_core(jnp.stack(mine[:3])), other_core(jnp.concatenate(mine[3:]))]

    with jax.named_scope("weight_two"):
        column, _ = lax.optimization_barrier((column, mine))
        later = column[:, TILE_ROWS:]
        later = [later] + [onward(later, d, "group") for d in range(1, lax.axis_size("group"))]

    base = lax.axis_index(SLOT) * frames
    slots = base + jnp.arange(frames, dtype=jnp.int32)
    begins = video_start(slots, counts)
    before = 2 - jnp.arange(3, dtype=jnp.int32)
    valid = (slots[:, None] - before[None, :] >= begins[:, None]).astype(jnp.float32)

    with jax.named_scope("first"):
        first = conv_one_call(valid, place, own, halo, mine, swapped)

    with jax.named_scope("weight_two"):
        squares = jnp.sum(first * first, axis=-1)
        squares = squares + across(squares, 1)
        squares, later = lax.optimization_barrier((squares, later))
        mine = jnp.stack(later)
        swapped = other_core(mine)
        taps = shards * shard // channels
        weight_two = assemble_call(
            assemble_two_kernel, place, mine, swapped, (taps * LANE, channels),
            [pltpu.VMEM((2 * TILE_ROWS, channels), jnp.float32)], "assemble_two"
        )

    with jax.named_scope("second"):
        squares = squares + across(squares, 2)
        gain_mine = lax.dynamic_index_in_dim(gain_two.reshape(share, parts), part, 1, keepdims=False)
        gain_mine = jnp.pad(gain_mine, (0, LANE - share))
        scale = lax.rsqrt(squares / channels + EPS)
        hidden_two = jax.nn.silu(first * scale[..., None] * gain_mine).astype(jnp.bfloat16)
        prior_two = earlier(hidden_two)
        own_sum, up, down, up_last, down_last = conv_two_call(
            valid, place, prior_two, hidden_two, weight_two, parts
        )
        up, down = onward(up, 1), onward(down, -1)
        up_last = onward(up_last + up[:1], 1)
        down_last = onward(down_last + down[1:], -1)
        arrived = [jnp.concatenate([down[:1], up[1:]]), jnp.concatenate([up_last, down_last])]
        second = sum((r.astype(jnp.float32) for r in arrived), own_sum.astype(jnp.float32))

    block = (source + second).astype(jnp.bfloat16)
    result = jnp.broadcast_to(
        block[:, :, None, :, None, :], (frames, each, 2, width, 2, channels)
    ).reshape(frames, 2 * each, 2 * width, channels)
    return result[None]


def solution(mesh):
    sizes = mesh.devices.shape
    fine = Mesh(mesh.devices.reshape((sizes[0] // 2, 2) + sizes[1:]), ("z", "core", "tile", "group"))
    in_specs = (
        P("group", SLOT, "tile", None, None),
        P("group", None),
        P(),
        P(),
        P(SLOT + ("group",), None),
        P(SLOT + ("group",), None),
    )
    out_specs = P("group", SLOT, "tile", None, None)
    return jax.shard_map(body, mesh=fine, in_specs=in_specs, out_specs=out_specs, check_vma=False)
```

```python
import functools
import jax
import jax.numpy as jnp
from jax import lax
from jax.experimental import pallas as pl
from jax.experimental.pallas import tpu as pltpu
from jax.sharding import Mesh, PartitionSpec as P

EPS = 1e-06
SLOT = ("z", "core")
LANE = 128
TILE_ROWS = 48


def video_start(slots, counts):
    starts = jnp.cumsum(counts) - counts
    hit = starts[None, :] <= slots[:, None]
    return jnp.max(jnp.where(hit, starts[None, :], 0), axis=1)


def earlier(x):
    n = lax.axis_size(SLOT)
    return lax.ppermute(x, SLOT, [(i, i + 1) for i in range(n - 1)])


def onward(x, by, axis="tile"):
    n = lax.axis_size(axis)
    return lax.ppermute(x, axis, [(i, (i + by) % n) for i in range(n)])


def across(x, bit):
    return lax.ppermute(x, "tile", [(i, i ^ bit) for i in range(lax.axis_size("tile"))])


def from_all(x, axis):
    return jnp.stack([x] + [onward(x, d, axis) for d in range(1, lax.axis_size(axis))])


def fill_shifted(taps, slot, row, frame_row):
    width, channels = frame_row.shape
    wide = frame_row.astype(jnp.float32)
    col = lax.broadcasted_iota(jnp.int32, (width, channels), 0)
    left = jnp.where(col == 0, 0.0, pltpu.roll(wide, 1, 0))
    right = jnp.where(col == width - 1, 0.0, pltpu.roll(wide, width - 1, 0))
    taps[0, slot, row] = left.astype(frame_row.dtype)
    taps[1, slot, row] = frame_row
    taps[2, slot, row] = right.astype(frame_row.dtype)


def clear_border(taps):
    _, slots, rows, width, channels = taps.shape
    blank = jnp.zeros((width, channels), taps.dtype)
    for e in range(3):
        for slot in range(slots):
            taps[e, slot, 0] = blank
            taps[e, slot, rows - 1] = blank


def assemble_one(pieces, out, wide):
    cores, ys, zs, _, lanes = pieces.shape
    shard = out.shape[0] // (cores * ys * zs)
    share = lanes // 4
    piece_rows = shard // 4 + 1
    for z in range(zs):
        for c in range(cores):
            for y in range(ys):
                piece = pieces[c, y, z].astype(jnp.float32)
                for j in range(4):
                    rows = min(piece_rows, shard - j * piece_rows)
                    low = (j * share) // LANE * LANE
                    window = piece[:, low : min(low + 2 * LANE, lanes)]
                    shift = j * share - low
                    if shift:
                        window = pltpu.roll(window, window.shape[1] - shift, 1)
                    first = shard * (z * cores * ys + c * ys + y) + j * piece_rows
                    wide[first : first + rows, :] = window[:rows, :LANE]
    out[...] = wide[...].astype(out.dtype)


def conv_one_kernel(share, valid, place, *refs):
    own_refs, halo_refs, mine_refs, other_ref = refs[:5], refs[5:7], refs[7:12], refs[12]
    out, squares, frame_buf, acc, weight, wide, pieces = refs[13:]
    frames, each, width, channels = own_refs[0].shape
    rows = out.shape[1]
    parts = rows // each
    cores, ys, zs = pieces.shape[:3]
    blank = jnp.zeros((width, channels), frame_buf.dtype)
    for slot in range(2 * frames):
        frame_buf[slot, 0] = blank
        frame_buf[slot, rows + 1] = blank

    def put(slot, back, block):
        top = lax.rem(place[2] + parts - back, parts) * each + 1
        for j in range(each):
            frame_buf[slot, top + j] = block[j]

    for s in range(frames):
        for back, ref in zip((0, 1, 3), own_refs):
            put(frames + s, back, ref[s])
        put(frames + s, 2, own_refs[3 + s][0])
        for i, back in enumerate((0, 1, 3)):
            put(s, back, halo_refs[0][i, s])
        put(s, 2, halo_refs[1][s])
    for i, back in enumerate((0, 1, 3, 2)):
        y = lax.rem(place[1] + ys - back, ys)
        for z in range(zs):
            ref, at = (mine_refs[i], z) if i < 3 else (mine_refs[3 + 2 * z // zs], z % (zs // 2))
            pieces[place[0], y, z] = ref[at]
            pieces[1 - place[0], y, z] = other_ref[i, z]
    assemble_one(pieces, weight, wide)
    for slot in range(2 * frames):
        pairs = [(s, slot - s) for s in range(frames) if 0 <= slot - s < 3]
        columns = jnp.concatenate(
            [frame_buf[slot, b : b + rows].reshape(rows * width, channels) for b in range(3)], axis=1
        )
        for e in range(3):
            blocks = []
            for _, a in pairs:
                taps = [(a * 3 + b) * 3 + e for b in range(3)]
                blocks.append(jnp.concatenate([weight[t * channels : (t + 1) * channels, :] for t in taps], axis=0))
            packed = blocks[0] if len(blocks) == 1 else jnp.concatenate(blocks, axis=1)
            term = jnp.dot(columns, packed, preferred_element_type=jnp.float32)
            for i, (s, a) in enumerate(pairs):
                piece = valid[s, a] * term[:, i * LANE : (i + 1) * LANE]
                if a == 0:
                    acc[s, e] = piece
                else:
                    acc[s, e] = acc[s, e] + piece
    pixels = rows * width
    lane = lax.broadcasted_iota(jnp.int32, (pixels, LANE), 1)
    col = lax.rem(lax.broadcasted_iota(jnp.int32, (pixels, LANE), 0), width)
    for s in range(frames):
        left = jnp.where(col == 0, 0.0, pltpu.roll(acc[s, 0], 1, 0))
        right = jnp.where(col == width - 1, 0.0, pltpu.roll(acc[s, 2], pixels - 1, 0))
        done = jnp.where(lane < share, acc[s, 1] + left + right, 0.0)
        done = done.reshape(rows, width, LANE)
        out[s] = done
        squares[s] = jnp.sum(done * done, axis=-1)


def conv_two_kernel(valid, place, halo, own, weight, own_sum, up, down, up_last, down_last, taps, acc):
    frames, rows, width, lanes = own.shape
    each = own_sum.shape[1]
    parts = rows // each
    channels = weight.shape[1]
    clear_border(taps)
    for slot in range(2 * frames):
        source = halo if slot < frames else own
        for row in range(rows):
            fill_shifted(taps, slot, row + 1, source[slot % frames, row])
    for slot in range(2 * frames):
        pairs = [(s, slot - s) for s in range(frames) if 0 <= slot - s < 3]
        columns = jnp.concatenate(
            [
                taps[e, slot, b : b + rows].reshape(rows * width, lanes)
                for b in range(3)
                for e in range(3)
            ],
            axis=1,
        )
        blocks = [weight[a * 9 * lanes : (a + 1) * 9 * lanes, :] for _, a in pairs]
        packed = blocks[0] if len(blocks) == 1 else jnp.concatenate(blocks, axis=1)
        term = jnp.dot(columns, packed, preferred_element_type=jnp.float32)
        for i, (s, a) in enumerate(pairs):
            piece = valid[s, a] * term[:, i * channels : (i + 1) * channels]
            if a == 0:
                acc[s] = piece
            else:
                acc[s] = acc[s] + piece
    for ref, d, s, at in ((own_sum, 0, 0, 0), (own_sum, 0, 1, 1), (up, 2, 0, 0), (up, 1, 1, 1),
                          (down, 3, 0, 0), (down, 2, 1, 1), (up_last, 1, 0, 0), (down_last, 3, 1, 0)):
        top = pl.multiple_of(lax.rem(place[2] + d, parts) * (each * width), 64)
        done = acc[s, pl.ds(top, each * width), :].astype(ref.dtype)
        ref[at] = done.reshape(each, width, channels)


VMEM = pl.BlockSpec(memory_space=pltpu.VMEM)
SMEM = pl.BlockSpec(memory_space=pltpu.SMEM)
PARAMS = pltpu.CompilerParams(vmem_limit_bytes=52 * 1024 * 1024)


def conv_one_call(valid, place, own, halo, mine, other):
    frames, each, width, channels = own[0].shape
    rows = each * lax.axis_size("tile")
    zs, piece_rows, lanes = mine[0].shape
    flops = 2 * 6 * rows * width * 9 * channels * LANE
    arrays = [*own, *halo, *mine, other]
    return pl.pallas_call(
        functools.partial(conv_one_kernel, channels * each // rows),
        out_shape=[
            jax.ShapeDtypeStruct((frames, rows, width, LANE), jnp.float32),
            jax.ShapeDtypeStruct((frames, rows, width), jnp.float32),
        ],
        in_specs=[SMEM, SMEM] + [VMEM] * len(arrays),
        out_specs=[VMEM, VMEM],
        scratch_shapes=[
            pltpu.VMEM((2 * frames, rows + 2, width, channels), jnp.bfloat16),
            pltpu.VMEM((frames, 3, rows * width, LANE), jnp.float32),
            pltpu.VMEM((27 * channels, LANE), jnp.bfloat16),
            pltpu.VMEM((27 * channels, LANE), jnp.float32),
            pltpu.VMEM((2, lax.axis_size("group"), zs, piece_rows, lanes), jnp.bfloat16),
        ],
        compiler_params=PARAMS,
        cost_estimate=pl.CostEstimate(flops=flops, bytes_accessed=6_000_000, transcendentals=0),
        name="conv_one",
    )(valid, place, *arrays)


def conv_two_call(valid, place, halo, own, weight, parts):
    frames, rows, width, lanes = own.shape
    channels = weight.shape[1]
    flops = 2 * 6 * rows * width * 9 * lanes * channels
    shapes = [(n, rows // parts, width, channels) for n in (frames, frames, frames, 1, 1)]
    return pl.pallas_call(
        conv_two_kernel,
        out_shape=[jax.ShapeDtypeStruct(shape, jnp.bfloat16) for shape in shapes],
        in_specs=[SMEM, SMEM, VMEM, VMEM, VMEM],
        out_specs=[VMEM] * len(shapes),
        scratch_shapes=[
            pltpu.VMEM((3, 2 * frames, rows + 2, width, lanes), jnp.bfloat16),
            pltpu.VMEM((frames, rows * width, channels), jnp.float32),
        ],
        compiler_params=PARAMS,
        cost_estimate=pl.CostEstimate(flops=flops, bytes_accessed=6_000_000, transcendentals=0),
        name="conv_two",
    )(valid, place, halo, own, weight)


def gathered(place, mine, other, i):
    ys, zs = mine.shape[:2]
    z, c, y = i // (2 * ys), i // ys % 2, i % ys
    at = lax.rem(place[1] + ys - y, ys), z
    return jnp.where(place[0] == c, mine[at].astype(jnp.float32), other[at].astype(jnp.float32))


def assemble_two_kernel(place, mine, other, out, wide, piece_buf):
    shards = 2 * mine.shape[0] * mine.shape[1]
    channels = mine.shape[3]
    taps = out.shape[0] // LANE
    width = channels // 4
    share = 2 * taps * width // shards
    piece_rows = (share + 1) // 2
    for t in range(taps):
        wide[t * LANE + width : (t + 1) * LANE, :] = jnp.zeros((LANE - width, channels), jnp.float32)
    for m in range(shards // 2):
        even, odd = gathered(place, mine, other, 2 * m), gathered(place, mine, other, 2 * m + 1)
        half = piece_rows - 1
        piece_buf[0:TILE_ROWS, :] = even
        piece_buf[TILE_ROWS : 2 * TILE_ROWS, :] = odd
        piece_buf[half : half + 1, :] = even[half : half + 1] + odd[0:1]
        done = 0
        while done < share:
            first = share * m + done
            source = done if done <= half else done - half + TILE_ROWS
            count = min((first // width + 1) * width - first, (piece_rows if done <= half else share) - done)
            at = first // width * LANE + first % width
            wide[at : at + count, :] = piece_buf[source : source + count, :]
            done += count
    out[...] = wide[...].astype(out.dtype)


def assemble_call(kernel, place, mine, other, shape, extra, name):
    return pl.pallas_call(
        kernel,
        out_shape=jax.ShapeDtypeStruct(shape, jnp.bfloat16),
        in_specs=[SMEM, VMEM, VMEM],
        out_specs=VMEM,
        scratch_shapes=[pltpu.VMEM(shape, jnp.float32)] + extra,
        compiler_params=PARAMS,
        cost_estimate=pl.CostEstimate(flops=4_000_000, bytes_accessed=5_000_000, transcendentals=0),
        name=name,
    )(place, mine, other)


def pick(rows, columns, transposed, part, step):
    big = lax.broadcasted_iota(jnp.int32, (rows, columns), 1 if transposed else 0)
    small = lax.broadcasted_iota(jnp.int32, (rows, columns), 0 if transposed else 1)
    return (big == step * small + part).astype(jnp.bfloat16)


def body(latents, frame_counts, gain_one, gain_two, conv_one, conv_two):
    part = lax.axis_index("tile")
    parts = lax.axis_size("tile")
    side = lax.axis_index("group") % 2
    core = lax.axis_index("core")
    counts = frame_counts.reshape(-1)
    source = latents[0].astype(jnp.float32)
    frames, each, width, channels = source.shape
    share = channels // parts
    shard = conv_one.shape[0]
    piece_rows = shard // 4 + 1
    shards = lax.axis_size(SLOT) * lax.axis_size("group")
    place = jnp.stack([core, lax.axis_index("group"), part]).astype(jnp.int32)

    with jax.named_scope("pixels"):
        mean_sq = jnp.mean(source * source, axis=-1, keepdims=True)
        hidden_one = jax.nn.silu(source * lax.rsqrt(mean_sq + EPS) * gain_one).astype(jnp.bfloat16)
        own = [hidden_one, onward(hidden_one, 1), onward(hidden_one, -1)]

    def column_of(piece):
        n = lax.axis_size("z")
        return lax.all_to_all(jnp.broadcast_to(piece, (n,) + piece.shape), "z", 0, 0)

    with jax.named_scope("pieces"):
        take = pick(channels, share, False, part, parts)
        piece = jnp.dot(conv_one, take, preferred_element_type=jnp.float32).astype(jnp.bfloat16)
        piece = jnp.pad(piece, ((0, 4 * piece_rows - shard), (0, 0)))
        piece = jnp.concatenate([piece[j * piece_rows : (j + 1) * piece_rows] for j in range(4)], axis=1)
        piece = jnp.pad(piece, ((0, TILE_ROWS - piece_rows), (0, 0)))
        column = column_of(piece)

    with jax.named_scope("pixels"):
        own, column = lax.optimization_barrier((own, column))
        own = own + [onward(own[1][:1], 1), onward(own[2][1:], -1)]
        halo = [earlier(jnp.stack(own[:3])), earlier(jnp.concatenate(own[3:]))]

    def other_core(x):
        return lax.ppermute(x, "core", [(0, 1), (1, 0)])

    with jax.named_scope("weight_one"):
        mine = [column, onward(column, 1, "group"), onward(column, -1, "group")]
        conv_two, mine = lax.optimization_barrier((conv_two, mine))
        half = column.shape[0] // 2
        mine = mine + [onward(mine[1][:half], 1, "group"), onward(mine[2][half:], -1, "group")]
        rows_take = pick(TILE_ROWS, shard, True, part - 2 * side, parts)
        piece = jnp.dot(rows_take, conv_two, preferred_element_type=jnp.float32).astype(jnp.bfloat16)
        later = column_of(piece)
        mine, halo, later = lax.optimization_barrier((mine, halo, later))
        swapped = other_core(jnp.stack(mine[:3] + [jnp.concatenate(mine[3:])]))

    with jax.named_scope("weight_two"):
        later = [later] + [onward(later, d, "group") for d in range(1, lax.axis_size("group"))]

    base = lax.axis_index(SLOT) * frames
    slots = base + jnp.arange(frames, dtype=jnp.int32)
    begins = video_start(slots, counts)
    before = 2 - jnp.arange(3, dtype=jnp.int32)
    valid = (slots[:, None] - before[None, :] >= begins[:, None]).astype(jnp.float32)

    with jax.named_scope("first"):
        first, squares = conv_one_call(valid, place, own, halo, mine, swapped)

    with jax.named_scope("weight_two"):
        squares = squares + across(squares, 1)
        squares, later = lax.optimization_barrier((squares, later))
        mine = jnp.stack(later)
        swapped = other_core(mine)
        taps = shards * shard // channels
        weight_two = assemble_call(
            assemble_two_kernel, place, mine, swapped, (taps * LANE, channels),
            [pltpu.VMEM((2 * TILE_ROWS, channels), jnp.float32)], "assemble_two"
        )

    with jax.named_scope("second"):
        squares = squares + across(squares, 2)
        gain_mine = lax.dynamic_index_in_dim(gain_two.reshape(share, parts), part, 1, keepdims=False)
        gain_mine = jnp.pad(gain_mine, (0, LANE - share))
        scale = lax.rsqrt(squares / channels + EPS)
        hidden_two = jax.nn.silu(first * scale[..., None] * gain_mine).astype(jnp.bfloat16)
        prior_two = earlier(hidden_two)
        own_sum, up, down, up_last, down_last = conv_two_call(
            valid, place, prior_two, hidden_two, weight_two, parts
        )
        up, down = onward(up, 1), onward(down, -1)
        up_last = onward(up_last + up[:1], 1)
        down_last = onward(down_last + down[1:], -1)
        arrived = [jnp.concatenate([down[:1], up[1:]]), jnp.concatenate([up_last, down_last])]
        second = sum((r.astype(jnp.float32) for r in arrived), own_sum.astype(jnp.float32))

    block = (source + second).astype(jnp.bfloat16)
    result = jnp.broadcast_to(
        block[:, :, None, :, None, :], (frames, each, 2, width, 2, channels)
    ).reshape(frames, 2 * each, 2 * width, channels)
    return result[None]


def solution(mesh):
    sizes = mesh.devices.shape
    fine = Mesh(mesh.devices.reshape((sizes[0] // 2, 2) + sizes[1:]), ("z", "core", "tile", "group"))
    in_specs = (
        P("group", SLOT, "tile", None, None),
        P("group", None),
        P(),
        P(),
        P(SLOT + ("group",), None),
        P(SLOT + ("group",), None),
    )
    out_specs = P("group", SLOT, "tile", None, None)
    return jax.shard_map(body, mesh=fine, in_specs=in_specs, out_specs=out_specs, check_vma=False)
```

```python
import functools
import jax
import jax.numpy as jnp
from jax import lax
from jax.experimental import pallas as pl
from jax.experimental.pallas import tpu as pltpu
from jax.sharding import Mesh, PartitionSpec as P

EPS = 1e-06
SLOT = ("z", "core")
LANE = 128
TILE_ROWS = 48


def video_start(slots, counts):
    starts = jnp.cumsum(counts) - counts
    hit = starts[None, :] <= slots[:, None]
    return jnp.max(jnp.where(hit, starts[None, :], 0), axis=1)


def earlier(x):
    n = lax.axis_size(SLOT)
    return lax.ppermute(x, SLOT, [(i, i + 1) for i in range(n - 1)])


def onward(x, by, axis="tile"):
    n = lax.axis_size(axis)
    return lax.ppermute(x, axis, [(i, (i + by) % n) for i in range(n)])


def across(x, bit):
    return lax.ppermute(x, "tile", [(i, i ^ bit) for i in range(lax.axis_size("tile"))])


def from_all(x, axis):
    return jnp.stack([x] + [onward(x, d, axis) for d in range(1, lax.axis_size(axis))])


def fill_shifted(taps, slot, row, frame_row):
    width, channels = frame_row.shape
    wide = frame_row.astype(jnp.float32)
    col = lax.broadcasted_iota(jnp.int32, (width, channels), 0)
    left = jnp.where(col == 0, 0.0, pltpu.roll(wide, 1, 0))
    right = jnp.where(col == width - 1, 0.0, pltpu.roll(wide, width - 1, 0))
    taps[0, slot, row] = left.astype(frame_row.dtype)
    taps[1, slot, row] = frame_row
    taps[2, slot, row] = right.astype(frame_row.dtype)


def clear_border(taps):
    _, slots, rows, width, channels = taps.shape
    blank = jnp.zeros((width, channels), taps.dtype)
    for e in range(3):
        for slot in range(slots):
            taps[e, slot, 0] = blank
            taps[e, slot, rows - 1] = blank


def assemble_one(pieces, out, wide):
    cores, ys, zs, _, lanes = pieces.shape
    shard = out.shape[0] // (cores * ys * zs)
    share = lanes // 4
    piece_rows = shard // 4 + 1
    for z in range(zs):
        for c in range(cores):
            for y in range(ys):
                piece = pieces[c, y, z].astype(jnp.float32)
                for j in range(4):
                    rows = min(piece_rows, shard - j * piece_rows)
                    low = (j * share) // LANE * LANE
                    window = piece[:, low : min(low + 2 * LANE, lanes)]
                    shift = j * share - low
                    if shift:
                        window = pltpu.roll(window, window.shape[1] - shift, 1)
                    first = shard * (z * cores * ys + c * ys + y) + j * piece_rows
                    wide[first : first + rows, :] = window[:rows, :LANE]
    out[...] = wide[...].astype(out.dtype)


def conv_one_kernel(share, valid, place, halo, own, *refs):
    mine_refs, other_ref = refs[:4], refs[4]
    out, squares, frame_buf, acc, weight, wide, pieces = refs[5:]
    parts, frames, each, width, channels = own.shape
    rows = parts * each
    cores, ys, zs = pieces.shape[:3]
    blank = jnp.zeros((width, channels), frame_buf.dtype)
    for slot in range(2 * frames):
        frame_buf[slot, 0] = blank
        frame_buf[slot, rows + 1] = blank
        source = halo if slot < frames else own
        for row in range(rows):
            frame_buf[slot, row + 1] = source[row // each, slot % frames, row % each]
    for back in range(ys):
        y = lax.rem(place[1] + ys - back, ys)
        for z in range(zs):
            pieces[place[0], y, z] = mine_refs[back][z]
            pieces[1 - place[0], y, z] = other_ref[back, z]
    assemble_one(pieces, weight, wide)
    for slot in range(2 * frames):
        pairs = [(s, slot - s) for s in range(frames) if 0 <= slot - s < 3]
        columns = jnp.concatenate(
            [frame_buf[slot, b : b + rows].reshape(rows * width, channels) for b in range(3)], axis=1
        )
        for e in range(3):
            blocks = []
            for _, a in pairs:
                taps = [(a * 3 + b) * 3 + e for b in range(3)]
                blocks.append(jnp.concatenate([weight[t * channels : (t + 1) * channels, :] for t in taps], axis=0))
            packed = blocks[0] if len(blocks) == 1 else jnp.concatenate(blocks, axis=1)
            term = jnp.dot(columns, packed, preferred_element_type=jnp.float32)
            for i, (s, a) in enumerate(pairs):
                piece = valid[s, a] * term[:, i * LANE : (i + 1) * LANE]
                if a == 0:
                    acc[s, e] = piece
                else:
                    acc[s, e] = acc[s, e] + piece
    pixels = rows * width
    lane = lax.broadcasted_iota(jnp.int32, (pixels, LANE), 1)
    col = lax.rem(lax.broadcasted_iota(jnp.int32, (pixels, LANE), 0), width)
    for s in range(frames):
        left = jnp.where(col == 0, 0.0, pltpu.roll(acc[s, 0], 1, 0))
        right = jnp.where(col == width - 1, 0.0, pltpu.roll(acc[s, 2], pixels - 1, 0))
        done = jnp.where(lane < share, acc[s, 1] + left + right, 0.0)
        done = done.reshape(rows, width, LANE)
        out[s] = done
        squares[s] = jnp.sum(done * done, axis=-1)


def conv_two_kernel(valid, place, halo, own, weight, own_sum, up, down, up_last, down_last, taps, acc):
    frames, rows, width, lanes = own.shape
    each = own_sum.shape[1]
    parts = rows // each
    channels = weight.shape[1]
    clear_border(taps)
    for slot in range(2 * frames):
        source = halo if slot < frames else own
        for row in range(rows):
            fill_shifted(taps, slot, row + 1, source[slot % frames, row])
    for slot in range(2 * frames):
        pairs = [(s, slot - s) for s in range(frames) if 0 <= slot - s < 3]
        columns = jnp.concatenate(
            [
                taps[e, slot, b : b + rows].reshape(rows * width, lanes)
                for b in range(3)
                for e in range(3)
            ],
            axis=1,
        )
        blocks = [weight[a * 9 * lanes : (a + 1) * 9 * lanes, :] for _, a in pairs]
        packed = blocks[0] if len(blocks) == 1 else jnp.concatenate(blocks, axis=1)
        term = jnp.dot(columns, packed, preferred_element_type=jnp.float32)
        for i, (s, a) in enumerate(pairs):
            piece = valid[s, a] * term[:, i * channels : (i + 1) * channels]
            if a == 0:
                acc[s] = piece
            else:
                acc[s] = acc[s] + piece
    for ref, d, s, at in ((own_sum, 0, 0, 0), (own_sum, 0, 1, 1), (up, 2, 0, 0), (up, 1, 1, 1),
                          (down, 3, 0, 0), (down, 2, 1, 1), (up_last, 1, 0, 0), (down_last, 3, 1, 0)):
        top = pl.multiple_of(lax.rem(place[2] + d, parts) * (each * width), 64)
        done = acc[s, pl.ds(top, each * width), :].astype(ref.dtype)
        ref[at] = done.reshape(each, width, channels)


VMEM = pl.BlockSpec(memory_space=pltpu.VMEM)
SMEM = pl.BlockSpec(memory_space=pltpu.SMEM)
PARAMS = pltpu.CompilerParams(vmem_limit_bytes=52 * 1024 * 1024)


def conv_one_call(valid, place, own, halo, mine, other):
    parts, frames, each, width, channels = own.shape
    rows = parts * each
    zs, piece_rows, lanes = mine[0].shape
    flops = 2 * 6 * rows * width * 9 * channels * LANE
    arrays = [halo, own, *mine, other]
    return pl.pallas_call(
        functools.partial(conv_one_kernel, channels // parts),
        out_shape=[
            jax.ShapeDtypeStruct((frames, rows, width, LANE), jnp.float32),
            jax.ShapeDtypeStruct((frames, rows, width), jnp.float32),
        ],
        in_specs=[SMEM, SMEM] + [VMEM] * len(arrays),
        out_specs=[VMEM, VMEM],
        scratch_shapes=[
            pltpu.VMEM((2 * frames, rows + 2, width, channels), jnp.bfloat16),
            pltpu.VMEM((frames, 3, rows * width, LANE), jnp.float32),
            pltpu.VMEM((27 * channels, LANE), jnp.bfloat16),
            pltpu.VMEM((27 * channels, LANE), jnp.float32),
            pltpu.VMEM((2, lax.axis_size("group"), zs, piece_rows, lanes), jnp.bfloat16),
        ],
        compiler_params=PARAMS,
        cost_estimate=pl.CostEstimate(flops=flops, bytes_accessed=6_000_000, transcendentals=0),
        name="conv_one",
    )(valid, place, *arrays)


def conv_two_call(valid, place, halo, own, weight, parts):
    frames, rows, width, lanes = own.shape
    channels = weight.shape[1]
    flops = 2 * 6 * rows * width * 9 * lanes * channels
    shapes = [(n, rows // parts, width, channels) for n in (frames, frames, frames, 1, 1)]
    return pl.pallas_call(
        conv_two_kernel,
        out_shape=[jax.ShapeDtypeStruct(shape, jnp.bfloat16) for shape in shapes],
        in_specs=[SMEM, SMEM, VMEM, VMEM, VMEM],
        out_specs=[VMEM] * len(shapes),
        scratch_shapes=[
            pltpu.VMEM((3, 2 * frames, rows + 2, width, lanes), jnp.bfloat16),
            pltpu.VMEM((frames, rows * width, channels), jnp.float32),
        ],
        compiler_params=PARAMS,
        cost_estimate=pl.CostEstimate(flops=flops, bytes_accessed=6_000_000, transcendentals=0),
        name="conv_two",
    )(valid, place, halo, own, weight)


def gathered(place, mine, other, i):
    ys, zs = mine.shape[:2]
    z, c, y = i // (2 * ys), i // ys % 2, i % ys
    return jnp.where(place[0] == c, mine[y, z].astype(jnp.float32), other[y, z].astype(jnp.float32))


def assemble_two_kernel(place, mine, other, out, wide, piece_buf):
    shards = 2 * mine.shape[0] * mine.shape[1]
    channels = mine.shape[3]
    taps = out.shape[0] // LANE
    width = channels // 4
    share = 2 * taps * width // shards
    piece_rows = (share + 1) // 2
    for t in range(taps):
        wide[t * LANE + width : (t + 1) * LANE, :] = jnp.zeros((LANE - width, channels), jnp.float32)
    for m in range(shards // 2):
        even, odd = gathered(place, mine, other, 2 * m), gathered(place, mine, other, 2 * m + 1)
        half = piece_rows - 1
        piece_buf[0:TILE_ROWS, :] = even
        piece_buf[TILE_ROWS : 2 * TILE_ROWS, :] = odd
        piece_buf[half : half + 1, :] = even[half : half + 1] + odd[0:1]
        done = 0
        while done < share:
            first = share * m + done
            source = done if done <= half else done - half + TILE_ROWS
            count = min((first // width + 1) * width - first, (piece_rows if done <= half else share) - done)
            at = first // width * LANE + first % width
            wide[at : at + count, :] = piece_buf[source : source + count, :]
            done += count
    out[...] = wide[...].astype(out.dtype)


def assemble_call(kernel, place, mine, other, shape, extra, name):
    return pl.pallas_call(
        kernel,
        out_shape=jax.ShapeDtypeStruct(shape, jnp.bfloat16),
        in_specs=[SMEM, VMEM, VMEM],
        out_specs=VMEM,
        scratch_shapes=[pltpu.VMEM(shape, jnp.float32)] + extra,
        compiler_params=PARAMS,
        cost_estimate=pl.CostEstimate(flops=4_000_000, bytes_accessed=5_000_000, transcendentals=0),
        name=name,
    )(place, mine, other)


def pick(rows, columns, transposed, part, step):
    big = lax.broadcasted_iota(jnp.int32, (rows, columns), 1 if transposed else 0)
    small = lax.broadcasted_iota(jnp.int32, (rows, columns), 0 if transposed else 1)
    return (big == step * small + part).astype(jnp.bfloat16)


def body(latents, frame_counts, gain_one, gain_two, conv_one, conv_two):
    part = lax.axis_index("tile")
    parts = lax.axis_size("tile")
    side = lax.axis_index("group") % 2
    core = lax.axis_index("core")
    counts = frame_counts.reshape(-1)
    source = latents[0].astype(jnp.float32)
    frames, each, width, channels = source.shape
    share = channels // parts
    shard = conv_one.shape[0]
    piece_rows = shard // 4 + 1
    shards = lax.axis_size(SLOT) * lax.axis_size("group")
    place = jnp.stack([core, lax.axis_index("group"), part]).astype(jnp.int32)

    with jax.named_scope("pixels"):
        mean_sq = jnp.mean(source * source, axis=-1, keepdims=True)
        hidden_one = jax.nn.silu(source * lax.rsqrt(mean_sq + EPS) * gain_one).astype(jnp.bfloat16)
        own = lax.all_gather(hidden_one, "tile")

    def column_of(piece):
        n = lax.axis_size("z")
        return lax.all_to_all(jnp.broadcast_to(piece, (n,) + piece.shape), "z", 0, 0)

    with jax.named_scope("pieces"):
        take = pick(channels, share, False, part, parts)
        piece = jnp.dot(conv_one, take, preferred_element_type=jnp.float32).astype(jnp.bfloat16)
        piece = jnp.pad(piece, ((0, 4 * piece_rows - shard), (0, 0)))
        piece = jnp.concatenate([piece[j * piece_rows : (j + 1) * piece_rows] for j in range(4)], axis=1)
        piece = jnp.pad(piece, ((0, TILE_ROWS - piece_rows), (0, 0)))
        rows_take = pick(TILE_ROWS, shard, True, part - 2 * side, parts)
        piece_two = jnp.dot(rows_take, conv_two, preferred_element_type=jnp.float32).astype(jnp.bfloat16)
        column = column_of(jnp.concatenate([piece, piece_two], axis=0))
        column, later = column[:, :TILE_ROWS], column[:, TILE_ROWS:]

    with jax.named_scope("pixels"):
        halo = earlier(own)

    def other_core(x):
        return lax.ppermute(x, "core", [(0, 1), (1, 0)])

    with jax.named_scope("weight_one"):
        mine = [column] + [onward(column, d, "group") for d in range(1, lax.axis_size("group"))]
        mine, halo = lax.optimization_barrier((mine, halo))
        swapped = other_core(jnp.stack(mine))

    with jax.named_scope("weight_two"):
        later = lax.all_gather(later, "group")

    base = lax.axis_index(SLOT) * frames
    slots = base + jnp.arange(frames, dtype=jnp.int32)
    begins = video_start(slots, counts)
    before = 2 - jnp.arange(3, dtype=jnp.int32)
    valid = (slots[:, None] - before[None, :] >= begins[:, None]).astype(jnp.float32)

    with jax.named_scope("first"):
        first, squares = conv_one_call(valid, place, own, halo, mine, swapped)

    with jax.named_scope("weight_two"):
        squares = squares + across(squares, 1)
        squares, later = lax.optimization_barrier((squares, later))
        swapped = other_core(later)
        taps = shards * shard // channels
        weight_two = assemble_call(
            assemble_two_kernel, place, later, swapped, (taps * LANE, channels),
            [pltpu.VMEM((2 * TILE_ROWS, channels), jnp.float32)], "assemble_two"
        )

    with jax.named_scope("second"):
        squares = squares + across(squares, 2)
        gain_mine = lax.dynamic_index_in_dim(gain_two.reshape(share, parts), part, 1, keepdims=False)
        gain_mine = jnp.pad(gain_mine, (0, LANE - share))
        scale = lax.rsqrt(squares / channels + EPS)
        hidden_two = jax.nn.silu(first * scale[..., None] * gain_mine).astype(jnp.bfloat16)
        prior_two = earlier(hidden_two)
        own_sum, up, down, up_last, down_last = conv_two_call(
            valid, place, prior_two, hidden_two, weight_two, parts
        )
        up, down = onward(up, 1), onward(down, -1)
        up_last = onward(up_last + up[:1], 1)
        down_last = onward(down_last + down[1:], -1)
        arrived = [jnp.concatenate([down[:1], up[1:]]), jnp.concatenate([up_last, down_last])]
        second = sum((r.astype(jnp.float32) for r in arrived), own_sum.astype(jnp.float32))

    block = (source + second).astype(jnp.bfloat16)
    result = jnp.broadcast_to(
        block[:, :, None, :, None, :], (frames, each, 2, width, 2, channels)
    ).reshape(frames, 2 * each, 2 * width, channels)
    return result[None]


def solution(mesh):
    sizes = mesh.devices.shape
    fine = Mesh(mesh.devices.reshape((sizes[0] // 2, 2) + sizes[1:]), ("z", "core", "tile", "group"))
    in_specs = (
        P("group", SLOT, "tile", None, None),
        P("group", None),
        P(),
        P(),
        P(SLOT + ("group",), None),
        P(SLOT + ("group",), None),
    )
    out_specs = P("group", SLOT, "tile", None, None)
    return jax.shard_map(body, mesh=fine, in_specs=in_specs, out_specs=out_specs, check_vma=False)
```

```python
import functools
import jax
import jax.numpy as jnp
from jax import lax
from jax.experimental import pallas as pl
from jax.experimental.pallas import tpu as pltpu
from jax.sharding import Mesh, PartitionSpec as P

EPS = 1e-06
SLOT = ("z", "core")
LANE = 128
TILE_ROWS = 48


def video_start(slots, counts):
    starts = jnp.cumsum(counts) - counts
    hit = starts[None, :] <= slots[:, None]
    return jnp.max(jnp.where(hit, starts[None, :], 0), axis=1)


def earlier(x):
    n = lax.axis_size(SLOT)
    return lax.ppermute(x, SLOT, [(i, i + 1) for i in range(n - 1)])


def onward(x, by, axis="tile"):
    n = lax.axis_size(axis)
    return lax.ppermute(x, axis, [(i, (i + by) % n) for i in range(n)])


def across(x, bit):
    return lax.ppermute(x, "tile", [(i, i ^ bit) for i in range(lax.axis_size("tile"))])


def from_all(x, axis):
    return jnp.stack([x] + [onward(x, d, axis) for d in range(1, lax.axis_size(axis))])


def fill_shifted(taps, slot, row, frame_row):
    width, channels = frame_row.shape
    wide = frame_row.astype(jnp.float32)
    col = lax.broadcasted_iota(jnp.int32, (width, channels), 0)
    left = jnp.where(col == 0, 0.0, pltpu.roll(wide, 1, 0))
    right = jnp.where(col == width - 1, 0.0, pltpu.roll(wide, width - 1, 0))
    taps[0, slot, row] = left.astype(frame_row.dtype)
    taps[1, slot, row] = frame_row
    taps[2, slot, row] = right.astype(frame_row.dtype)


def clear_border(taps):
    _, slots, rows, width, channels = taps.shape
    blank = jnp.zeros((width, channels), taps.dtype)
    for e in range(3):
        for slot in range(slots):
            taps[e, slot, 0] = blank
            taps[e, slot, rows - 1] = blank


def assemble_one(place, mine, other, out, wide):
    ys, zs, _, lanes = mine.shape
    shard = out.shape[0] // (2 * ys * zs)
    share = lanes // 4
    piece_rows = shard // 4 + 1
    for pieces, core in ((mine, place[0]), (other, 1 - place[0])):
        for z in range(zs):
            top = pl.multiple_of((2 * z + core) * (ys * shard), 8)
            view = wide.at[pl.ds(top, ys * shard), :]
            for y in range(ys):
                piece = pieces[lax.rem(place[1] + ys - y, ys), z].astype(jnp.float32)
                for j in range(4):
                    rows = min(piece_rows, shard - j * piece_rows)
                    low = (j * share) // LANE * LANE
                    window = piece[:, low : min(low + 2 * LANE, lanes)]
                    shift = j * share - low
                    if shift:
                        window = pltpu.roll(window, window.shape[1] - shift, 1)
                    first = shard * y + j * piece_rows
                    view[first : first + rows, :] = window[:rows, :LANE]
    out[...] = wide[...].astype(out.dtype)


def conv_one_kernel(share, valid, place, halo, own, mine, other, out, squares, frame_buf, acc, weight, wide):
    parts, frames, each, width, channels = own.shape
    rows = parts * each
    blank = jnp.zeros((width, channels), own.dtype)
    for slot in range(2 * frames):
        frame_buf[slot, 0] = blank
        frame_buf[slot, rows + 1] = blank
        source = halo if slot < frames else own
        for back in range(parts):
            top = lax.rem(place[2] + parts - back, parts) * each + 1
            for j in range(each):
                frame_buf[slot, top + j] = source[back, slot % frames, j]
    assemble_one(place, mine, other, weight, wide)
    for slot in range(2 * frames):
        pairs = [(s, slot - s) for s in range(frames) if 0 <= slot - s < 3]
        columns = jnp.concatenate(
            [frame_buf[slot, b : b + rows].reshape(rows * width, channels) for b in range(3)], axis=1
        )
        for e in range(3):
            blocks = []
            for _, a in pairs:
                taps = [(a * 3 + b) * 3 + e for b in range(3)]
                blocks.append(jnp.concatenate([weight[t * channels : (t + 1) * channels, :] for t in taps], axis=0))
            packed = blocks[0] if len(blocks) == 1 else jnp.concatenate(blocks, axis=1)
            term = jnp.dot(columns, packed, preferred_element_type=jnp.float32)
            for i, (s, a) in enumerate(pairs):
                piece = valid[s, a] * term[:, i * LANE : (i + 1) * LANE]
                if a == 0:
                    acc[s, e] = piece
                else:
                    acc[s, e] = acc[s, e] + piece
    pixels = rows * width
    lane = lax.broadcasted_iota(jnp.int32, (pixels, LANE), 1)
    col = lax.rem(lax.broadcasted_iota(jnp.int32, (pixels, LANE), 0), width)
    for s in range(frames):
        left = jnp.where(col == 0, 0.0, pltpu.roll(acc[s, 0], 1, 0))
        right = jnp.where(col == width - 1, 0.0, pltpu.roll(acc[s, 2], pixels - 1, 0))
        done = jnp.where(lane < share, acc[s, 1] + left + right, 0.0)
        done = done.reshape(rows, width, LANE)
        out[s] = done
        squares[s] = jnp.sum(done * done, axis=-1)


def add_frames(valid, slots, source, weight, taps, add):
    frames, rows, width, lanes = source.shape
    channels = weight.shape[1]
    clear_border(taps)
    for slot in slots:
        for row in range(rows):
            fill_shifted(taps, slot % frames, row + 1, source[slot % frames, row])
    for slot in slots:
        pairs = [(s, slot - s) for s in range(frames) if 0 <= slot - s < 3]
        columns = jnp.concatenate(
            [
                taps[e, slot % frames, b : b + rows].reshape(rows * width, lanes)
                for b in range(3)
                for e in range(3)
            ],
            axis=1,
        )
        blocks = [weight[a * 9 * lanes : (a + 1) * 9 * lanes, :] for _, a in pairs]
        packed = blocks[0] if len(blocks) == 1 else jnp.concatenate(blocks, axis=1)
        term = jnp.dot(columns, packed, preferred_element_type=jnp.float32)
        for i, (s, a) in enumerate(pairs):
            add(s, valid[s, a] * term[:, i * channels : (i + 1) * channels])


def conv_two_own_kernel(valid, own, weight, acc, taps):
    frames = own.shape[0]
    seen = set()

    def add(s, piece):
        acc[s] = acc[s] + piece if s in seen else piece
        seen.add(s)

    add_frames(valid, range(frames, 2 * frames), own, weight, taps, add)


def conv_two_halo_kernel(valid, place, halo, weight, started, own_sum, up, down, up_last, down_last, taps, acc):
    frames, rows, width, _ = halo.shape
    each = own_sum.shape[1]
    parts = rows // each
    seen = set()

    def add(s, piece):
        acc[s] = (acc if s in seen else started)[s] + piece
        seen.add(s)

    add_frames(valid, range(frames), halo, weight, taps, add)
    for ref, d, s, at in ((own_sum, 0, 0, 0), (own_sum, 0, 1, 1), (up, 2, 0, 0), (up, 1, 1, 1),
                          (down, 3, 0, 0), (down, 2, 1, 1), (up_last, 1, 0, 0), (down_last, 3, 1, 0)):
        top = pl.multiple_of(lax.rem(place[2] + d, parts) * (each * width), 64)
        done = acc[s, pl.ds(top, each * width), :].astype(ref.dtype)
        ref[at] = done.reshape(each, width, done.shape[1])


VMEM = pl.BlockSpec(memory_space=pltpu.VMEM)
SMEM = pl.BlockSpec(memory_space=pltpu.SMEM)
PARAMS = pltpu.CompilerParams(vmem_limit_bytes=52 * 1024 * 1024)


def conv_one_call(valid, place, halo, own, mine, other):
    parts, frames, each, width, channels = own.shape
    rows = parts * each
    flops = 2 * 6 * rows * width * 9 * channels * LANE
    return pl.pallas_call(
        functools.partial(conv_one_kernel, channels // parts),
        out_shape=[
            jax.ShapeDtypeStruct((frames, rows, width, LANE), jnp.float32),
            jax.ShapeDtypeStruct((frames, rows, width), jnp.float32),
        ],
        in_specs=[SMEM, SMEM, VMEM, VMEM, VMEM, VMEM],
        out_specs=[VMEM, VMEM],
        scratch_shapes=[
            pltpu.VMEM((2 * frames, rows + 2, width, channels), jnp.bfloat16),
            pltpu.VMEM((frames, 3, rows * width, LANE), jnp.float32),
            pltpu.VMEM((27 * channels, LANE), jnp.bfloat16),
            pltpu.VMEM((27 * channels, LANE), jnp.float32),
        ],
        compiler_params=PARAMS,
        cost_estimate=pl.CostEstimate(flops=flops, bytes_accessed=6_000_000, transcendentals=0),
        name="conv_one",
    )(valid, place, halo, own, mine, other)


def conv_two_own_call(valid, own, weight):
    frames, rows, width, lanes = own.shape
    channels = weight.shape[1]
    return pl.pallas_call(
        conv_two_own_kernel,
        out_shape=jax.ShapeDtypeStruct((frames, rows * width, channels), jnp.float32),
        in_specs=[SMEM, VMEM, VMEM],
        out_specs=VMEM,
        scratch_shapes=[pltpu.VMEM((3, frames, rows + 2, width, lanes), jnp.bfloat16)],
        compiler_params=PARAMS,
        cost_estimate=pl.CostEstimate(flops=3_000_000_000, bytes_accessed=5_000_000, transcendentals=0),
        name="conv_two_own",
    )(valid, own, weight)


def conv_two_halo_call(valid, place, halo, weight, started, parts):
    frames, rows, width, lanes = halo.shape
    channels = weight.shape[1]
    shapes = [(n, rows // parts, width, channels) for n in (frames, frames, frames, 1, 1)]
    return pl.pallas_call(
        conv_two_halo_kernel,
        out_shape=[jax.ShapeDtypeStruct(shape, jnp.bfloat16) for shape in shapes],
        in_specs=[SMEM, SMEM, VMEM, VMEM, VMEM],
        out_specs=[VMEM] * len(shapes),
        scratch_shapes=[
            pltpu.VMEM((3, frames, rows + 2, width, lanes), jnp.bfloat16),
            pltpu.VMEM((frames, rows * width, channels), jnp.float32),
        ],
        compiler_params=PARAMS,
        cost_estimate=pl.CostEstimate(flops=3_000_000_000, bytes_accessed=6_000_000, transcendentals=0),
        name="conv_two_halo",
    )(valid, place, halo, weight, started)


def gathered(place, mine, other, i):
    ys, zs = mine.shape[:2]
    z, c, y = i // (2 * ys), i // ys % 2, i % ys
    at = lax.rem(place[1] + ys - y, ys), z
    return jnp.where(place[0] == c, mine[at].astype(jnp.float32), other[at].astype(jnp.float32))


def assemble_two_kernel(place, mine, other, out, wide, piece_buf):
    shards = 2 * mine.shape[0] * mine.shape[1]
    channels = mine.shape[3]
    taps = out.shape[0] // LANE
    width = channels // 4
    share = 2 * taps * width // shards
    piece_rows = (share + 1) // 2
    for t in range(taps):
        wide[t * LANE + width : (t + 1) * LANE, :] = jnp.zeros((LANE - width, channels), jnp.float32)
    for m in range(shards // 2):
        even, odd = gathered(place, mine, other, 2 * m), gathered(place, mine, other, 2 * m + 1)
        half = piece_rows - 1
        piece_buf[0:TILE_ROWS, :] = even
        piece_buf[TILE_ROWS : 2 * TILE_ROWS, :] = odd
        piece_buf[half : half + 1, :] = even[half : half + 1] + odd[0:1]
        done = 0
        while done < share:
            first = share * m + done
            source = done if done <= half else done - half + TILE_ROWS
            count = min((first // width + 1) * width - first, (piece_rows if done <= half else share) - done)
            at = first // width * LANE + first % width
            wide[at : at + count, :] = piece_buf[source : source + count, :]
            done += count
    out[...] = wide[...].astype(out.dtype)


def assemble_call(kernel, place, mine, other, shape, extra, name):
    return pl.pallas_call(
        kernel,
        out_shape=jax.ShapeDtypeStruct(shape, jnp.bfloat16),
        in_specs=[SMEM, VMEM, VMEM],
        out_specs=VMEM,
        scratch_shapes=[pltpu.VMEM(shape, jnp.float32)] + extra,
        compiler_params=PARAMS,
        cost_estimate=pl.CostEstimate(flops=4_000_000, bytes_accessed=12_000_000, transcendentals=0),
        name=name,
    )(place, mine, other)


def pick(rows, columns, transposed, part, step):
    big = lax.broadcasted_iota(jnp.int32, (rows, columns), 1 if transposed else 0)
    small = lax.broadcasted_iota(jnp.int32, (rows, columns), 0 if transposed else 1)
    return (big == step * small + part).astype(jnp.bfloat16)


def body(latents, frame_counts, gain_one, gain_two, conv_one, conv_two):
    part = lax.axis_index("tile")
    parts = lax.axis_size("tile")
    side = lax.axis_index("group") % 2
    core = lax.axis_index("core")
    counts = frame_counts.reshape(-1)
    source = latents[0].astype(jnp.float32)
    frames, each, width, channels = source.shape
    share = channels // parts
    shard = conv_one.shape[0]
    piece_rows = shard // 4 + 1
    shards = lax.axis_size(SLOT) * lax.axis_size("group")
    place = jnp.stack([core, lax.axis_index("group"), part]).astype(jnp.int32)

    with jax.named_scope("pixels"):
        mean_sq = jnp.mean(source * source, axis=-1, keepdims=True)
        hidden_one = jax.nn.silu(source * lax.rsqrt(mean_sq + EPS) * gain_one).astype(jnp.bfloat16)
        own_all = from_all(hidden_one, "tile")

    with jax.named_scope("pieces"):
        take = pick(channels, share, False, part, parts)
        piece = jnp.dot(conv_one, take, preferred_element_type=jnp.float32).astype(jnp.bfloat16)
        piece = jnp.pad(piece, ((0, 4 * piece_rows - shard), (0, 0)))
        piece = jnp.concatenate([piece[j * piece_rows : (j + 1) * piece_rows] for j in range(4)], axis=1)
        piece = jnp.pad(piece, ((0, TILE_ROWS - piece_rows), (0, 0)))
        rows_take = pick(TILE_ROWS, shard, True, part - 2 * side, parts)
        piece_two = jnp.dot(rows_take, conv_two, preferred_element_type=jnp.float32).astype(jnp.bfloat16)
        pieces = jnp.concatenate([piece, piece_two], axis=0)
        column = lax.all_to_all(jnp.broadcast_to(pieces, (lax.axis_size("z"),) + pieces.shape), "z", 0, 0)

    column, own_all = lax.optimization_barrier((column, own_all))
    with jax.named_scope("weight_one"):
        mine = [column[:, :TILE_ROWS]]
        mine += [onward(mine[0], d, "group") for d in range(1, lax.axis_size("group"))]
        prior_all = earlier(own_all)

    with jax.named_scope("weight_two"):
        later, _ = lax.optimization_barrier((column[:, TILE_ROWS:], mine[1]))
        later = [later] + [onward(later, d, "group") for d in range(1, lax.axis_size("group"))]

    with jax.named_scope("weight_one"):
        mine, prior_all = lax.optimization_barrier((mine, prior_all))
        one_mine = jnp.stack(mine)
        one_swapped = lax.ppermute(one_mine, "core", [(0, 1), (1, 0)])

    base = lax.axis_index(SLOT) * frames
    slots = base + jnp.arange(frames, dtype=jnp.int32)
    begins = video_start(slots, counts)
    before = 2 - jnp.arange(3, dtype=jnp.int32)
    valid = (slots[:, None] - before[None, :] >= begins[:, None]).astype(jnp.float32)

    with jax.named_scope("first"):
        first, squares = conv_one_call(valid, place, prior_all, own_all, one_mine, one_swapped)

    with jax.named_scope("weight_two"):
        squares = squares + across(squares, 1)
        squares, later = lax.optimization_barrier((squares, later))
        mine = jnp.stack(later)
        swapped = lax.ppermute(mine, "core", [(0, 1), (1, 0)])
        taps = shards * shard // channels
        weight_two = assemble_call(
            assemble_two_kernel, place, mine, swapped, (taps * LANE, channels),
            [pltpu.VMEM((2 * TILE_ROWS, channels), jnp.float32)], "assemble_two"
        )

    with jax.named_scope("second"):
        other_squares, weight_two = lax.optimization_barrier((across(squares, 2), weight_two))
        squares = squares + other_squares
        gain_mine = lax.dynamic_index_in_dim(gain_two.reshape(share, parts), part, 1, keepdims=False)
        gain_mine = jnp.pad(gain_mine, (0, LANE - share))
        scale = lax.rsqrt(squares / channels + EPS)
        hidden_two = jax.nn.silu(first * scale[..., None] * gain_mine).astype(jnp.bfloat16)
        prior_two = earlier(hidden_two)
        started = conv_two_own_call(valid, hidden_two, weight_two)
        own_sum, up, down, up_last, down_last = conv_two_halo_call(
            valid, place, prior_two, weight_two, started, parts
        )
        up, down = onward(up, 1), onward(down, -1)
        up_last = onward(up_last + up[:1], 1)
        down_last = onward(down_last + down[1:], -1)
        arrived = [jnp.concatenate([down[:1], up[1:]]), jnp.concatenate([up_last, down_last])]
        second = sum((r.astype(jnp.float32) for r in arrived), own_sum.astype(jnp.float32))

    block = (source + second).astype(jnp.bfloat16)
    result = jnp.broadcast_to(
        block[:, :, None, :, None, :], (frames, each, 2, width, 2, channels)
    ).reshape(frames, 2 * each, 2 * width, channels)
    return result[None]


def solution(mesh):
    sizes = mesh.devices.shape
    fine = Mesh(mesh.devices.reshape((sizes[0] // 2, 2) + sizes[1:]), ("z", "core", "tile", "group"))
    in_specs = (
        P("group", SLOT, "tile", None, None),
        P("group", None),
        P(),
        P(),
        P(SLOT + ("group",), None),
        P(SLOT + ("group",), None),
    )
    out_specs = P("group", SLOT, "tile", None, None)
    return jax.shard_map(body, mesh=fine, in_specs=in_specs, out_specs=out_specs, check_vma=False)
```

```python
import functools
import jax
import jax.numpy as jnp
from jax import lax
from jax.experimental import pallas as pl
from jax.experimental.pallas import tpu as pltpu
from jax.sharding import Mesh, PartitionSpec as P

EPS = 1e-06
SLOT = ("z", "core")
LANE = 128
TILE_ROWS = 48


def video_start(slots, counts):
    starts = jnp.cumsum(counts) - counts
    hit = starts[None, :] <= slots[:, None]
    return jnp.max(jnp.where(hit, starts[None, :], 0), axis=1)


def earlier(x):
    n = lax.axis_size(SLOT)
    return lax.ppermute(x, SLOT, [(i, i + 1) for i in range(n - 1)])


def onward(x, by, axis="tile"):
    n = lax.axis_size(axis)
    return lax.ppermute(x, axis, [(i, (i + by) % n) for i in range(n)])


def across(x, bit):
    return lax.ppermute(x, "tile", [(i, i ^ bit) for i in range(lax.axis_size("tile"))])


def from_all(x, axis):
    return jnp.stack([x] + [onward(x, d, axis) for d in range(1, lax.axis_size(axis))])


def fill_shifted(taps, slot, row, frame_row):
    width, channels = frame_row.shape
    wide = frame_row.astype(jnp.float32)
    col = lax.broadcasted_iota(jnp.int32, (width, channels), 0)
    left = jnp.where(col == 0, 0.0, pltpu.roll(wide, 1, 0))
    right = jnp.where(col == width - 1, 0.0, pltpu.roll(wide, width - 1, 0))
    taps[0, slot, row] = left.astype(frame_row.dtype)
    taps[1, slot, row] = frame_row
    taps[2, slot, row] = right.astype(frame_row.dtype)


def clear_border(taps):
    _, slots, rows, width, channels = taps.shape
    blank = jnp.zeros((width, channels), taps.dtype)
    for e in range(3):
        for slot in range(slots):
            taps[e, slot, 0] = blank
            taps[e, slot, rows - 1] = blank


def assemble_one(place, mine, other, out, wide):
    ys, zs, _, lanes = mine.shape
    shard = out.shape[0] // (2 * ys * zs)
    share = lanes // 4
    piece_rows = shard // 4 + 1
    for pieces, core in ((mine, place[0]), (other, 1 - place[0])):
        for z in range(zs):
            top = pl.multiple_of((2 * z + core) * (ys * shard), 8)
            view = wide.at[pl.ds(top, ys * shard), :]
            for y in range(ys):
                piece = pieces[lax.rem(place[1] + ys - y, ys), z].astype(jnp.float32)
                for j in range(4):
                    rows = min(piece_rows, shard - j * piece_rows)
                    low = (j * share) // LANE * LANE
                    window = piece[:, low : min(low + 2 * LANE, lanes)]
                    shift = j * share - low
                    if shift:
                        window = pltpu.roll(window, window.shape[1] - shift, 1)
                    first = shard * y + j * piece_rows
                    view[first : first + rows, :] = window[:rows, :LANE]
    out[...] = wide[...].astype(out.dtype)


def conv_one_kernel(share, valid, place, halo, own, mine, other, out, squares, frame_buf, acc, weight, wide):
    parts, frames, each, width, channels = own.shape
    rows = parts * each
    blank = jnp.zeros((width, channels), own.dtype)
    for slot in range(2 * frames):
        frame_buf[slot, 0] = blank
        frame_buf[slot, rows + 1] = blank
        source = halo if slot < frames else own
        for back in range(parts):
            top = lax.rem(place[2] + parts - back, parts) * each + 1
            for j in range(each):
                frame_buf[slot, top + j] = source[back, slot % frames, j]
    assemble_one(place, mine, other, weight, wide)
    for slot in range(2 * frames):
        pairs = [(s, slot - s) for s in range(frames) if 0 <= slot - s < 3]
        columns = jnp.concatenate(
            [frame_buf[slot, b : b + rows].reshape(rows * width, channels) for b in range(3)], axis=1
        )
        for e in range(3):
            blocks = []
            for _, a in pairs:
                taps = [(a * 3 + b) * 3 + e for b in range(3)]
                blocks.append(jnp.concatenate([weight[t * channels : (t + 1) * channels, :] for t in taps], axis=0))
            packed = blocks[0] if len(blocks) == 1 else jnp.concatenate(blocks, axis=1)
            term = jnp.dot(columns, packed, preferred_element_type=jnp.float32)
            for i, (s, a) in enumerate(pairs):
                piece = valid[s, a] * term[:, i * LANE : (i + 1) * LANE]
                if a == 0:
                    acc[s, e] = piece
                else:
                    acc[s, e] = acc[s, e] + piece
    pixels = rows * width
    lane = lax.broadcasted_iota(jnp.int32, (pixels, LANE), 1)
    col = lax.rem(lax.broadcasted_iota(jnp.int32, (pixels, LANE), 0), width)
    for s in range(frames):
        left = jnp.where(col == 0, 0.0, pltpu.roll(acc[s, 0], 1, 0))
        right = jnp.where(col == width - 1, 0.0, pltpu.roll(acc[s, 2], pixels - 1, 0))
        done = jnp.where(lane < share, acc[s, 1] + left + right, 0.0)
        done = done.reshape(rows, width, LANE)
        out[s] = done
        squares[s] = jnp.sum(done * done, axis=-1)


def conv_two_kernel(plan, valid, place, halo, own, weight, *rest):
    *outs, taps = rest
    frames, rows, width, lanes = own.shape
    each = outs[0].shape[1]
    parts = rows // each
    channels = weight.shape[1]
    clear_border(taps)
    for slot in range(2 * frames):
        source = halo if slot < frames else own
        for row in range(rows):
            fill_shifted(taps, slot, row + 1, source[slot % frames, row])
    for s, targets in enumerate(plan):
        tops = [lax.rem(place[2] + d, parts) * each for d, _, _ in targets]
        total = None
        for a in range(3):
            columns = jnp.concatenate(
                [
                    jnp.concatenate(
                        [
                            taps[e, s + a, pl.ds(top + b, each)].reshape(each * width, lanes)
                            for b in range(3)
                            for e in range(3)
                        ],
                        axis=1,
                    )
                    for top in tops
                ],
                axis=0,
            )
            block = weight[a * 9 * lanes : (a + 1) * 9 * lanes, :]
            term = valid[s, a] * jnp.dot(columns, block, preferred_element_type=jnp.float32)
            total = term if total is None else total + term
        for i, (_, ref, at) in enumerate(targets):
            done = total[i * each * width : (i + 1) * each * width]
            outs[ref][at] = done.astype(outs[ref].dtype).reshape(each, width, channels)


def finish_kernel(latents, own_sum, up, down, up_last, down_last, out, wide):
    frames, each, width, _ = own_sum.shape
    for s in range(frames):
        for r in range(each):
            terms = [own_sum[s, r], down[0, r], up_last[0, r]] if s == 0 else [own_sum[s, r], up[1, r], down_last[0, r]]
            total = sum((t.astype(jnp.float32) for t in terms[1:]), terms[0].astype(jnp.float32))
            block = (latents[s, r].astype(jnp.float32) + total).astype(out.dtype).astype(jnp.float32)
            for k in range(wide.shape[0]):
                lanes = slice(k * LANE, (k + 1) * LANE)
                wide[k, pl.ds(0, width, stride=2), :] = block[:, lanes]
                wide[k, pl.ds(1, width, stride=2), :] = block[:, lanes]
                doubled = wide[k].astype(out.dtype)
                out[s, 2 * r, :, lanes] = doubled
                out[s, 2 * r + 1, :, lanes] = doubled


VMEM = pl.BlockSpec(memory_space=pltpu.VMEM)
SMEM = pl.BlockSpec(memory_space=pltpu.SMEM)
PARAMS = pltpu.CompilerParams(vmem_limit_bytes=52 * 1024 * 1024)


def conv_one_call(valid, place, halo, own, mine, other):
    parts, frames, each, width, channels = own.shape
    rows = parts * each
    flops = 2 * 6 * rows * width * 9 * channels * LANE
    return pl.pallas_call(
        functools.partial(conv_one_kernel, channels // parts),
        out_shape=[
            jax.ShapeDtypeStruct((frames, rows, width, LANE), jnp.float32),
            jax.ShapeDtypeStruct((frames, rows, width), jnp.float32),
        ],
        in_specs=[SMEM, SMEM, VMEM, VMEM, VMEM, VMEM],
        out_specs=[VMEM, VMEM],
        scratch_shapes=[
            pltpu.VMEM((2 * frames, rows + 2, width, channels), jnp.bfloat16),
            pltpu.VMEM((frames, 3, rows * width, LANE), jnp.float32),
            pltpu.VMEM((27 * channels, LANE), jnp.bfloat16),
            pltpu.VMEM((27 * channels, LANE), jnp.float32),
        ],
        compiler_params=PARAMS,
        cost_estimate=pl.CostEstimate(flops=flops, bytes_accessed=6_000_000, transcendentals=0),
        name="conv_one",
    )(valid, place, halo, own, mine, other)


def conv_two_call(plan, leads, valid, place, halo, own, weight, parts):
    frames, rows, width, lanes = own.shape
    channels = weight.shape[1]
    shapes = [(n, rows // parts, width, channels) for n in leads]
    return pl.pallas_call(
        functools.partial(conv_two_kernel, plan),
        out_shape=[jax.ShapeDtypeStruct(shape, jnp.bfloat16) for shape in shapes],
        in_specs=[SMEM, SMEM, VMEM, VMEM, VMEM],
        out_specs=[VMEM] * len(shapes),
        scratch_shapes=[pltpu.VMEM((3, 2 * frames, rows + 2, width, lanes), jnp.bfloat16)],
        compiler_params=PARAMS,
        cost_estimate=pl.CostEstimate(flops=3_000_000_000, bytes_accessed=6_000_000, transcendentals=0),
        name="conv_two",
    )(valid, place, halo, own, weight)


def finish_call(*arrays):
    frames, each, width, channels = arrays[0].shape
    return pl.pallas_call(
        finish_kernel,
        out_shape=jax.ShapeDtypeStruct((frames, 2 * each, 2 * width, channels), jnp.bfloat16),
        in_specs=[VMEM] * len(arrays),
        out_specs=VMEM,
        scratch_shapes=[pltpu.VMEM((channels // LANE, 2 * width, LANE), jnp.float32)],
        compiler_params=PARAMS,
        cost_estimate=pl.CostEstimate(flops=2_000_000, bytes_accessed=3_000_000, transcendentals=0),
        name="finish",
    )(*arrays)


def gathered(place, mine, other, i):
    ys, zs = mine.shape[:2]
    z, c, y = i // (2 * ys), i // ys % 2, i % ys
    at = lax.rem(place[1] + ys - y, ys), z
    return jnp.where(place[0] == c, mine[at].astype(jnp.float32), other[at].astype(jnp.float32))


def assemble_two_kernel(place, mine, other, out, wide, piece_buf):
    shards = 2 * mine.shape[0] * mine.shape[1]
    channels = mine.shape[3]
    taps = out.shape[0] // LANE
    width = channels // 4
    share = 2 * taps * width // shards
    piece_rows = (share + 1) // 2
    for t in range(taps):
        wide[t * LANE + width : (t + 1) * LANE, :] = jnp.zeros((LANE - width, channels), jnp.float32)
    for m in range(shards // 2):
        even, odd = gathered(place, mine, other, 2 * m), gathered(place, mine, other, 2 * m + 1)
        half = piece_rows - 1
        piece_buf[0:TILE_ROWS, :] = even
        piece_buf[TILE_ROWS : 2 * TILE_ROWS, :] = odd
        piece_buf[half : half + 1, :] = even[half : half + 1] + odd[0:1]
        done = 0
        while done < share:
            first = share * m + done
            source = done if done <= half else done - half + TILE_ROWS
            count = min((first // width + 1) * width - first, (piece_rows if done <= half else share) - done)
            at = first // width * LANE + first % width
            wide[at : at + count, :] = piece_buf[source : source + count, :]
            done += count
    out[...] = wide[...].astype(out.dtype)


def assemble_call(kernel, place, mine, other, shape, extra, name):
    return pl.pallas_call(
        kernel,
        out_shape=jax.ShapeDtypeStruct(shape, jnp.bfloat16),
        in_specs=[SMEM, VMEM, VMEM],
        out_specs=VMEM,
        scratch_shapes=[pltpu.VMEM(shape, jnp.float32)] + extra,
        compiler_params=PARAMS,
        cost_estimate=pl.CostEstimate(flops=4_000_000, bytes_accessed=12_000_000, transcendentals=0),
        name=name,
    )(place, mine, other)


def pick(rows, columns, transposed, part, step):
    big = lax.broadcasted_iota(jnp.int32, (rows, columns), 1 if transposed else 0)
    small = lax.broadcasted_iota(jnp.int32, (rows, columns), 0 if transposed else 1)
    return (big == step * small + part).astype(jnp.bfloat16)


def body(latents, frame_counts, gain_one, gain_two, conv_one, conv_two):
    part = lax.axis_index("tile")
    parts = lax.axis_size("tile")
    side = lax.axis_index("group") % 2
    core = lax.axis_index("core")
    counts = frame_counts.reshape(-1)
    source = latents[0].astype(jnp.float32)
    frames, each, width, channels = source.shape
    share = channels // parts
    shard = conv_one.shape[0]
    piece_rows = shard // 4 + 1
    shards = lax.axis_size(SLOT) * lax.axis_size("group")
    place = jnp.stack([core, lax.axis_index("group"), part]).astype(jnp.int32)

    with jax.named_scope("pixels"):
        mean_sq = jnp.mean(source * source, axis=-1, keepdims=True)
        hidden_one = jax.nn.silu(source * lax.rsqrt(mean_sq + EPS) * gain_one).astype(jnp.bfloat16)
        own_all = from_all(hidden_one, "tile")

    with jax.named_scope("pieces"):
        take = pick(channels, share, False, part, parts)
        piece = jnp.dot(conv_one, take, preferred_element_type=jnp.float32).astype(jnp.bfloat16)
        piece = jnp.pad(piece, ((0, 4 * piece_rows - shard), (0, 0)))
        piece = jnp.concatenate([piece[j * piece_rows : (j + 1) * piece_rows] for j in range(4)], axis=1)
        piece = jnp.pad(piece, ((0, TILE_ROWS - piece_rows), (0, 0)))
        rows_take = pick(TILE_ROWS, shard, True, part - 2 * side, parts)
        piece_two = jnp.dot(rows_take, conv_two, preferred_element_type=jnp.float32).astype(jnp.bfloat16)
        pieces = jnp.concatenate([piece, piece_two], axis=0)
        column = lax.all_to_all(jnp.broadcast_to(pieces, (lax.axis_size("z"),) + pieces.shape), "z", 0, 0)

    column, own_all = lax.optimization_barrier((column, own_all))
    with jax.named_scope("weight_one"):
        mine = [column[:, :TILE_ROWS]]
        mine += [onward(mine[0], d, "group") for d in range(1, lax.axis_size("group"))]
        prior_all = earlier(own_all)

    with jax.named_scope("weight_two"):
        later, _ = lax.optimization_barrier((column[:, TILE_ROWS:], mine[1]))
        later = [later] + [onward(later, d, "group") for d in range(1, lax.axis_size("group"))]

    with jax.named_scope("weight_one"):
        mine, prior_all = lax.optimization_barrier((mine, prior_all))
        one_mine = jnp.stack(mine)
        one_swapped = lax.ppermute(one_mine, "core", [(0, 1), (1, 0)])

    base = lax.axis_index(SLOT) * frames
    slots = base + jnp.arange(frames, dtype=jnp.int32)
    begins = video_start(slots, counts)
    before = 2 - jnp.arange(3, dtype=jnp.int32)
    valid = (slots[:, None] - before[None, :] >= begins[:, None]).astype(jnp.float32)

    with jax.named_scope("first"):
        first, squares = conv_one_call(valid, place, prior_all, own_all, one_mine, one_swapped)

    with jax.named_scope("weight_two"):
        squares, later = lax.optimization_barrier((squares, later))
        squares = squares + across(squares, 1)
        mine = jnp.stack(later)
        swapped = lax.ppermute(mine, "core", [(0, 1), (1, 0)])
        taps = shards * shard // channels
        weight_two = assemble_call(
            assemble_two_kernel, place, mine, swapped, (taps * LANE, channels),
            [pltpu.VMEM((2 * TILE_ROWS, channels), jnp.float32)], "assemble_two"
        )

    with jax.named_scope("second"):
        other_squares, weight_two = lax.optimization_barrier((across(squares, 2), weight_two))
        squares = squares + other_squares
        gain_mine = lax.dynamic_index_in_dim(gain_two.reshape(share, parts), part, 1, keepdims=False)
        gain_mine = jnp.pad(gain_mine, (0, LANE - share))
        scale = lax.rsqrt(squares / channels + EPS)
        hidden_two = jax.nn.silu(first * scale[..., None] * gain_mine).astype(jnp.bfloat16)
        prior_two = earlier(hidden_two)
        operands = (valid, place, prior_two, hidden_two, weight_two, parts)
        up, down = conv_two_call((((2, 0, 0), (3, 1, 0)), ((1, 0, 1), (2, 1, 1))), (2, 2), *operands)
        up, down = onward(up, 1), onward(down, -1)
        own_sum, up_last, down_last = conv_two_call(
            (((0, 0, 0), (1, 1, 0)), ((3, 2, 0), (0, 0, 1))), (2, 1, 1), *operands
        )
        up_last = onward(up_last + up[:1], 1)
        down_last = onward(down_last + down[1:], -1)

    return finish_call(latents[0], own_sum, up, down, up_last, down_last)[None]


def solution(mesh):
    sizes = mesh.devices.shape
    fine = Mesh(mesh.devices.reshape((sizes[0] // 2, 2) + sizes[1:]), ("z", "core", "tile", "group"))
    in_specs = (
        P("group", SLOT, "tile", None, None),
        P("group", None),
        P(),
        P(),
        P(SLOT + ("group",), None),
        P(SLOT + ("group",), None),
    )
    out_specs = P("group", SLOT, "tile", None, None)
    return jax.shard_map(body, mesh=fine, in_specs=in_specs, out_specs=out_specs, check_vma=False)
```

```python
import functools
import jax
import jax.numpy as jnp
from jax import lax
from jax.experimental import pallas as pl
from jax.experimental.pallas import tpu as pltpu
from jax.sharding import Mesh, PartitionSpec as P

EPS = 1e-06
SLOT = ("z", "core")
LANE = 128
TILE_ROWS = 48


def video_start(slots, counts):
    starts = jnp.cumsum(counts) - counts
    hit = starts[None, :] <= slots[:, None]
    return jnp.max(jnp.where(hit, starts[None, :], 0), axis=1)


def earlier(x):
    n = lax.axis_size(SLOT)
    return lax.ppermute(x, SLOT, [(i, i + 1) for i in range(n - 1)])


def onward(x, by, axis="tile"):
    n = lax.axis_size(axis)
    return lax.ppermute(x, axis, [(i, (i + by) % n) for i in range(n)])


def across(x, bit):
    return lax.ppermute(x, "tile", [(i, i ^ bit) for i in range(lax.axis_size("tile"))])


def from_all(x, axis):
    return jnp.stack([x] + [onward(x, d, axis) for d in range(1, lax.axis_size(axis))])


def fill_shifted(taps, slot, row, frame_row):
    width, channels = frame_row.shape
    wide = frame_row.astype(jnp.float32)
    col = lax.broadcasted_iota(jnp.int32, (width, channels), 0)
    left = jnp.where(col == 0, 0.0, pltpu.roll(wide, 1, 0))
    right = jnp.where(col == width - 1, 0.0, pltpu.roll(wide, width - 1, 0))
    taps[0, slot, row] = left.astype(frame_row.dtype)
    taps[1, slot, row] = frame_row
    taps[2, slot, row] = right.astype(frame_row.dtype)


def clear_border(taps):
    _, slots, rows, width, channels = taps.shape
    blank = jnp.zeros((width, channels), taps.dtype)
    for e in range(3):
        for slot in range(slots):
            taps[e, slot, 0] = blank
            taps[e, slot, rows - 1] = blank


def assemble_one(place, mine, other, out, wide):
    ys, zs, _, lanes = mine.shape
    shard = out.shape[0] // (2 * ys * zs)
    share = lanes // 4
    piece_rows = shard // 4 + 1
    for pieces, core in ((mine, place[0]), (other, 1 - place[0])):
        for z in range(zs):
            top = pl.multiple_of((2 * z + core) * (ys * shard), 8)
            view = wide.at[pl.ds(top, ys * shard), :]
            for y in range(ys):
                piece = pieces[lax.rem(place[1] + ys - y, ys), z].astype(jnp.float32)
                for j in range(4):
                    rows = min(piece_rows, shard - j * piece_rows)
                    low = (j * share) // LANE * LANE
                    window = piece[:, low : min(low + 2 * LANE, lanes)]
                    shift = j * share - low
                    if shift:
                        window = pltpu.roll(window, window.shape[1] - shift, 1)
                    first = shard * y + j * piece_rows
                    view[first : first + rows, :] = window[:rows, :LANE]
    out[...] = wide[...].astype(out.dtype)


def conv_one_kernel(share, valid, place, halo, own, mine, other, out, squares, frame_buf, acc, weight, wide):
    parts, frames, each, width, channels = own.shape
    rows = parts * each
    blank = jnp.zeros((width, channels), own.dtype)
    for slot in range(2 * frames):
        frame_buf[slot, 0] = blank
        frame_buf[slot, rows + 1] = blank
        source = halo if slot < frames else own
        for back in range(parts):
            top = lax.rem(place[2] + parts - back, parts) * each + 1
            for j in range(each):
                frame_buf[slot, top + j] = source[back, slot % frames, j]
    assemble_one(place, mine, other, weight, wide)
    for slot in range(2 * frames):
        pairs = [(s, slot - s) for s in range(frames) if 0 <= slot - s < 3]
        columns = jnp.concatenate(
            [frame_buf[slot, b : b + rows].reshape(rows * width, channels) for b in range(3)], axis=1
        )
        for e in range(3):
            blocks = []
            for _, a in pairs:
                taps = [(a * 3 + b) * 3 + e for b in range(3)]
                blocks.append(jnp.concatenate([weight[t * channels : (t + 1) * channels, :] for t in taps], axis=0))
            packed = blocks[0] if len(blocks) == 1 else jnp.concatenate(blocks, axis=1)
            term = jnp.dot(columns, packed, preferred_element_type=jnp.float32)
            for i, (s, a) in enumerate(pairs):
                piece = valid[s, a] * term[:, i * LANE : (i + 1) * LANE]
                if a == 0:
                    acc[s, e] = piece
                else:
                    acc[s, e] = acc[s, e] + piece
    pixels = rows * width
    lane = lax.broadcasted_iota(jnp.int32, (pixels, LANE), 1)
    col = lax.rem(lax.broadcasted_iota(jnp.int32, (pixels, LANE), 0), width)
    for s in range(frames):
        left = jnp.where(col == 0, 0.0, pltpu.roll(acc[s, 0], 1, 0))
        right = jnp.where(col == width - 1, 0.0, pltpu.roll(acc[s, 2], pixels - 1, 0))
        done = jnp.where(lane < share, acc[s, 1] + left + right, 0.0)
        done = done.reshape(rows, width, LANE)
        out[s] = done
        squares[s] = jnp.sum(done * done, axis=-1)


def conv_two_kernel(valid, place, halo, own, weight, own_sum, up, down, up_last, down_last, taps, acc):
    frames, rows, width, lanes = own.shape
    each = own_sum.shape[1]
    parts = rows // each
    channels = weight.shape[1]
    clear_border(taps)
    for slot in range(2 * frames):
        source = halo if slot < frames else own
        for row in range(rows):
            fill_shifted(taps, slot, row + 1, source[slot % frames, row])
    for slot in range(2 * frames):
        pairs = [(s, slot - s) for s in range(frames) if 0 <= slot - s < 3]
        columns = jnp.concatenate(
            [
                taps[e, slot, b : b + rows].reshape(rows * width, lanes)
                for b in range(3)
                for e in range(3)
            ],
            axis=1,
        )
        blocks = [weight[a * 9 * lanes : (a + 1) * 9 * lanes, :] for _, a in pairs]
        packed = blocks[0] if len(blocks) == 1 else jnp.concatenate(blocks, axis=1)
        term = jnp.dot(columns, packed, preferred_element_type=jnp.float32)
        for i, (s, a) in enumerate(pairs):
            piece = valid[s, a] * term[:, i * channels : (i + 1) * channels]
            if a == 0:
                acc[s] = piece
            else:
                acc[s] = acc[s] + piece
    for ref, d, s, at in ((own_sum, 0, 0, 0), (own_sum, 0, 1, 1), (up, 2, 0, 0), (up, 1, 1, 1),
                          (down, 3, 0, 0), (down, 2, 1, 1), (up_last, 1, 0, 0), (down_last, 3, 1, 0)):
        top = pl.multiple_of(lax.rem(place[2] + d, parts) * (each * width), 64)
        done = acc[s, pl.ds(top, each * width), :].astype(ref.dtype)
        ref[at] = done.reshape(each, width, channels)


def finish_kernel(latents, own_sum, up, down, up_last, down_last, out, wide):
    frames, each, width, _ = own_sum.shape
    for s in range(frames):
        for r in range(each):
            terms = [own_sum[s, r], down[0, r], up_last[0, r]] if s == 0 else [own_sum[s, r], up[1, r], down_last[0, r]]
            total = sum((t.astype(jnp.float32) for t in terms[1:]), terms[0].astype(jnp.float32))
            block = (latents[s, r].astype(jnp.float32) + total).astype(out.dtype).astype(jnp.float32)
            for k in range(wide.shape[0]):
                lanes = slice(k * LANE, (k + 1) * LANE)
                wide[k, pl.ds(0, width, stride=2), :] = block[:, lanes]
                wide[k, pl.ds(1, width, stride=2), :] = block[:, lanes]
                doubled = wide[k].astype(out.dtype)
                out[s, 2 * r, :, lanes] = doubled
                out[s, 2 * r + 1, :, lanes] = doubled


VMEM = pl.BlockSpec(memory_space=pltpu.VMEM)
SMEM = pl.BlockSpec(memory_space=pltpu.SMEM)
PARAMS = pltpu.CompilerParams(vmem_limit_bytes=52 * 1024 * 1024)


def conv_one_call(valid, place, halo, own, mine, other):
    parts, frames, each, width, channels = own.shape
    rows = parts * each
    flops = 2 * 6 * rows * width * 9 * channels * LANE
    return pl.pallas_call(
        functools.partial(conv_one_kernel, channels // parts),
        out_shape=[
            jax.ShapeDtypeStruct((frames, rows, width, LANE), jnp.float32),
            jax.ShapeDtypeStruct((frames, rows, width), jnp.float32),
        ],
        in_specs=[SMEM, SMEM, VMEM, VMEM, VMEM, VMEM],
        out_specs=[VMEM, VMEM],
        scratch_shapes=[
            pltpu.VMEM((2 * frames, rows + 2, width, channels), jnp.bfloat16),
            pltpu.VMEM((frames, 3, rows * width, LANE), jnp.float32),
            pltpu.VMEM((27 * channels, LANE), jnp.bfloat16),
            pltpu.VMEM((27 * channels, LANE), jnp.float32),
        ],
        compiler_params=PARAMS,
        cost_estimate=pl.CostEstimate(flops=flops, bytes_accessed=6_000_000, transcendentals=0),
        name="conv_one",
    )(valid, place, halo, own, mine, other)


def conv_two_call(valid, place, halo, own, weight, parts):
    frames, rows, width, lanes = own.shape
    channels = weight.shape[1]
    flops = 2 * 6 * rows * width * 9 * lanes * channels
    shapes = [(n, rows // parts, width, channels) for n in (frames, frames, frames, 1, 1)]
    return pl.pallas_call(
        conv_two_kernel,
        out_shape=[jax.ShapeDtypeStruct(shape, jnp.bfloat16) for shape in shapes],
        in_specs=[SMEM, SMEM, VMEM, VMEM, VMEM],
        out_specs=[VMEM] * len(shapes),
        scratch_shapes=[
            pltpu.VMEM((3, 2 * frames, rows + 2, width, lanes), jnp.bfloat16),
            pltpu.VMEM((frames, rows * width, channels), jnp.float32),
        ],
        compiler_params=PARAMS,
        cost_estimate=pl.CostEstimate(flops=flops, bytes_accessed=6_000_000, transcendentals=0),
        name="conv_two",
    )(valid, place, halo, own, weight)


def finish_call(*arrays):
    frames, each, width, channels = arrays[0].shape
    return pl.pallas_call(
        finish_kernel,
        out_shape=jax.ShapeDtypeStruct((frames, 2 * each, 2 * width, channels), jnp.bfloat16),
        in_specs=[VMEM] * len(arrays),
        out_specs=VMEM,
        scratch_shapes=[pltpu.VMEM((channels // LANE, 2 * width, LANE), jnp.float32)],
        compiler_params=PARAMS,
        cost_estimate=pl.CostEstimate(flops=2_000_000, bytes_accessed=3_000_000, transcendentals=0),
        name="finish",
    )(*arrays)


def gathered(place, mine, other, i):
    ys, zs = mine.shape[:2]
    z, c, y = i // (2 * ys), i // ys % 2, i % ys
    at = lax.rem(place[1] + ys - y, ys), z
    return jnp.where(place[0] == c, mine[at].astype(jnp.float32), other[at].astype(jnp.float32))


def assemble_two_kernel(place, mine, other, out, wide, piece_buf):
    shards = 2 * mine.shape[0] * mine.shape[1]
    channels = mine.shape[3]
    taps = out.shape[0] // LANE
    width = channels // 4
    share = 2 * taps * width // shards
    piece_rows = (share + 1) // 2
    for t in range(taps):
        wide[t * LANE + width : (t + 1) * LANE, :] = jnp.zeros((LANE - width, channels), jnp.float32)
    for m in range(shards // 2):
        even, odd = gathered(place, mine, other, 2 * m), gathered(place, mine, other, 2 * m + 1)
        half = piece_rows - 1
        piece_buf[0:TILE_ROWS, :] = even
        piece_buf[TILE_ROWS : 2 * TILE_ROWS, :] = odd
        piece_buf[half : half + 1, :] = even[half : half + 1] + odd[0:1]
        done = 0
        while done < share:
            first = share * m + done
            source = done if done <= half else done - half + TILE_ROWS
            count = min((first // width + 1) * width - first, (piece_rows if done <= half else share) - done)
            at = first // width * LANE + first % width
            wide[at : at + count, :] = piece_buf[source : source + count, :]
            done += count
    out[...] = wide[...].astype(out.dtype)


def assemble_call(kernel, place, mine, other, shape, extra, name):
    return pl.pallas_call(
        kernel,
        out_shape=jax.ShapeDtypeStruct(shape, jnp.bfloat16),
        in_specs=[SMEM, VMEM, VMEM],
        out_specs=VMEM,
        scratch_shapes=[pltpu.VMEM(shape, jnp.float32)] + extra,
        compiler_params=PARAMS,
        cost_estimate=pl.CostEstimate(flops=4_000_000, bytes_accessed=12_000_000, transcendentals=0),
        name=name,
    )(place, mine, other)


def pick(rows, columns, transposed, part, step):
    big = lax.broadcasted_iota(jnp.int32, (rows, columns), 1 if transposed else 0)
    small = lax.broadcasted_iota(jnp.int32, (rows, columns), 0 if transposed else 1)
    return (big == step * small + part).astype(jnp.bfloat16)


def body(latents, frame_counts, gain_one, gain_two, conv_one, conv_two):
    part = lax.axis_index("tile")
    parts = lax.axis_size("tile")
    side = lax.axis_index("group") % 2
    core = lax.axis_index("core")
    counts = frame_counts.reshape(-1)
    source = latents[0].astype(jnp.float32)
    frames, each, width, channels = source.shape
    share = channels // parts
    shard = conv_one.shape[0]
    piece_rows = shard // 4 + 1
    shards = lax.axis_size(SLOT) * lax.axis_size("group")
    place = jnp.stack([core, lax.axis_index("group"), part]).astype(jnp.int32)

    with jax.named_scope("pixels"):
        mean_sq = jnp.mean(source * source, axis=-1, keepdims=True)
        hidden_one = jax.nn.silu(source * lax.rsqrt(mean_sq + EPS) * gain_one).astype(jnp.bfloat16)
        own_all = from_all(hidden_one, "tile")

    with jax.named_scope("pieces"):
        take = pick(channels, share, False, part, parts)
        piece = jnp.dot(conv_one, take, preferred_element_type=jnp.float32).astype(jnp.bfloat16)
        piece = jnp.pad(piece, ((0, 4 * piece_rows - shard), (0, 0)))
        piece = jnp.concatenate([piece[j * piece_rows : (j + 1) * piece_rows] for j in range(4)], axis=1)
        piece = jnp.pad(piece, ((0, TILE_ROWS - piece_rows), (0, 0)))
        rows_take = pick(TILE_ROWS, shard, True, part - 2 * side, parts)
        piece_two = jnp.dot(rows_take, conv_two, preferred_element_type=jnp.float32).astype(jnp.bfloat16)
        pieces = jnp.concatenate([piece, piece_two], axis=0)
        column = lax.all_to_all(jnp.broadcast_to(pieces, (lax.axis_size("z"),) + pieces.shape), "z", 0, 0)

    column, own_all = lax.optimization_barrier((column, own_all))
    with jax.named_scope("weight_one"):
        mine = [column[:, :TILE_ROWS]]
        mine += [onward(mine[0], d, "group") for d in range(1, lax.axis_size("group"))]
        prior_all = earlier(own_all)

    with jax.named_scope("weight_two"):
        later, _ = lax.optimization_barrier((column[:, TILE_ROWS:], mine[1]))
        later = [later] + [onward(later, d, "group") for d in range(1, lax.axis_size("group"))]

    with jax.named_scope("weight_one"):
        mine, prior_all = lax.optimization_barrier((mine, prior_all))
        one_mine = jnp.stack(mine)
        one_swapped = lax.ppermute(one_mine, "core", [(0, 1), (1, 0)])

    base = lax.axis_index(SLOT) * frames
    slots = base + jnp.arange(frames, dtype=jnp.int32)
    begins = video_start(slots, counts)
    before = 2 - jnp.arange(3, dtype=jnp.int32)
    valid = (slots[:, None] - before[None, :] >= begins[:, None]).astype(jnp.float32)

    with jax.named_scope("first"):
        first, squares = conv_one_call(valid, place, prior_all, own_all, one_mine, one_swapped)

    with jax.named_scope("weight_two"):
        squares = squares + across(squares, 1)
        other_squares, later = lax.optimization_barrier((across(squares, 2), later))
        mine = jnp.stack(later)
        swapped = lax.ppermute(mine, "core", [(0, 1), (1, 0)])
        taps = shards * shard // channels
        weight_two = assemble_call(
            assemble_two_kernel, place, mine, swapped, (taps * LANE, channels),
            [pltpu.VMEM((2 * TILE_ROWS, channels), jnp.float32)], "assemble_two"
        )

    with jax.named_scope("second"):
        squares = squares + other_squares
        gain_mine = lax.dynamic_index_in_dim(gain_two.reshape(share, parts), part, 1, keepdims=False)
        gain_mine = jnp.pad(gain_mine, (0, LANE - share))
        scale = lax.rsqrt(squares / channels + EPS)
        hidden_two = jax.nn.silu(first * scale[..., None] * gain_mine).astype(jnp.bfloat16)
        prior_two = earlier(hidden_two)
        own_sum, up, down, up_last, down_last = conv_two_call(
            valid, place, prior_two, hidden_two, weight_two, parts
        )
        up, down = onward(up, 1), onward(down, -1)
        up_last = onward(up_last + up[:1], 1)
        down_last = onward(down_last + down[1:], -1)

    return finish_call(latents[0], own_sum, up, down, up_last, down_last)[None]


def solution(mesh):
    sizes = mesh.devices.shape
    fine = Mesh(mesh.devices.reshape((sizes[0] // 2, 2) + sizes[1:]), ("z", "core", "tile", "group"))
    in_specs = (
        P("group", SLOT, "tile", None, None),
        P("group", None),
        P(),
        P(),
        P(SLOT + ("group",), None),
        P(SLOT + ("group",), None),
    )
    out_specs = P("group", SLOT, "tile", None, None)
    return jax.shard_map(body, mesh=fine, in_specs=in_specs, out_specs=out_specs, check_vma=False)
```

```python
import functools
import jax
import jax.numpy as jnp
from jax import lax
from jax.experimental import pallas as pl
from jax.experimental.pallas import tpu as pltpu
from jax.sharding import Mesh, PartitionSpec as P

EPS = 1e-06
SLOT = ("z", "core")
LANE = 128
TILE_ROWS = 48


def video_start(slots, counts):
    starts = jnp.cumsum(counts) - counts
    hit = starts[None, :] <= slots[:, None]
    return jnp.max(jnp.where(hit, starts[None, :], 0), axis=1)


def earlier(x):
    n = lax.axis_size(SLOT)
    return lax.ppermute(x, SLOT, [(i, i + 1) for i in range(n - 1)])


def onward(x, by, axis="tile"):
    n = lax.axis_size(axis)
    return lax.ppermute(x, axis, [(i, (i + by) % n) for i in range(n)])


def across(x, bit):
    return lax.ppermute(x, "tile", [(i, i ^ bit) for i in range(lax.axis_size("tile"))])


def from_all(x, axis):
    return jnp.stack([x] + [onward(x, d, axis) for d in range(1, lax.axis_size(axis))])


def fill_shifted(taps, slot, row, frame_row):
    width, channels = frame_row.shape
    wide = frame_row.astype(jnp.float32)
    col = lax.broadcasted_iota(jnp.int32, (width, channels), 0)
    left = jnp.where(col == 0, 0.0, pltpu.roll(wide, 1, 0))
    right = jnp.where(col == width - 1, 0.0, pltpu.roll(wide, width - 1, 0))
    taps[0, slot, row] = left.astype(frame_row.dtype)
    taps[1, slot, row] = frame_row
    taps[2, slot, row] = right.astype(frame_row.dtype)


def clear_border(taps):
    _, slots, rows, width, channels = taps.shape
    blank = jnp.zeros((width, channels), taps.dtype)
    for e in range(3):
        for slot in range(slots):
            taps[e, slot, 0] = blank
            taps[e, slot, rows - 1] = blank


def assemble_one(place, mine, other, out, wide):
    ys, zs, _, lanes = mine.shape
    shard = out.shape[0] // (2 * ys * zs)
    share = lanes // 4
    piece_rows = shard // 4 + 1
    for pieces, core in ((mine, place[0]), (other, 1 - place[0])):
        for z in range(zs):
            top = pl.multiple_of((2 * z + core) * (ys * shard), 8)
            view = wide.at[pl.ds(top, ys * shard), :]
            for y in range(ys):
                piece = pieces[lax.rem(place[1] + ys - y, ys), z].astype(jnp.float32)
                for j in range(4):
                    rows = min(piece_rows, shard - j * piece_rows)
                    low = (j * share) // LANE * LANE
                    window = piece[:, low : min(low + 2 * LANE, lanes)]
                    shift = j * share - low
                    if shift:
                        window = pltpu.roll(window, window.shape[1] - shift, 1)
                    first = shard * y + j * piece_rows
                    view[first : first + rows, :] = window[:rows, :LANE]
    out[...] = wide[...].astype(out.dtype)


def conv_one_kernel(share, valid, place, halo, own, mine, other, out, squares, frame_buf, acc, weight, wide):
    parts, frames, each, width, channels = own.shape
    rows = parts * each
    blank = jnp.zeros((width, channels), own.dtype)
    for slot in range(2 * frames):
        frame_buf[slot, 0] = blank
        frame_buf[slot, rows + 1] = blank
        source = halo if slot < frames else own
        for back in range(parts):
            top = lax.rem(place[2] + parts - back, parts) * each + 1
            for j in range(each):
                frame_buf[slot, top + j] = source[back, slot % frames, j]
    assemble_one(place, mine, other, weight, wide)
    for slot in range(2 * frames):
        pairs = [(s, slot - s) for s in range(frames) if 0 <= slot - s < 3]
        columns = jnp.concatenate(
            [frame_buf[slot, b : b + rows].reshape(rows * width, channels) for b in range(3)], axis=1
        )
        for e in range(3):
            blocks = []
            for _, a in pairs:
                taps = [(a * 3 + b) * 3 + e for b in range(3)]
                blocks.append(jnp.concatenate([weight[t * channels : (t + 1) * channels, :] for t in taps], axis=0))
            packed = blocks[0] if len(blocks) == 1 else jnp.concatenate(blocks, axis=1)
            term = jnp.dot(columns, packed, preferred_element_type=jnp.float32)
            for i, (s, a) in enumerate(pairs):
                piece = valid[s, a] * term[:, i * LANE : (i + 1) * LANE]
                if a == 0:
                    acc[s, e] = piece
                else:
                    acc[s, e] = acc[s, e] + piece
    pixels = rows * width
    lane = lax.broadcasted_iota(jnp.int32, (pixels, LANE), 1)
    col = lax.rem(lax.broadcasted_iota(jnp.int32, (pixels, LANE), 0), width)
    for s in range(frames):
        left = jnp.where(col == 0, 0.0, pltpu.roll(acc[s, 0], 1, 0))
        right = jnp.where(col == width - 1, 0.0, pltpu.roll(acc[s, 2], pixels - 1, 0))
        done = jnp.where(lane < share, acc[s, 1] + left + right, 0.0)
        done = done.reshape(rows, width, LANE)
        out[s] = done
        squares[s] = jnp.sum(done * done, axis=-1)


def add_frames(valid, slots, source, weight, taps, add):
    frames, rows, width, lanes = source.shape
    channels = weight.shape[1]
    clear_border(taps)
    for slot in slots:
        for row in range(rows):
            fill_shifted(taps, slot % frames, row + 1, source[slot % frames, row])
    for slot in slots:
        pairs = [(s, slot - s) for s in range(frames) if 0 <= slot - s < 3]
        columns = jnp.concatenate(
            [
                taps[e, slot % frames, b : b + rows].reshape(rows * width, lanes)
                for b in range(3)
                for e in range(3)
            ],
            axis=1,
        )
        blocks = [weight[a * 9 * lanes : (a + 1) * 9 * lanes, :] for _, a in pairs]
        packed = blocks[0] if len(blocks) == 1 else jnp.concatenate(blocks, axis=1)
        term = jnp.dot(columns, packed, preferred_element_type=jnp.float32)
        for i, (s, a) in enumerate(pairs):
            add(s, valid[s, a] * term[:, i * channels : (i + 1) * channels])


def conv_two_own_kernel(valid, own, weight, acc, taps):
    frames = own.shape[0]
    seen = set()

    def add(s, piece):
        acc[s] = acc[s] + piece if s in seen else piece
        seen.add(s)

    add_frames(valid, range(frames, 2 * frames), own, weight, taps, add)


def conv_two_halo_kernel(valid, place, halo, weight, started, own_sum, up, down, up_last, down_last, taps, acc):
    frames, rows, width, _ = halo.shape
    each = own_sum.shape[1]
    parts = rows // each
    seen = set()

    def add(s, piece):
        acc[s] = (acc if s in seen else started)[s] + piece
        seen.add(s)

    add_frames(valid, range(frames), halo, weight, taps, add)
    for ref, d, s, at in ((own_sum, 0, 0, 0), (own_sum, 0, 1, 1), (up, 2, 0, 0), (up, 1, 1, 1),
                          (down, 3, 0, 0), (down, 2, 1, 1), (up_last, 1, 0, 0), (down_last, 3, 1, 0)):
        top = pl.multiple_of(lax.rem(place[2] + d, parts) * (each * width), 64)
        done = acc[s, pl.ds(top, each * width), :].astype(ref.dtype)
        ref[at] = done.reshape(each, width, done.shape[1])


def finish_kernel(latents, own_sum, up, down, up_last, down_last, out, wide):
    frames, each, width, _ = own_sum.shape
    for s in range(frames):
        for r in range(each):
            terms = [own_sum[s, r], down[0, r], up_last[0, r]] if s == 0 else [own_sum[s, r], up[1, r], down_last[0, r]]
            total = sum((t.astype(jnp.float32) for t in terms[1:]), terms[0].astype(jnp.float32))
            block = (latents[s, r].astype(jnp.float32) + total).astype(out.dtype).astype(jnp.float32)
            for k in range(wide.shape[0]):
                lanes = slice(k * LANE, (k + 1) * LANE)
                wide[k, pl.ds(0, width, stride=2), :] = block[:, lanes]
                wide[k, pl.ds(1, width, stride=2), :] = block[:, lanes]
                doubled = wide[k].astype(out.dtype)
                out[s, 2 * r, :, lanes] = doubled
                out[s, 2 * r + 1, :, lanes] = doubled


VMEM = pl.BlockSpec(memory_space=pltpu.VMEM)
SMEM = pl.BlockSpec(memory_space=pltpu.SMEM)
PARAMS = pltpu.CompilerParams(vmem_limit_bytes=52 * 1024 * 1024)


def conv_one_call(valid, place, halo, own, mine, other):
    parts, frames, each, width, channels = own.shape
    rows = parts * each
    flops = 2 * 6 * rows * width * 9 * channels * LANE
    return pl.pallas_call(
        functools.partial(conv_one_kernel, channels // parts),
        out_shape=[
            jax.ShapeDtypeStruct((frames, rows, width, LANE), jnp.float32),
            jax.ShapeDtypeStruct((frames, rows, width), jnp.float32),
        ],
        in_specs=[SMEM, SMEM, VMEM, VMEM, VMEM, VMEM],
        out_specs=[VMEM, VMEM],
        scratch_shapes=[
            pltpu.VMEM((2 * frames, rows + 2, width, channels), jnp.bfloat16),
            pltpu.VMEM((frames, 3, rows * width, LANE), jnp.float32),
            pltpu.VMEM((27 * channels, LANE), jnp.bfloat16),
            pltpu.VMEM((27 * channels, LANE), jnp.float32),
        ],
        compiler_params=PARAMS,
        cost_estimate=pl.CostEstimate(flops=flops, bytes_accessed=6_000_000, transcendentals=0),
        name="conv_one",
    )(valid, place, halo, own, mine, other)


def conv_two_own_call(valid, own, weight):
    frames, rows, width, lanes = own.shape
    channels = weight.shape[1]
    return pl.pallas_call(
        conv_two_own_kernel,
        out_shape=jax.ShapeDtypeStruct((frames, rows * width, channels), jnp.float32),
        in_specs=[SMEM, VMEM, VMEM],
        out_specs=VMEM,
        scratch_shapes=[pltpu.VMEM((3, frames, rows + 2, width, lanes), jnp.bfloat16)],
        compiler_params=PARAMS,
        cost_estimate=pl.CostEstimate(flops=3_000_000_000, bytes_accessed=5_000_000, transcendentals=0),
        name="conv_two_own",
    )(valid, own, weight)


def conv_two_halo_call(valid, place, halo, weight, started, parts):
    frames, rows, width, lanes = halo.shape
    channels = weight.shape[1]
    shapes = [(n, rows // parts, width, channels) for n in (frames, frames, frames, 1, 1)]
    return pl.pallas_call(
        conv_two_halo_kernel,
        out_shape=[jax.ShapeDtypeStruct(shape, jnp.bfloat16) for shape in shapes],
        in_specs=[SMEM, SMEM, VMEM, VMEM, VMEM],
        out_specs=[VMEM] * len(shapes),
        scratch_shapes=[
            pltpu.VMEM((3, frames, rows + 2, width, lanes), jnp.bfloat16),
            pltpu.VMEM((frames, rows * width, channels), jnp.float32),
        ],
        compiler_params=PARAMS,
        cost_estimate=pl.CostEstimate(flops=3_000_000_000, bytes_accessed=6_000_000, transcendentals=0),
        name="conv_two_halo",
    )(valid, place, halo, weight, started)


def finish_call(*arrays):
    frames, each, width, channels = arrays[0].shape
    return pl.pallas_call(
        finish_kernel,
        out_shape=jax.ShapeDtypeStruct((frames, 2 * each, 2 * width, channels), jnp.bfloat16),
        in_specs=[VMEM] * len(arrays),
        out_specs=VMEM,
        scratch_shapes=[pltpu.VMEM((channels // LANE, 2 * width, LANE), jnp.float32)],
        compiler_params=PARAMS,
        cost_estimate=pl.CostEstimate(flops=2_000_000, bytes_accessed=3_000_000, transcendentals=0),
        name="finish",
    )(*arrays)


def gathered(place, mine, other, i):
    ys, zs = mine.shape[:2]
    z, c, y = i // (2 * ys), i // ys % 2, i % ys
    at = lax.rem(place[1] + ys - y, ys), z
    return jnp.where(place[0] == c, mine[at].astype(jnp.float32), other[at].astype(jnp.float32))


def assemble_two_kernel(place, mine, other, out, wide, piece_buf):
    shards = 2 * mine.shape[0] * mine.shape[1]
    channels = mine.shape[3]
    taps = out.shape[0] // LANE
    width = channels // 4
    share = 2 * taps * width // shards
    piece_rows = (share + 1) // 2
    for t in range(taps):
        wide[t * LANE + width : (t + 1) * LANE, :] = jnp.zeros((LANE - width, channels), jnp.float32)
    for m in range(shards // 2):
        even, odd = gathered(place, mine, other, 2 * m), gathered(place, mine, other, 2 * m + 1)
        half = piece_rows - 1
        piece_buf[0:TILE_ROWS, :] = even
        piece_buf[TILE_ROWS : 2 * TILE_ROWS, :] = odd
        piece_buf[half : half + 1, :] = even[half : half + 1] + odd[0:1]
        done = 0
        while done < share:
            first = share * m + done
            source = done if done <= half else done - half + TILE_ROWS
            count = min((first // width + 1) * width - first, (piece_rows if done <= half else share) - done)
            at = first // width * LANE + first % width
            wide[at : at + count, :] = piece_buf[source : source + count, :]
            done += count
    out[...] = wide[...].astype(out.dtype)


def assemble_call(kernel, place, mine, other, shape, extra, name):
    return pl.pallas_call(
        kernel,
        out_shape=jax.ShapeDtypeStruct(shape, jnp.bfloat16),
        in_specs=[SMEM, VMEM, VMEM],
        out_specs=VMEM,
        scratch_shapes=[pltpu.VMEM(shape, jnp.float32)] + extra,
        compiler_params=PARAMS,
        cost_estimate=pl.CostEstimate(flops=4_000_000, bytes_accessed=12_000_000, transcendentals=0),
        name=name,
    )(place, mine, other)


def pick(rows, columns, transposed, part, step):
    big = lax.broadcasted_iota(jnp.int32, (rows, columns), 1 if transposed else 0)
    small = lax.broadcasted_iota(jnp.int32, (rows, columns), 0 if transposed else 1)
    return (big == step * small + part).astype(jnp.bfloat16)


def body(latents, frame_counts, gain_one, gain_two, conv_one, conv_two):
    part = lax.axis_index("tile")
    parts = lax.axis_size("tile")
    side = lax.axis_index("group") % 2
    core = lax.axis_index("core")
    counts = frame_counts.reshape(-1)
    source = latents[0].astype(jnp.float32)
    frames, each, width, channels = source.shape
    share = channels // parts
    shard = conv_one.shape[0]
    piece_rows = shard // 4 + 1
    shards = lax.axis_size(SLOT) * lax.axis_size("group")
    place = jnp.stack([core, lax.axis_index("group"), part]).astype(jnp.int32)

    with jax.named_scope("pixels"):
        mean_sq = jnp.mean(source * source, axis=-1, keepdims=True)
        hidden_one = jax.nn.silu(source * lax.rsqrt(mean_sq + EPS) * gain_one).astype(jnp.bfloat16)
        own_all = from_all(hidden_one, "tile")

    with jax.named_scope("pieces"):
        take = pick(channels, share, False, part, parts)
        piece = jnp.dot(conv_one, take, preferred_element_type=jnp.float32).astype(jnp.bfloat16)
        piece = jnp.pad(piece, ((0, 4 * piece_rows - shard), (0, 0)))
        piece = jnp.concatenate([piece[j * piece_rows : (j + 1) * piece_rows] for j in range(4)], axis=1)
        piece = jnp.pad(piece, ((0, TILE_ROWS - piece_rows), (0, 0)))
        rows_take = pick(TILE_ROWS, shard, True, part - 2 * side, parts)
        piece_two = jnp.dot(rows_take, conv_two, preferred_element_type=jnp.float32).astype(jnp.bfloat16)
        pieces = jnp.concatenate([piece, piece_two], axis=0)
        column = lax.all_to_all(jnp.broadcast_to(pieces, (lax.axis_size("z"),) + pieces.shape), "z", 0, 0)

    column, own_all = lax.optimization_barrier((column, own_all))
    with jax.named_scope("weight_one"):
        mine = [column[:, :TILE_ROWS]]
        mine += [onward(mine[0], d, "group") for d in range(1, lax.axis_size("group"))]
        prior_all = earlier(own_all)

    with jax.named_scope("weight_two"):
        later, _ = lax.optimization_barrier((column[:, TILE_ROWS:], mine[1]))
        later = [later] + [onward(later, d, "group") for d in range(1, lax.axis_size("group"))]

    with jax.named_scope("weight_one"):
        mine, prior_all = lax.optimization_barrier((mine, prior_all))
        one_mine = jnp.stack(mine)
        one_swapped = lax.ppermute(one_mine, "core", [(0, 1), (1, 0)])

    base = lax.axis_index(SLOT) * frames
    slots = base + jnp.arange(frames, dtype=jnp.int32)
    begins = video_start(slots, counts)
    before = 2 - jnp.arange(3, dtype=jnp.int32)
    valid = (slots[:, None] - before[None, :] >= begins[:, None]).astype(jnp.float32)

    with jax.named_scope("first"):
        first, squares = conv_one_call(valid, place, prior_all, own_all, one_mine, one_swapped)

    with jax.named_scope("weight_two"):
        squares = squares + across(squares, 1)
        squares, later = lax.optimization_barrier((squares, later))
        mine = jnp.stack(later)
        swapped = lax.ppermute(mine, "core", [(0, 1), (1, 0)])
        taps = shards * shard // channels
        weight_two = assemble_call(
            assemble_two_kernel, place, mine, swapped, (taps * LANE, channels),
            [pltpu.VMEM((2 * TILE_ROWS, channels), jnp.float32)], "assemble_two"
        )

    with jax.named_scope("second"):
        other_squares, weight_two = lax.optimization_barrier((across(squares, 2), weight_two))
        squares = squares + other_squares
        gain_mine = lax.dynamic_index_in_dim(gain_two.reshape(share, parts), part, 1, keepdims=False)
        gain_mine = jnp.pad(gain_mine, (0, LANE - share))
        scale = lax.rsqrt(squares / channels + EPS)
        hidden_two = jax.nn.silu(first * scale[..., None] * gain_mine).astype(jnp.bfloat16)
        prior_two = earlier(hidden_two)
        started = conv_two_own_call(valid, hidden_two, weight_two)
        own_sum, up, down, up_last, down_last = conv_two_halo_call(
            valid, place, prior_two, weight_two, started, parts
        )
        up, down = onward(up, 1), onward(down, -1)
        up_last = onward(up_last + up[:1], 1)
        down_last = onward(down_last + down[1:], -1)

    return finish_call(latents[0], own_sum, up, down, up_last, down_last)[None]


def solution(mesh):
    sizes = mesh.devices.shape
    fine = Mesh(mesh.devices.reshape((sizes[0] // 2, 2) + sizes[1:]), ("z", "core", "tile", "group"))
    in_specs = (
        P("group", SLOT, "tile", None, None),
        P("group", None),
        P(),
        P(),
        P(SLOT + ("group",), None),
        P(SLOT + ("group",), None),
    )
    out_specs = P("group", SLOT, "tile", None, None)
    return jax.shard_map(body, mesh=fine, in_specs=in_specs, out_specs=out_specs, check_vma=False)
```

```python
import functools
import jax
import jax.numpy as jnp
from jax import lax
from jax.experimental import pallas as pl
from jax.experimental.pallas import tpu as pltpu
from jax.sharding import Mesh, PartitionSpec as P

EPS = 1e-06
SLOT = ("z", "core")
LANE = 128
TILE_ROWS = 48


def video_start(slots, counts):
    starts = jnp.cumsum(counts) - counts
    hit = starts[None, :] <= slots[:, None]
    return jnp.max(jnp.where(hit, starts[None, :], 0), axis=1)


def earlier(x):
    n = lax.axis_size(SLOT)
    return lax.ppermute(x, SLOT, [(i, i + 1) for i in range(n - 1)])


def onward(x, by, axis="tile"):
    n = lax.axis_size(axis)
    return lax.ppermute(x, axis, [(i, (i + by) % n) for i in range(n)])


def across(x, bit):
    return lax.ppermute(x, "tile", [(i, i ^ bit) for i in range(lax.axis_size("tile"))])


def from_all(x, axis):
    return jnp.stack([x] + [onward(x, d, axis) for d in range(1, lax.axis_size(axis))])


def fill_shifted(taps, slot, row, frame_row):
    width, channels = frame_row.shape
    wide = frame_row.astype(jnp.float32)
    col = lax.broadcasted_iota(jnp.int32, (width, channels), 0)
    left = jnp.where(col == 0, 0.0, pltpu.roll(wide, 1, 0))
    right = jnp.where(col == width - 1, 0.0, pltpu.roll(wide, width - 1, 0))
    taps[0, slot, row] = left.astype(frame_row.dtype)
    taps[1, slot, row] = frame_row
    taps[2, slot, row] = right.astype(frame_row.dtype)


def clear_border(taps):
    _, slots, rows, width, channels = taps.shape
    blank = jnp.zeros((width, channels), taps.dtype)
    for e in range(3):
        for slot in range(slots):
            taps[e, slot, 0] = blank
            taps[e, slot, rows - 1] = blank


def assemble_one(place, mine, other, out, wide):
    ys, zs, _, lanes = mine.shape
    shard = out.shape[0] // (2 * ys * zs)
    share = lanes // 4
    piece_rows = shard // 4 + 1
    for pieces, core in ((mine, place[0]), (other, 1 - place[0])):
        for z in range(zs):
            top = pl.multiple_of((2 * z + core) * (ys * shard), 8)
            view = wide.at[pl.ds(top, ys * shard + 8), :]
            for y in range(ys):
                piece = pieces[lax.rem(place[1] + ys - y, ys), z].astype(jnp.float32)
                for j in range(4):
                    rows = min(piece_rows, shard - j * piece_rows)
                    low = (j * share) // LANE * LANE
                    window = piece[:, low : min(low + 2 * LANE, lanes)]
                    shift = j * share - low
                    if shift:
                        window = pltpu.roll(window, window.shape[1] - shift, 1)
                    first = shard * y + j * piece_rows
                    view[first : first + rows, :] = window[:rows, :LANE]
    out[...] = wide[: out.shape[0], :].astype(out.dtype)


def conv_one_kernel(share, valid, place, halo, own, mine, other, out, frame_buf, acc, weight, wide):
    parts, frames, each, width, channels = own.shape
    rows = parts * each
    blank = jnp.zeros((width, channels), own.dtype)
    for slot in range(2 * frames):
        frame_buf[slot, 0] = blank
        frame_buf[slot, rows + 1] = blank
        source = halo if slot < frames else own
        for back in range(parts):
            top = lax.rem(place[2] + parts - back, parts) * each + 1
            for j in range(each):
                frame_buf[slot, top + j] = source[back, slot % frames, j]
    assemble_one(place, mine, other, weight, wide)
    for slot in range(2 * frames):
        pairs = [(s, slot - s) for s in range(frames) if 0 <= slot - s < 3]
        columns = jnp.concatenate(
            [frame_buf[slot, b : b + rows].reshape(rows * width, channels) for b in range(3)], axis=1
        )
        for e in range(3):
            blocks = []
            for _, a in pairs:
                taps = [(a * 3 + b) * 3 + e for b in range(3)]
                blocks.append(jnp.concatenate([weight[t * channels : (t + 1) * channels, :] for t in taps], axis=0))
            packed = blocks[0] if len(blocks) == 1 else jnp.concatenate(blocks, axis=1)
            term = jnp.dot(columns, packed, preferred_element_type=jnp.float32)
            for i, (s, a) in enumerate(pairs):
                piece = valid[s, a] * term[:, i * LANE : (i + 1) * LANE]
                if a == 0:
                    acc[s, e] = piece
                else:
                    acc[s, e] = acc[s, e] + piece
    pixels = rows * width
    lane = lax.broadcasted_iota(jnp.int32, (pixels, LANE), 1)
    col = lax.rem(lax.broadcasted_iota(jnp.int32, (pixels, LANE), 0), width)
    for s in range(frames):
        left = jnp.where(col == 0, 0.0, pltpu.roll(acc[s, 0], 1, 0))
        right = jnp.where(col == width - 1, 0.0, pltpu.roll(acc[s, 2], pixels - 1, 0))
        done = jnp.where(lane < share, acc[s, 1] + left + right, 0.0)
        out[s] = done.reshape(rows, width, LANE)


def conv_two_kernel(valid, place, halo, own, weight, *rest):
    *outs, taps, acc = rest
    frames, rows, width, lanes = own.shape
    parts = len(outs)
    each = rows // parts
    channels = weight.shape[1]
    clear_border(taps)
    for slot in range(2 * frames):
        source = halo if slot < frames else own
        for row in range(rows):
            fill_shifted(taps, slot, row + 1, source[slot % frames, row])
    for slot in range(2 * frames):
        pairs = [(s, slot - s) for s in range(frames) if 0 <= slot - s < 3]
        columns = jnp.concatenate(
            [
                taps[e, slot, b : b + rows].reshape(rows * width, lanes)
                for b in range(3)
                for e in range(3)
            ],
            axis=1,
        )
        blocks = [weight[a * 9 * lanes : (a + 1) * 9 * lanes, :] for _, a in pairs]
        packed = blocks[0] if len(blocks) == 1 else jnp.concatenate(blocks, axis=1)
        term = jnp.dot(columns, packed, preferred_element_type=jnp.float32)
        for i, (s, a) in enumerate(pairs):
            piece = valid[s, a] * term[:, i * channels : (i + 1) * channels]
            if a == 0:
                acc[s] = piece
            else:
                acc[s] = acc[s] + piece
    for d in range(parts):
        top = pl.multiple_of(lax.rem(place[2] + d, parts) * (each * width), 64)
        for s in range(frames):
            done = acc[s, pl.ds(top, each * width), :].astype(outs[d].dtype)
            outs[d][s] = done.reshape(each, width, channels)


VMEM = pl.BlockSpec(memory_space=pltpu.VMEM)
SMEM = pl.BlockSpec(memory_space=pltpu.SMEM)
PARAMS = pltpu.CompilerParams(vmem_limit_bytes=52 * 1024 * 1024)


def conv_one_call(valid, place, halo, own, mine, other):
    parts, frames, each, width, channels = own.shape
    rows = parts * each
    flops = 2 * 6 * rows * width * 9 * channels * LANE
    return pl.pallas_call(
        functools.partial(conv_one_kernel, channels // parts),
        out_shape=jax.ShapeDtypeStruct((frames, rows, width, LANE), jnp.float32),
        in_specs=[SMEM, SMEM, VMEM, VMEM, VMEM, VMEM],
        out_specs=VMEM,
        scratch_shapes=[
            pltpu.VMEM((2 * frames, rows + 2, width, channels), jnp.bfloat16),
            pltpu.VMEM((frames, 3, rows * width, LANE), jnp.float32),
            pltpu.VMEM((27 * channels, LANE), jnp.bfloat16),
            pltpu.VMEM((27 * channels + 8, LANE), jnp.float32),
        ],
        compiler_params=PARAMS,
        cost_estimate=pl.CostEstimate(flops=flops, bytes_accessed=6_000_000, transcendentals=0),
        name="conv_one",
    )(valid, place, halo, own, mine, other)


def conv_two_call(valid, place, halo, own, weight, parts):
    frames, rows, width, lanes = own.shape
    channels = weight.shape[1]
    flops = 2 * 6 * rows * width * 9 * lanes * channels
    return pl.pallas_call(
        conv_two_kernel,
        out_shape=[jax.ShapeDtypeStruct((frames, rows // parts, width, channels), jnp.bfloat16)] * parts,
        in_specs=[SMEM, SMEM, VMEM, VMEM, VMEM],
        out_specs=[VMEM] * parts,
        scratch_shapes=[
            pltpu.VMEM((3, 2 * frames, rows + 2, width, lanes), jnp.bfloat16),
            pltpu.VMEM((frames, rows * width, channels), jnp.float32),
        ],
        compiler_params=PARAMS,
        cost_estimate=pl.CostEstimate(flops=flops, bytes_accessed=6_000_000, transcendentals=0),
        name="conv_two",
    )(valid, place, halo, own, weight)


def gathered(place, mine, other, i):
    ys, zs = mine.shape[:2]
    z, c, y = i // (2 * ys), i // ys % 2, i % ys
    at = lax.rem(place[1] + ys - y, ys), z
    return jnp.where(place[0] == c, mine[at].astype(jnp.float32), other[at].astype(jnp.float32))


def assemble_two_kernel(place, mine, other, out, wide, piece_buf):
    shards = 2 * mine.shape[0] * mine.shape[1]
    channels = mine.shape[3]
    taps = out.shape[0] // LANE
    width = channels // 4
    share = 2 * taps * width // shards
    piece_rows = (share + 1) // 2
    for t in range(taps):
        wide[t * LANE + width : (t + 1) * LANE, :] = jnp.zeros((LANE - width, channels), jnp.float32)
    for m in range(shards // 2):
        even, odd = gathered(place, mine, other, 2 * m), gathered(place, mine, other, 2 * m + 1)
        half = piece_rows - 1
        piece_buf[0:TILE_ROWS, :] = even
        piece_buf[TILE_ROWS : 2 * TILE_ROWS, :] = odd
        piece_buf[half : half + 1, :] = even[half : half + 1] + odd[0:1]
        done = 0
        while done < share:
            first = share * m + done
            source = done if done <= half else done - half + TILE_ROWS
            count = min((first // width + 1) * width - first, (piece_rows if done <= half else share) - done)
            at = first // width * LANE + first % width
            wide[at : at + count, :] = piece_buf[source : source + count, :]
            done += count
    out[...] = wide[...].astype(out.dtype)


def assemble_call(kernel, place, mine, other, shape, extra, name):
    return pl.pallas_call(
        kernel,
        out_shape=jax.ShapeDtypeStruct(shape, jnp.bfloat16),
        in_specs=[SMEM, VMEM, VMEM],
        out_specs=VMEM,
        scratch_shapes=[pltpu.VMEM(shape, jnp.float32)] + extra,
        compiler_params=PARAMS,
        cost_estimate=pl.CostEstimate(flops=4_000_000, bytes_accessed=5_000_000, transcendentals=0),
        name=name,
    )(place, mine, other)


def pick(rows, columns, transposed, part, step):
    big = lax.broadcasted_iota(jnp.int32, (rows, columns), 1 if transposed else 0)
    small = lax.broadcasted_iota(jnp.int32, (rows, columns), 0 if transposed else 1)
    return (big == step * small + part).astype(jnp.bfloat16)


def body(latents, frame_counts, gain_one, gain_two, conv_one, conv_two):
    part = lax.axis_index("tile")
    parts = lax.axis_size("tile")
    side = lax.axis_index("group") % 2
    core = lax.axis_index("core")
    counts = frame_counts.reshape(-1)
    source = latents[0].astype(jnp.float32)
    frames, each, width, channels = source.shape
    share = channels // parts
    shard = conv_one.shape[0]
    piece_rows = shard // 4 + 1
    shards = lax.axis_size(SLOT) * lax.axis_size("group")
    place = jnp.stack([core, lax.axis_index("group"), part]).astype(jnp.int32)

    with jax.named_scope("pixels"):
        mean_sq = jnp.mean(source * source, axis=-1, keepdims=True)
        hidden_one = jax.nn.silu(source * lax.rsqrt(mean_sq + EPS) * gain_one).astype(jnp.bfloat16)
        own_all = from_all(hidden_one, "tile")

    with jax.named_scope("pieces"):
        take = pick(channels, share, False, part, parts)
        piece = jnp.dot(conv_one, take, preferred_element_type=jnp.float32).astype(jnp.bfloat16)
        piece = jnp.pad(piece, ((0, 4 * piece_rows - shard), (0, 0)))
        piece = jnp.concatenate([piece[j * piece_rows : (j + 1) * piece_rows] for j in range(4)], axis=1)
        piece = jnp.pad(piece, ((0, TILE_ROWS - piece_rows), (0, 0)))
        rows_take = pick(TILE_ROWS, shard, True, part - 2 * side, parts)
        piece_two = jnp.dot(rows_take, conv_two, preferred_element_type=jnp.float32).astype(jnp.bfloat16)
        pieces = jnp.concatenate([piece, piece_two], axis=0)
        column = lax.all_to_all(jnp.broadcast_to(pieces, (lax.axis_size("z"),) + pieces.shape), "z", 0, 0)

    column, own_all = lax.optimization_barrier((column, own_all))
    with jax.named_scope("weight_one"):
        mine = from_all(column[:, :TILE_ROWS], "group")
        prior_all = earlier(own_all)
        mine, prior_all = lax.optimization_barrier((mine, prior_all))
        swapped = lax.ppermute(mine, "core", [(0, 1), (1, 0)])
        one_mine, one_swapped = mine, swapped

    with jax.named_scope("weight_two"):
        column, _ = lax.optimization_barrier((column, mine))
        later = column[:, TILE_ROWS:]
        later = [later] + [onward(later, d, "group") for d in range(1, lax.axis_size("group"))]

    base = lax.axis_index(SLOT) * frames
    slots = base + jnp.arange(frames, dtype=jnp.int32)
    begins = video_start(slots, counts)
    before = 2 - jnp.arange(3, dtype=jnp.int32)
    valid = (slots[:, None] - before[None, :] >= begins[:, None]).astype(jnp.float32)

    with jax.named_scope("first"):
        first = conv_one_call(valid, place, prior_all, own_all, one_mine, one_swapped)

    with jax.named_scope("weight_two"):
        squares = jnp.sum(first * first, axis=-1)
        squares = squares + across(squares, 1)
        squares, later = lax.optimization_barrier((squares, later))
        mine = jnp.stack(later)
        swapped = lax.ppermute(mine, "core", [(0, 1), (1, 0)])
        taps = shards * shard // channels
        weight_two = assemble_call(
            assemble_two_kernel, place, mine, swapped, (taps * LANE, channels),
            [pltpu.VMEM((2 * TILE_ROWS, channels), jnp.float32)], "assemble_two"
        )

    with jax.named_scope("second"):
        squares = squares + across(squares, 2)
        gain_mine = lax.dynamic_index_in_dim(gain_two.reshape(share, parts), part, 1, keepdims=False)
        gain_mine = jnp.pad(gain_mine, (0, LANE - share))
        scale = lax.rsqrt(squares / channels + EPS)
        hidden_two = jax.nn.silu(first * scale[..., None] * gain_mine).astype(jnp.bfloat16)
        prior_two = earlier(hidden_two)
        sums, *rest = conv_two_call(valid, place, prior_two, hidden_two, weight_two, parts)
        arrived = [onward(r, d) for d, r in enumerate(rest, 1)]
        second = sum((r.astype(jnp.float32) for r in arrived), sums.astype(jnp.float32))

    block = (source + second).astype(jnp.bfloat16)
    result = jnp.broadcast_to(
        block[:, :, None, :, None, :], (frames, each, 2, width, 2, channels)
    ).reshape(frames, 2 * each, 2 * width, channels)
    return result[None]


def solution(mesh):
    sizes = mesh.devices.shape
    fine = Mesh(mesh.devices.reshape((sizes[0] // 2, 2) + sizes[1:]), ("z", "core", "tile", "group"))
    in_specs = (
        P("group", SLOT, "tile", None, None),
        P("group", None),
        P(),
        P(),
        P(SLOT + ("group",), None),
        P(SLOT + ("group",), None),
    )
    out_specs = P("group", SLOT, "tile", None, None)
    return jax.shard_map(body, mesh=fine, in_specs=in_specs, out_specs=out_specs, check_vma=False)
```
